128 devices in a mesh: dp: 2 (over core), gy: 8 (over x, z_hi), gx: 8 (over y, z_lo).
Axes of the slice: x: 4, y: 4, z: 4 (z_hi: 2, z_lo: 2; z = z_hi * 2 + z_lo), core: 2. Of those that a mesh axis runs over, the one named last changes fastest.
Arguments:
- fine_input: bfloat16 [2, 8, 128, 9216], P('dp', None, 'gy', 'gx'), may hold values from -6 to 6
- fine_weight: bfloat16 [3, 3, 72, 72], replicated, may hold values from -0.25 to 0.25
- entry_weight: bfloat16 [3, 3, 3, 72, 96], replicated, may hold values from -0.125 to 0.125
- middle_weight: bfloat16 [3, 3, 3, 96, 96], replicated, may hold values from -0.125 to 0.125
- lift_weight: bfloat16 [96, 72], replicated, may hold values from -0.625 to 0.625
- upstream: bfloat16 [2, 8, 128, 9216], P('dp', None, 'gy', 'gx'), may hold values from -6 to 6
Outputs:
- mixed: bfloat16 [2, 8, 128, 9216], P('dp', None, 'gy', 'gx')
- input_grad: bfloat16 [2, 8, 128, 9216], P('dp', None, 'gy', 'gx')
- fine_weight_grad: float32 [3, 3, 72, 72], replicated
- entry_weight_grad: float32 [3, 3, 3, 72, 96], replicated
- middle_weight_grad: float32 [3, 3, 3, 96, 96], replicated
- lift_weight_grad: float32 [96, 72], replicated
The draws below stay inside these ranges and needn't reach their ends.
All inputs are finite; a program needn't handle non-finite values.
Results may differ from the reference program's by a relative error of at most 0.018.
Values may be sent and summed in bfloat16 or wider, within the bound.
A program may use at most 128 MiB of HBM per device.

```python
import jax
import jax.numpy as jnp
from jax import lax

C2 = 72
C3 = 96
Z = 8
B = 2
Y2 = 128
X2 = 128


def block_levels(own_key, extent, cuts, low, largest):
    loudness = 1.0
    for dim, shards_of in cuts:
        steps = jax.random.uniform(jax.random.fold_in(jax.random.fold_in(own_key, 6), dim), (shards_of,), jnp.float32, low / len(cuts), largest / len(cuts))
        loudness = loudness * jnp.repeat(jnp.exp(steps), extent[dim] // shards_of).reshape((-1,) + (1,) * (len(extent) - 1 - dim))
    return loudness


def bell_draw(key, extent, deviation, most, cuts=(), held_as=jnp.bfloat16):
    loudness = block_levels(key, extent, cuts, -0.22, 0.18) if cuts else 1.0
    array = jax.random.normal(key, extent, jnp.float32) * deviation * loudness
    return jnp.minimum(jnp.maximum(array, -most), most).astype(held_as)


def setup_inputs(seed: int = 0) -> dict:
    keys = jax.random.split(jax.random.key(seed), 7)
    return {
        "fine_input": bell_draw(keys[0], (B, Z, Y2, X2 * C2), 1.0, 6.0, ((0, 2), (2, 8), (3, 8))),
        "fine_weight": bell_draw(keys[1], (3, 3, C2, C2), (9 * C2) ** -0.5, 0.25),
        "entry_weight": bell_draw(keys[2], (3, 3, 3, C2, C3), (27 * C2) ** -0.5, 0.125),
        "middle_weight": bell_draw(keys[3], (3, 3, 3, C3, C3), (27 * C3) ** -0.5, 0.125),
        "lift_weight": bell_draw(keys[4], (C3, C2), C3 ** -0.5, 0.625),
        "upstream": bell_draw(keys[5], (B, Z, Y2, X2 * C2), 1.0, 6.0, ((0, 2), (2, 8), (3, 8))),
    }


def activate(values):
    return jnp.where(values > 0, values, jnp.expm1(jnp.minimum(values, 0.0)))

def activation_slope(stored):
    widened = stored.astype(jnp.float32)
    return jnp.where(widened > 0, 1.0, 1.0 + widened)

def conv_taps(padded, weight, cell_shape):
    count, depth, row_count, col_count = cell_shape
    kernel_depth = weight.shape[0]
    channels = weight.shape[3]
    outputs = weight.shape[4]
    summed = jnp.zeros((count * depth * row_count * col_count, outputs), jnp.float32)
    for z_tap in range(kernel_depth):
        for y_tap in range(3):
            stacked = jnp.concatenate([padded[:, z_tap:z_tap + depth, y_tap:y_tap + row_count, x_tap:x_tap + col_count, :] for x_tap in range(3)], axis=-1)
            summed = summed + jnp.dot(stacked.reshape(-1, 3 * channels), weight[z_tap, y_tap].reshape(3 * channels, outputs), preferred_element_type=jnp.float32)
    return summed.reshape(count, depth, row_count, col_count, outputs)

def weight_grad(padded, gradient, kernel_depth):
    count, depth, row_count, col_count, outputs = gradient.shape
    channels = padded.shape[-1]
    flattened = gradient.reshape(-1, outputs)
    pieces = []
    for z_tap in range(kernel_depth):
        for y_tap in range(3):
            stacked = jnp.concatenate([padded[:, z_tap:z_tap + depth, y_tap:y_tap + row_count, x_tap:x_tap + col_count, :] for x_tap in range(3)], axis=-1)
            product = lax.dot_general(stacked.reshape(-1, 3 * channels), flattened, (((0,), (0,)), ((), ())), preferred_element_type=jnp.float32)
            pieces.append(product.reshape(3, channels, outputs))
    return jnp.stack(pieces).reshape(kernel_depth, 3, 3, channels, outputs)

def flipped(weight):
    return jnp.swapaxes(jnp.flip(weight, axis=(0, 1, 2)), 3, 4)

def pad_cells(values, depth_pad):
    return jnp.pad(values, ((0, 0), (depth_pad, depth_pad), (1, 1), (1, 1), (0, 0)))

def pool_sum(values):
    count, depth, row_count, col_count, channels = values.shape
    grouped = values.astype(jnp.float32).reshape(count, depth, row_count // 2, 2, col_count // 2, 2, channels)
    return grouped.sum(axis=(3, 5))

def upsample(values):
    return jnp.repeat(jnp.repeat(values, 2, axis=2), 2, axis=3)

def reference(fine_input, fine_weight, entry_weight, middle_weight, lift_weight, upstream):
    count, depth, row_count, merged = fine_input.shape
    channels = fine_weight.shape[2]
    wide = lift_weight.shape[0]
    col_count = merged // channels
    fine_shape = (count, depth, row_count, col_count)
    features = fine_input.reshape(count, depth, row_count, col_count, channels)
    upstream_cells = upstream.reshape(count, depth, row_count, col_count, channels)
    kernel_fine = fine_weight[None]
    padded_in = pad_cells(features, 0)
    fine_act = activate(conv_taps(padded_in, kernel_fine, fine_shape)).astype(jnp.bfloat16)
    pooled = (0.25 * pool_sum(fine_act)).astype(jnp.bfloat16)
    low_shape = pooled.shape[:4]
    pooled_pad = pad_cells(pooled, 1)
    coarse_one = activate(conv_taps(pooled_pad, entry_weight, low_shape)).astype(jnp.bfloat16)
    one_pad = pad_cells(coarse_one, 1)
    coarse_two = activate(conv_taps(one_pad, middle_weight, low_shape)).astype(jnp.bfloat16)
    low_cells = coarse_two.reshape(-1, wide)
    lifted = jnp.dot(low_cells, lift_weight, preferred_element_type=jnp.float32).astype(jnp.bfloat16).reshape(low_shape + (channels,))
    mixed = (fine_act.astype(jnp.float32) + upsample(lifted).astype(jnp.float32)).astype(jnp.bfloat16)
    upstream_low = pool_sum(upstream_cells).astype(jnp.bfloat16)
    low_grad = upstream_low.reshape(-1, channels)
    lift_grad = lax.dot_general(low_cells, low_grad, (((0,), (0,)), ((), ())), preferred_element_type=jnp.float32)
    back_lift = lax.dot_general(low_grad, lift_weight, (((1,), (1,)), ((), ())), preferred_element_type=jnp.float32)
    grad_two = (back_lift.reshape(low_shape + (wide,)) * activation_slope(coarse_two)).astype(jnp.bfloat16)
    middle_grad = weight_grad(one_pad, grad_two, 3)
    grad_one = (conv_taps(pad_cells(grad_two, 1), flipped(middle_weight), low_shape) * activation_slope(coarse_one)).astype(jnp.bfloat16)
    entry_grad = weight_grad(pooled_pad, grad_one, 3)
    grad_pool = conv_taps(pad_cells(grad_one, 1), flipped(entry_weight), low_shape).astype(jnp.bfloat16)
    grad_fine_pre = ((upstream_cells.astype(jnp.float32) + 0.25 * upsample(grad_pool).astype(jnp.float32)) * activation_slope(fine_act)).astype(jnp.bfloat16)
    fine_grad = weight_grad(padded_in, grad_fine_pre, 1)[0]
    grad_input = conv_taps(pad_cells(grad_fine_pre, 0), flipped(kernel_fine), fine_shape).astype(jnp.bfloat16)
    return (mixed.reshape(fine_input.shape), grad_input.reshape(fine_input.shape), fine_grad, entry_grad, middle_grad, lift_grad)
```

```python
import functools

import jax
import jax.numpy as jnp
from jax import lax
from jax.experimental import pallas as pl
from jax.experimental.pallas import tpu as pltpu
from jax.sharding import PartitionSpec as P

MESH = pl.DeviceIdType.MESH
BF = jnp.bfloat16
F32 = jnp.float32

Z = 8
N2 = 16
N3 = 8
C2 = 72
C3 = 96
L = 128
GY = 8
GX = 8
MERGED = N2 * C2
TILES = MERGED // L
DIRS = [(dy, dx) for dy in (-1, 0, 1) for dx in (-1, 0, 1) if (dy, dx) != (0, 0)]

EX_IN, EX_POOL, EX_ONE, EX_G2, EX_G1, EX_FINE = range(6)

ROWS_M = 2048
ROWS_E = 1536
ROWS_F = 512


def lanes(shape):
    return lax.broadcasted_iota(jnp.int32, shape, len(shape) - 1)


def elu(v):
    return jnp.where(v > 0, v, jnp.exp(jnp.minimum(v, 0.0)) - 1.0)


def slope(s):
    return jnp.where(s > 0, 1.0, 1.0 + s)


def rounded(v):
    return v.astype(BF).astype(F32)


def shift_z(v, step):
    moved = pltpu.roll(v, step % Z, 1)
    row = lax.broadcasted_iota(jnp.int32, v.shape, 1)
    return jnp.where(row == (0 if step == 1 else Z - 1), 0.0, moved)


def nt(a, b):
    return lax.dot_general(a, b, (((1,), (1,)), ((), ())), preferred_element_type=F32)


def nn(a, b):
    return jnp.dot(a, b, preferred_element_type=F32)


class Ring:
    def __init__(self):
        self.dp = lax.axis_index("dp")
        self.gy = lax.axis_index("gy")
        self.gx = lax.axis_index("gx")

    def member(self, kind):
        if kind == "dp":
            return self.dp
        if kind == "y":
            return self.gx // 2
        if kind == "x":
            return self.gy // 2
        if kind == "z":
            return (self.gy % 2) * 2 + self.gx % 2
        if kind == "f":
            return self.dp * GX + self.gx
        return self.gy

    def device(self, kind, p):
        if kind == "dp":
            return (p, self.gy, self.gx)
        if kind == "y":
            return (self.dp, self.gy, p * 2 + self.gx % 2)
        if kind == "x":
            return (self.dp, p * 2 + self.gy % 2, self.gx)
        if kind == "z":
            return (self.dp, (self.gy // 2) * 2 + p // 2, (self.gx // 2) * 2 + p % 2)
        if kind == "f":
            return (p // GX, self.gy, p % GX)
        return (self.dp, p, self.gx)


SIZE = {"dp": 2, "y": 4, "x": 4, "z": 4, "f": 16, "g": 8}


class Reduce:
    def __init__(self, ring, rows, scatter, last, bufs, recvs, slots, out, send, recv, sent):
        self.ring = ring
        self.scatter = scatter
        self.last = last
        self.bufs = bufs
        self.recvs = recvs
        self.slots = slots
        self.out = out
        self.send = send
        self.recv = recv
        self.sent = sent
        self.used = 0
        self.rows = [rows]
        self.offs = [0]
        for kind in scatter:
            n = self.rows[-1] // SIZE[kind]
            self.offs.append(self.offs[-1] + ring.member(kind) * n)
            self.rows.append(n)

    def _go(self, src, dst, device):
        i = self.used
        self.used += 1
        c = pltpu.make_async_remote_copy(
            src_ref=src,
            dst_ref=dst,
            send_sem=self.send.at[i],
            recv_sem=self.recv.at[i],
            device_id=device,
            device_id_type=MESH,
        )
        c.start()
        self.sent.append(c)
        return c

    def scatter_start(self, s):
        kind, n = self.scatter[s], self.rows[s + 1]
        m, size = self.ring.member(kind), SIZE[kind]
        self.now = []
        for r in range(1, size):
            p = (m + r) % size
            src = self.bufs[s].at[pl.ds(pl.multiple_of(p * n, 16), n)]
            self.now.append(self._go(src, self.recvs[s].at[r - 1], self.ring.device(kind, p)))

    def scatter_end(self, s):
        kind, n = self.scatter[s], self.rows[s + 1]
        m, size = self.ring.member(kind), SIZE[kind]
        for c in self.now:
            c.wait_recv()
        total = self.bufs[s][pl.ds(pl.multiple_of(m * n, 16), n), :].astype(F32)
        for r in range(size - 1):
            total = total + self.recvs[s][r].astype(F32)
        total = total.astype(BF)
        if s + 1 < len(self.scatter):
            self.bufs[s + 1][...] = total
        else:
            self.slots[self.ring.member(self.last)] = total

    def last_start(self):
        m, size = self.ring.member(self.last), SIZE[self.last]
        self.now = []
        for r in range(1, size):
            p = (m + r) % size
            self.now.append(self._go(self.slots.at[m], self.slots.at[m], self.ring.device(self.last, p)))

    def last_end(self):
        for c in self.now:
            c.wait_recv()
        total = self.slots[0].astype(F32)
        for r in range(1, SIZE[self.last]):
            total = total + self.slots[r].astype(F32)
        self.out[pl.ds(pl.multiple_of(self.offs[-1], 16), self.rows[-1]), :] = total.astype(BF)

    def gather_start(self, s):
        kind, n = self.scatter[s], self.rows[s + 1]
        m, size = self.ring.member(kind), SIZE[kind]
        part = self.out.at[pl.ds(pl.multiple_of(self.offs[s + 1], 16), n)]
        self.now = []
        for r in range(1, size):
            p = (m + r) % size
            self.now.append(self._go(part, part, self.ring.device(kind, p)))

    def gather_end(self):
        for c in self.now:
            c.wait_recv()


def pack4(b):
    lane = lanes(b[0].shape)
    r1, r2, r3 = pltpu.roll(b[1], 96, 1), pltpu.roll(b[2], 64, 1), pltpu.roll(b[3], 32, 1)
    return (
        jnp.where(lane >= 96, r1, b[0]),
        jnp.where(lane < 64, r1, r2),
        jnp.where(lane < 32, r2, r3),
    )


def unpack4(d):
    lane = lanes(d[0].shape)
    return (
        d[0],
        pltpu.roll(jnp.where(lane >= 96, d[0], d[1]), 32, 1),
        pltpu.roll(jnp.where(lane >= 64, d[1], d[2]), 64, 1),
        pltpu.roll(d[2], 96, 1),
    )


def kernel(
    a_ref, wf_ref, we_ref, wm_ref, wl_ref, u_ref,
    mixed_ref, ig_ref, gf_ref, ge_ref, gm_ref, gl_ref,
    raw, pad2, pad3, e32, x3, x3t, fa, q, qet, qmt, c1, c2, ul, bl, gp, gfb, d32, mix32,
    wf, wft, we, wet, wm, wmt, wl, arm32, are32, arf32,
    sbuf, rbuf, h_send, h_recv,
    m0, m1, m2, mr0, mr1, mr2, mslot, mout, m_send, m_recv,
    e0, e1, e2, er0, er1, er2, eslot, eout, e_send, e_recv,
    f0, fr0, fslot, fout, f_send, f_recv,
):
    ring = Ring()
    dp, gy, gx = ring.dp, ring.gy, ring.gx

    barrier = pltpu.get_barrier_semaphore()
    met = 0
    for d in range(2):
        for x in range(GX):
            if (d, x) != (0, 0):
                pl.semaphore_signal(
                    barrier, inc=1, device_id=((dp + d) % 2, gy, (gx + x) % GX), device_id_type=MESH
                )
                met += 1
    for y in range(1, GY):
        for x in (-1, 0, 1) if y in (1, GY - 1) else (0,):
            pl.semaphore_signal(
                barrier, inc=1, device_id=(dp, (gy + y) % GY, (gx + x + GX) % GX), device_id_type=MESH
            )
            met += 1

    sent = []

    def edge(step, n):
        return {1: slice(n, n + 1), -1: slice(1, 2), 0: slice(1, n + 1)}[step]

    def outside(step, n):
        return {1: slice(0, 1), -1: slice(n + 1, n + 2), 0: slice(1, n + 1)}[step]

    def send_halo(ex, ref, n):
        copies = []
        for d, (dy, dx) in enumerate(DIRS):
            part = ref[edge(dy, n), edge(dx, n)].reshape(-1, L)
            if dy != 0 and dx != 0:
                part = jnp.concatenate([part, part], axis=0)
            rows = part.shape[0]
            sbuf[ex, d, 0:rows, :] = part.astype(BF)
            c = pltpu.make_async_remote_copy(
                src_ref=sbuf.at[ex, d, pl.ds(0, rows)],
                dst_ref=rbuf.at[ex, d, pl.ds(0, rows)],
                send_sem=h_send.at[ex * 8 + d],
                recv_sem=h_recv.at[ex * 8 + d],
                device_id=(dp, (gy + dy + GY) % GY, (gx + dx + GX) % GX),
                device_id_type=MESH,
            )
            c.start()
            sent.append(c)
            copies.append(c)
        return copies

    def take_halo(ex, ref, n, copies):
        for d, (dy, dx) in enumerate(DIRS):
            copies[d].wait_recv()
            there = jnp.logical_and(
                jnp.logical_and(gy - dy >= 0, gy - dy < GY),
                jnp.logical_and(gx - dx >= 0, gx - dx < GX),
            )
            keep = jnp.where(there, 1.0, 0.0).astype(F32)
            ys, xs = outside(dy, n), outside(dx, n)
            ny, nx = ys.stop - ys.start, xs.stop - xs.start
            part = rbuf[ex, d, 0 : max(ny * nx * Z, 16), :].astype(F32)[: ny * nx * Z]
            ref[ys, xs] = (part * keep).reshape(ny, nx, Z, L)

    def read_cells(src_ref, dst, shift):
        for t in range(TILES):
            raw[t] = src_ref[0, :, :, t * L : (t + 1) * L].astype(F32).reshape(Z * N2, L)

        def row(y, _):
            tiles = [raw[t, pl.ds(y, Z, stride=N2), :] for t in range(TILES)]
            lane = lanes((Z, L))
            for x in range(N2):
                t, o = (x * C2) // L, (x * C2) % L
                cell = tiles[t] if o == 0 else pltpu.roll(tiles[t], L - o, 1)
                if o + C2 > L:
                    cell = jnp.where(lane < L - o, cell, pltpu.roll(tiles[t + 1], L - o, 1))
                dst[y + shift, x + shift] = jnp.where(lane < C2, cell, 0.0)
            return 0

        lax.fori_loop(0, N2, row, 0)

    def write_cells(src, out32, dst_ref):
        def row(y, _):
            tiles = [None] * TILES
            lane = lanes((Z, L))
            for x in range(N2):
                t, o = (x * C2) // L, (x * C2) % L
                cell = src[y, x]
                cell = cell if o == 0 else pltpu.roll(cell, o, 1)
                tiles[t] = cell if o == 0 else jnp.where(lane >= o, cell, tiles[t])
                if o + C2 > L:
                    tiles[t + 1] = cell
            for t in range(TILES):
                out32[t, pl.ds(y, Z, stride=N2), :] = tiles[t]
            return 0

        lax.fori_loop(0, N2, row, 0)
        for t in range(TILES):
            dst_ref[0, :, :, t * L : (t + 1) * L] = out32[t].reshape(Z, N2, L).astype(BF)

    def fine_columns():
        def row(y, _):
            for k in range(3):
                x3[y, :, k * L : (k + 1) * L] = pad2[y, k : k + N2].reshape(N2 * Z, L).astype(BF)
            return 0

        lax.fori_loop(0, N2 + 2, row, 0)

    def fine_rows(chunk):
        parts = [x3[pl.ds(chunk * 4 + j, 4)].reshape(4 * N2 * Z, 3 * L) for j in range(3)]
        return jnp.concatenate(parts, axis=1)

    def coarse_columns():
        for j in range(3):
            for k in range(3):
                t = j * 3 + k
                q[:, t * L : (t + 1) * L] = (
                    pad3[j : j + N3, k : k + N3].reshape(N3 * N3 * Z, L).astype(BF)
                )

    def joined(acc):
        acc = acc.reshape(N3 * N3, Z, 3 * L)
        return shift_z(acc[:, :, 0:L], 1) + acc[:, :, L : 2 * L] + shift_z(acc[:, :, 2 * L :], -1)

    def put3(v):
        pad3[1 : N3 + 1, 1 : N3 + 1] = v.reshape(N3, N3, Z, L)

    def coarse_weight_grad(qt, g):
        g3 = jnp.concatenate([shift_z(g, -1), g, shift_z(g, 1)], axis=2)
        g3 = g3.reshape(N3 * N3 * Z, 3 * L).astype(BF)
        return nn(qt[...], g3).reshape(9, L, 3 * L)

    read_cells(a_ref, pad2, 1)
    pl.semaphore_wait(barrier, met)
    copies = send_halo(EX_IN, pad2, N2)

    for ref in (wf, wft, we, wet, wm, wmt, wl):
        ref[...] = jnp.zeros(ref.shape, BF)
    wl[0:C3, 0:C2] = wl_ref[...]
    for j in range(3):
        for k in range(3):
            t = (j * 3 + k) * L
            wf[t : t + C2, 0:C2] = wf_ref[j, k]
            wft[0:C2, t : t + C2] = wf_ref[2 - j, 2 - k]
            for i in range(3):
                we[t : t + C2, i * L : i * L + C3] = we_ref[i, j, k]
                wm[t : t + C3, i * L : i * L + C3] = wm_ref[i, j, k]
                wet[i * L : i * L + C2, t : t + C3] = we_ref[2 - i, 2 - j, 2 - k]
                wmt[i * L : i * L + C3, t : t + C3] = wm_ref[2 - i, 2 - j, 2 - k]
    read_cells(u_ref, e32, 0)
    low = e32[...].reshape(N3, 2, N3, 2, Z, L)
    low = (low[:, 0, :, 0] + low[:, 0, :, 1]) + (low[:, 1, :, 0] + low[:, 1, :, 1])
    ul[...] = low.reshape(N3 * N3 * Z, L).astype(BF)
    bl[...] = nt(ul[...], wl[...])

    take_halo(EX_IN, pad2, N2, copies)
    fine_columns()

    def fine_forward(chunk, _):
        act = elu(nn(fine_rows(chunk), wf[...])).astype(BF)
        fa[pl.ds(chunk * 4, 4)] = act.reshape(4, N2 * Z, L)
        v = act.astype(F32).reshape(2, 2, N3, 2, Z, L)
        v = (v[:, 0, :, 0] + v[:, 0, :, 1]) + (v[:, 1, :, 0] + v[:, 1, :, 1])
        pad3[pl.ds(chunk * 2 + 1, 2), 1 : N3 + 1] = rounded(0.25 * v)
        return 0

    lax.fori_loop(0, 4, fine_forward, 0)
    copies = send_halo(EX_POOL, pad3, N3)

    def turn(y, _):
        x3t[:, pl.ds(pl.multiple_of(y * L, L), L)] = x3[y].T
        return 0

    lax.fori_loop(0, N2 + 2, turn, 0)

    take_halo(EX_POOL, pad3, N3, copies)
    coarse_columns()
    c1[...] = rounded(elu(joined(nn(q[...], we[...]))))
    put3(c1[...])
    copies = send_halo(EX_ONE, pad3, N3)
    qet[...] = q[...].T

    take_halo(EX_ONE, pad3, N3, copies)
    coarse_columns()
    two = rounded(elu(joined(nn(q[...], wm[...]))))
    c2[...] = two
    g2 = rounded(bl[...].reshape(N3 * N3, Z, L) * slope(two))
    put3(g2)
    copies = send_halo(EX_G2, pad3, N3)

    qmt[...] = q[...].T
    mid = coarse_weight_grad(qmt, pad3[1 : N3 + 1, 1 : N3 + 1].reshape(N3 * N3, Z, L))
    two = c2[...].reshape(N3 * N3 * Z, L).astype(BF)
    lift_grad = nn(two.T, ul[...])
    blocks = [mid[t, :C3, i * L : (i + 1) * L] for i in range(3) for t in range(9)]
    blocks.append(lift_grad[:C3])
    for g in range(7):
        for d, part in enumerate(pack4(blocks[4 * g : 4 * g + 4])):
            m0[(g * 3 + d) * C3 : (g * 3 + d + 1) * C3, :] = part.astype(BF)
    m0[21 * C3 :, :] = jnp.zeros((ROWS_M - 21 * C3, L), BF)
    red_m = Reduce(
        ring, ROWS_M, ("dp", "y", "x"), "z", (m0, m1, m2), (mr0, mr1, mr2), mslot, mout, m_send, m_recv, sent
    )
    red_m.scatter_start(0)

    take_halo(EX_G2, pad3, N3, copies)
    coarse_columns()
    g1 = rounded(joined(nt(q[...], wmt[...])) * slope(c1[...]))
    put3(g1)
    copies = send_halo(EX_G1, pad3, N3)

    red_m.scatter_end(0)
    red_m.scatter_start(1)
    ent = coarse_weight_grad(qet, pad3[1 : N3 + 1, 1 : N3 + 1].reshape(N3 * N3, Z, L))
    blocks = [ent[t, :C2, i * L : (i + 1) * L] for i in range(3) for t in range(9)]
    blocks.append(jnp.zeros((C2, L), F32))
    for g in range(7):
        for d, part in enumerate(pack4(blocks[4 * g : 4 * g + 4])):
            are32[(g * 3 + d) * C2 : (g * 3 + d + 1) * C2, :] = part
    are32[21 * C2 :, :] = jnp.zeros((ROWS_E - 21 * C2, L), F32)
    e0[...] = are32[...].astype(BF)
    red_e = Reduce(
        ring, ROWS_E, ("dp", "x", "y"), "z", (e0, e1, e2), (er0, er1, er2), eslot, eout, e_send, e_recv, sent
    )
    red_e.scatter_start(0)

    take_halo(EX_G1, pad3, N3, copies)
    coarse_columns()
    gp[...] = 0.25 * rounded(joined(nt(q[...], wet[...]))).reshape(N3, N3, Z, L)

    def fine_back(y, _):
        act = fa[pl.ds(y * 2, 2)].astype(F32).reshape(2, N3, 2, Z, L)
        e = e32[pl.ds(y * 2, 2)].reshape(2, N3, 2, Z, L)
        up = gp[pl.ds(y, 1)].reshape(1, N3, 1, Z, L)
        g = ((e + up) * slope(act)).reshape(2, N2, Z, L).astype(BF)
        gfb[pl.ds(pl.multiple_of(y * 2 * L, 2 * L), 2 * L), :] = g.reshape(2 * N2 * Z, L)
        pad2[pl.ds(y * 2 + 1, 2), 1 : N2 + 1] = g.astype(F32)
        return 0

    lax.fori_loop(0, N3, fine_back, 0)
    copies = send_halo(EX_FINE, pad2, N2)

    for j in range(3):
        grad = nn(x3t[:, j * L : (j + N2) * L], gfb[...])
        b0, b1, b2 = grad[0:C2], grad[L : L + C2], grad[2 * L : 2 * L + C2]
        lane = lanes(b0.shape)
        r1, r2 = pltpu.roll(b1, C2, 1), pltpu.roll(b2, 2 * C2 - L, 1)
        arf32[2 * j * C2 : (2 * j + 1) * C2, :] = jnp.where(lane < C2, b0, r1)
        arf32[(2 * j + 1) * C2 : (2 * j + 2) * C2, :] = jnp.where(lane < 2 * C2 - L, r1, r2)
    arf32[6 * C2 :, :] = jnp.zeros((ROWS_F - 6 * C2, L), F32)
    f0[...] = arf32[...].astype(BF)
    red_f = Reduce(ring, ROWS_F, ("f",), "g", (f0,), (fr0,), fslot, fout, f_send, f_recv, sent)
    red_f.scatter_start(0)
    red_m.scatter_end(1)
    red_m.scatter_start(2)
    red_e.scatter_end(0)
    red_e.scatter_start(1)

    two = c2[...].reshape(N3 * N3 * Z, L).astype(BF)
    gp[...] = rounded(nn(two, wl[...])).reshape(N3, N3, Z, L)

    def mix(y, _):
        act = fa[pl.ds(y * 2, 2)].astype(F32).reshape(2, N3, 2, Z, L)
        up = gp[pl.ds(y, 1)].reshape(1, N3, 1, Z, L)
        d32[pl.ds(y * 2, 2)] = (act + up).reshape(2, N2, Z, L)
        return 0

    lax.fori_loop(0, N3, mix, 0)
    write_cells(d32, mix32, mixed_ref)

    red_f.scatter_end(0)
    red_f.last_start()
    red_m.scatter_end(2)
    red_m.last_start()
    red_e.scatter_end(1)
    red_e.scatter_start(2)

    take_halo(EX_FINE, pad2, N2, copies)
    fine_columns()

    def fine_backward(chunk, _):
        d32[pl.ds(chunk * 4, 4)] = nt(fine_rows(chunk), wft[...]).reshape(4, N2, Z, L)
        return 0

    lax.fori_loop(0, 4, fine_backward, 0)

    red_f.last_end()
    red_f.gather_start(0)
    red_m.last_end()
    red_m.gather_start(2)
    red_e.scatter_end(2)
    red_e.last_start()

    write_cells(d32, raw, ig_ref)

    red_m.gather_end()
    red_m.gather_start(1)
    red_e.last_end()
    red_e.gather_start(2)

    red_f.gather_end()
    arf32[...] = fout[...].astype(F32)
    for j in range(3):
        d0 = arf32[2 * j * C2 : (2 * j + 1) * C2, :]
        d1 = arf32[(2 * j + 1) * C2 : (2 * j + 2) * C2, :]
        lane = lanes(d0.shape)
        b1 = pltpu.roll(jnp.where(lane >= C2, d0, d1), L - C2, 1)
        b2 = pltpu.roll(d1, 2 * L - 2 * C2, 1)
        for k, b in enumerate((d0, b1, b2)):
            gf_ref[j, k] = b[:, 0:C2]

    red_e.gather_end()
    red_e.gather_start(1)
    red_m.gather_end()
    red_m.gather_start(0)
    red_e.gather_end()
    red_e.gather_start(0)

    red_m.gather_end()
    for g in range(7):
        d = [mout[(g * 3 + s) * C3 : (g * 3 + s + 1) * C3, :].astype(F32) for s in range(3)]
        for s, b in enumerate(unpack4(d)):
            t = g * 4 + s
            if t < 27:
                gm_ref[t // 9, (t // 3) % 3, t % 3] = b[:, 0:C3]
            else:
                gl_ref[...] = b[:, 0:C2]

    red_e.gather_end()
    are32[...] = eout[...].astype(F32)
    for g in range(7):
        d = [are32[(g * 3 + s) * C2 : (g * 3 + s + 1) * C2, :] for s in range(3)]
        for s, b in enumerate(unpack4(d)):
            t = g * 4 + s
            if t < 27:
                ge_ref[t // 9, (t // 3) % 3, t % 3] = b[:, 0:C3]

    for c in sent:
        c.wait_send()


def body(fine_input, fine_weight, entry_weight, middle_weight, lift_weight, upstream):
    field = jax.ShapeDtypeStruct(fine_input.shape, BF)
    vmem = pl.BlockSpec(memory_space=pltpu.VMEM)
    cells2, cells3 = N2 * N2 * Z, N3 * N3 * Z

    def v(*shape, dtype=BF):
        return pltpu.VMEM(shape, dtype)

    def w(*shape):
        return pltpu.VMEM(shape, F32)

    def sems(n):
        return [pltpu.SemaphoreType.DMA((n,)), pltpu.SemaphoreType.DMA((n,))]

    m, e, f = ROWS_M, ROWS_E, ROWS_F
    scratch = [
        w(TILES, Z * N2, L), w(N2 + 2, N2 + 2, Z, L), w(N3 + 2, N3 + 2, Z, L), w(N2, N2, Z, L),
        v(N2 + 2, N2 * Z, 3 * L), v(3 * L, (N2 + 2) * N2 * Z), v(N2, N2 * Z, L),
        v(cells3, 9 * L), v(9 * L, cells3), v(9 * L, cells3),
        w(N3 * N3, Z, L), w(N3 * N3, Z, L), v(cells3, L), w(cells3, L), w(N3, N3, Z, L),
        v(cells2, L), w(N2, N2, Z, L), w(TILES, Z * N2, L),
        v(9 * L, L), v(L, 9 * L), v(9 * L, 3 * L), v(3 * L, 9 * L), v(9 * L, 3 * L), v(3 * L, 9 * L), v(L, L),
        w(8, L), w(e, L), w(f, L),
        v(6, 8, N2 * Z, L), v(6, 8, N2 * Z, L), *sems(48),
        v(m, L), v(m // 2, L), v(m // 8, L),
        v(1, m // 2, L), v(3, m // 8, L), v(3, m // 32, L), v(4, m // 32, L), v(m, L), *sems(17),
        v(e, L), v(e // 2, L), v(e // 8, L),
        v(1, e // 2, L), v(3, e // 8, L), v(3, e // 32, L), v(4, e // 32, L), v(e, L), *sems(17),
        v(f, L), v(15, f // 16, L), v(8, f // 16, L), v(f, L), *sems(37),
    ]
    return pl.pallas_call(
        kernel,
        out_shape=(
            field,
            field,
            jax.ShapeDtypeStruct(fine_weight.shape, F32),
            jax.ShapeDtypeStruct(entry_weight.shape, F32),
            jax.ShapeDtypeStruct(middle_weight.shape, F32),
            jax.ShapeDtypeStruct(lift_weight.shape, F32),
        ),
        in_specs=[vmem] * 6,
        out_specs=[vmem] * 6,
        scratch_shapes=scratch,
        compiler_params=pltpu.CompilerParams(
            collective_id=0, has_side_effects=True, vmem_limit_bytes=60 * 1024 * 1024
        ),
    )(fine_input, fine_weight, entry_weight, middle_weight, lift_weight, upstream)


def solution(mesh):
    assert mesh.shape["gy"] == GY and mesh.shape["gx"] == GX
    return jax.shard_map(
        body,
        mesh=mesh,
        in_specs=(P("dp", None, "gy", "gx"), P(), P(), P(), P(), P("dp", None, "gy", "gx")),
        out_specs=(P("dp", None, "gy", "gx"), P("dp", None, "gy", "gx"), P(), P(), P(), P()),
        check_vma=False,
    )
```

```python
import jax
import jax.numpy as jnp
from jax import lax
from jax.experimental import pallas as pl
from jax.experimental.pallas import tpu as pltpu
from jax.sharding import PartitionSpec as P

MESH = pl.DeviceIdType.MESH
BF = jnp.bfloat16
F32 = jnp.float32

Z = 8
N2 = 16
N3 = 8
C2 = 72
C3 = 96
L = 128
GY = 8
GX = 8
MERGED = N2 * C2
TILES = MERGED // L
DIRS = [(dy, dx) for dy in (-1, 0, 1) for dx in (-1, 0, 1) if (dy, dx) != (0, 0)]

EX_IN, EX_POOL, EX_LOW, EX_G1, EX_FINE = range(5)

ROWS_M = 2048
ROWS_E = 1536
ROWS_F = 512


def lanes(shape):
    return lax.broadcasted_iota(jnp.int32, shape, len(shape) - 1)


def elu(v):
    return jnp.where(v > 0, v, jnp.exp(jnp.minimum(v, 0.0)) - 1.0)


def slope(s):
    return jnp.where(s > 0, 1.0, 1.0 + s)


def rounded(v):
    return v.astype(BF).astype(F32)


def shift_z(v, step):
    moved = pltpu.roll(v, step % Z, 1)
    row = lax.broadcasted_iota(jnp.int32, v.shape, 1)
    return jnp.where(row == (0 if step == 1 else Z - 1), 0.0, moved)


def nt(a, b):
    return lax.dot_general(a, b, (((1,), (1,)), ((), ())), preferred_element_type=F32)


def tn(a, b):
    return lax.dot_general(a, b, (((0,), (0,)), ((), ())), preferred_element_type=F32)


def nn(a, b):
    return jnp.dot(a, b, preferred_element_type=F32)


class Ring:
    def __init__(self):
        self.dp = lax.axis_index("dp")
        self.gy = lax.axis_index("gy")
        self.gx = lax.axis_index("gx")

    def member(self, kind):
        if kind == "dp":
            return self.dp
        if kind == "xy":
            return (self.gy // 2) * 4 + self.gx // 2
        return (self.gy % 2) * 2 + self.gx % 2

    def device(self, kind, p):
        if kind == "dp":
            return (p, self.gy, self.gx)
        if kind == "xy":
            return (self.dp, (p // 4) * 2 + self.gy % 2, (p % 4) * 2 + self.gx % 2)
        return (self.dp, (self.gy // 2) * 2 + p // 2, (self.gx // 2) * 2 + p % 2)

    def others(self, kind):
        m = self.member(kind)
        if kind == "dp":
            return [1 - m]
        if kind == "z":
            return [(m + r) % 4 for r in (2, 1, 3)]
        steps = [(2, 2), (2, 1), (1, 2), (2, 3), (3, 2), (1, 1), (1, 3), (3, 1), (3, 3)]
        steps += [(2, 0), (0, 2), (1, 0), (0, 1), (3, 0), (0, 3)]
        return [((m // 4 + x) % 4) * 4 + (m % 4 + y) % 4 for x, y in steps]


SIZE = {"dp": 2, "xy": 16, "z": 4}


class Reduce:
    scatter = ("dp", "xy")
    last = "z"

    def __init__(self, ring, rows, bufs, recvs, slots, out, send, recv, sent):
        self.ring = ring
        self.bufs = bufs
        self.recvs = recvs
        self.slots = slots
        self.out = out
        self.send = send
        self.recv = recv
        self.sent = sent
        self.used = 0
        self.rows = [rows]
        self.offs = [0]
        for kind in self.scatter:
            n = self.rows[-1] // SIZE[kind]
            self.offs.append(self.offs[-1] + ring.member(kind) * n)
            self.rows.append(n)

    def _go(self, src, dst, device):
        i = self.used
        self.used += 1
        c = pltpu.make_async_remote_copy(
            src_ref=src,
            dst_ref=dst,
            send_sem=self.send.at[i],
            recv_sem=self.recv.at[i],
            device_id=device,
            device_id_type=MESH,
        )
        c.start()
        self.sent.append(c)
        return c

    def scatter_start(self, s):
        kind, n = self.scatter[s], self.rows[s + 1]
        self.now = []
        for r, p in enumerate(self.ring.others(kind)):
            src = self.bufs[s].at[pl.ds(pl.multiple_of(p * n, 16), n)]
            self.now.append(self._go(src, self.recvs[s].at[r], self.ring.device(kind, p)))

    def scatter_end(self, s):
        kind, n = self.scatter[s], self.rows[s + 1]
        m, size = self.ring.member(kind), SIZE[kind]
        for c in self.now:
            c.wait_recv()
        total = self.bufs[s][pl.ds(pl.multiple_of(m * n, 16), n), :].astype(F32)
        for r in range(size - 1):
            total = total + self.recvs[s][r].astype(F32)
        total = total.astype(BF)
        if s + 1 < len(self.scatter):
            self.bufs[s + 1][...] = total
        else:
            self.slots[self.ring.member(self.last)] = total

    def last_start(self):
        m = self.ring.member(self.last)
        self.now = []
        for p in self.ring.others(self.last):
            self.now.append(self._go(self.slots.at[m], self.slots.at[m], self.ring.device(self.last, p)))

    def last_end(self):
        for c in self.now:
            c.wait_recv()
        total = self.slots[0].astype(F32)
        for r in range(1, SIZE[self.last]):
            total = total + self.slots[r].astype(F32)
        self.out[pl.ds(pl.multiple_of(self.offs[-1], 16), self.rows[-1]), :] = total.astype(BF)

    def gather_start(self, s):
        kind, n = self.scatter[s], self.rows[s + 1]
        part = self.out.at[pl.ds(pl.multiple_of(self.offs[s + 1], 16), n)]
        self.now = []
        for p in self.ring.others(kind):
            self.now.append(self._go(part, part, self.ring.device(kind, p)))

    def gather_end(self):
        for c in self.now:
            c.wait_recv()


def pack4(b):
    lane = lanes(b[0].shape)
    r1, r2, r3 = pltpu.roll(b[1], 96, 1), pltpu.roll(b[2], 64, 1), pltpu.roll(b[3], 32, 1)
    return (
        jnp.where(lane >= 96, r1, b[0]),
        jnp.where(lane < 64, r1, r2),
        jnp.where(lane < 32, r2, r3),
    )


def unpack4(d):
    lane = lanes(d[0].shape)
    return (
        d[0],
        pltpu.roll(jnp.where(lane >= 96, d[0], d[1]), 32, 1),
        pltpu.roll(jnp.where(lane >= 64, d[1], d[2]), 64, 1),
        pltpu.roll(d[2], 96, 1),
    )


def kernel(
    a_hbm, wf_hbm, we_hbm, wm_hbm, wl_hbm, u_hbm,
    mixed_hbm, ig_hbm, mout, eout, fout,
    a_ref, wf_ref, we_ref, wm_ref, wl_ref, u_ref, mixed_ref, ig_ref, in_sem, out_sem,
    raw, raw2, pad2, pad3, ulp, e32, x3, g3f, fa, q, c1p, c2, gp, gup, d32,
    wf, wft, we, wet, wm, wmt, wl, are32, arf32,
    sbuf, rbuf, h_send, h_recv,
    m0, m1, mr0, mr1, mslot, m_send, m_recv,
    e0, e1, er0, er1, eslot, e_send, e_recv,
    f0, f1, fr0, fr1, fslot, f_send, f_recv,
):
    ring = Ring()
    dp, gy, gx = ring.dp, ring.gy, ring.gx

    barrier = pltpu.get_barrier_semaphore()
    met = [(dp, (gy + dy + GY) % GY, (gx + dx + GX) % GX) for dy, dx in DIRS]
    met += [ring.device(kind, p) for kind in ("dp", "xy") for p in ring.others(kind)]
    for device in met:
        pl.semaphore_signal(barrier, inc=1, device_id=device, device_id_type=MESH)

    loads = [
        pltpu.make_async_copy(src, dst, in_sem.at[i])
        for i, (src, dst) in enumerate(
            (
                (a_hbm, a_ref), (u_hbm, u_ref), (wf_hbm, wf_ref),
                (we_hbm, we_ref), (wm_hbm, wm_ref), (wl_hbm, wl_ref),
            )
        )
    ]
    for c in loads:
        c.start()

    sent = []

    def edge(step, n, w):
        return {1: slice(n, n + w), -1: slice(w, 2 * w), 0: slice(w, n + w)}[step]

    def outside(step, n, w):
        return {1: slice(0, w), -1: slice(n + w, n + 2 * w), 0: slice(w, n + w)}[step]

    def send_halo(ex, ref, n, w):
        copies = []
        for d, (dy, dx) in enumerate(DIRS):
            part = ref[edge(dy, n, w), edge(dx, n, w)].reshape(-1, L)
            if part.shape[0] % 16:
                part = jnp.concatenate([part, part[:Z]], axis=0)
            rows = part.shape[0]
            sbuf[ex, d, 0:rows, :] = part.astype(BF)
            c = pltpu.make_async_remote_copy(
                src_ref=sbuf.at[ex, d, pl.ds(0, rows)],
                dst_ref=rbuf.at[ex, d, pl.ds(0, rows)],
                send_sem=h_send.at[ex * 8 + d],
                recv_sem=h_recv.at[ex * 8 + d],
                device_id=(dp, (gy + dy + GY) % GY, (gx + dx + GX) % GX),
                device_id_type=MESH,
            )
            c.start()
            sent.append(c)
            copies.append(c)
        return copies

    def take_halo(ex, ref, n, w, copies):
        for d, (dy, dx) in enumerate(DIRS):
            copies[d].wait_recv()
            there = jnp.logical_and(
                jnp.logical_and(gy - dy >= 0, gy - dy < GY),
                jnp.logical_and(gx - dx >= 0, gx - dx < GX),
            )
            keep = jnp.where(there, 1.0, 0.0).astype(F32)
            ys, xs = outside(dy, n, w), outside(dx, n, w)
            ny, nx = ys.stop - ys.start, xs.stop - xs.start
            part = rbuf[ex, d, 0 : max(ny * nx * Z, 16), :].astype(F32)[: ny * nx * Z]
            ref[ys, xs] = (part * keep).reshape(ny, nx, Z, L)

    def spread(src_ref):
        for t in range(TILES):
            raw[t] = src_ref[0, :, :, t * L : (t + 1) * L].astype(F32).reshape(Z * N2, L)

    def read_row(y, xs, dst, shift):
        lane = lanes((Z, L))
        tiles = {}
        for x in xs:
            t, o = (x * C2) // L, (x * C2) % L
            for s in (t, t + 1) if o + C2 > L else (t,):
                if s not in tiles:
                    tiles[s] = raw[s, pl.ds(y, Z, stride=N2), :]
            cell = tiles[t] if o == 0 else pltpu.roll(tiles[t], L - o, 1)
            if o + C2 > L:
                cell = jnp.where(lane < L - o, cell, pltpu.roll(tiles[t + 1], L - o, 1))
            dst[y + shift, x + shift] = jnp.where(lane < C2, cell, 0.0)

    def read_rows(first, last, xs, dst, shift):
        def row(y, _):
            read_row(y, xs, dst, shift)
            return 0

        lax.fori_loop(first, last, row, 0)

    def write_cells(src, out32, dst_ref):
        def row(y, _):
            tiles = [None] * TILES
            lane = lanes((Z, L))
            for x in range(N2):
                t, o = (x * C2) // L, (x * C2) % L
                cell = src[y, x]
                cell = cell if o == 0 else pltpu.roll(cell, o, 1)
                tiles[t] = cell if o == 0 else jnp.where(lane >= o, cell, tiles[t])
                if o + C2 > L:
                    tiles[t + 1] = cell
            for t in range(TILES):
                out32[t, pl.ds(y, Z, stride=N2), :] = tiles[t]
            return 0

        lax.fori_loop(0, N2, row, 0)
        for t in range(TILES):
            dst_ref[0, :, :, t * L : (t + 1) * L] = out32[t].reshape(Z, N2, L).astype(BF)

    def fine_columns():
        def row(y, _):
            for k in range(3):
                x3[y, :, k * L : (k + 1) * L] = pad2[y, k : k + N2].reshape(N2 * Z, L).astype(BF)
            return 0

        lax.fori_loop(0, N2 + 2, row, 0)

    def fine_rows(chunk):
        parts = [x3[pl.ds(chunk * 4 + j, 4)].reshape(4 * N2 * Z, 3 * L) for j in range(3)]
        return jnp.concatenate(parts, axis=1)

    def columns(ref, n, off=0):
        rows = n * n * Z
        for j in range(3):
            for k in range(3):
                t = (j * 3 + k) * L
                q[0:rows, t : t + L] = (
                    ref[off + j : off + j + n, off + k : off + k + n].reshape(rows, L).astype(BF)
                )
        return q[0:rows, :]

    def joined(acc):
        acc = acc.reshape(-1, Z, 3 * L)
        return shift_z(acc[:, :, 0:L], 1) + acc[:, :, L : 2 * L] + shift_z(acc[:, :, 2 * L :], -1)

    def coarse_weight_grad(taps, g):
        g3 = jnp.concatenate([shift_z(g, -1), g, shift_z(g, 1)], axis=2)
        g3 = g3.reshape(N3 * N3 * Z, 3 * L).astype(BF)
        return tn(taps, g3).reshape(9, L, 3 * L)

    loads[0].wait()
    spread(a_ref)
    read_row(0, range(N2), pad2, 1)
    read_row(N2 - 1, range(N2), pad2, 1)
    read_rows(1, N2 - 1, (0, N2 - 1), pad2, 1)
    pl.semaphore_wait(barrier, len(met))
    copies = send_halo(EX_IN, pad2, N2, 1)

    read_rows(1, N2 - 1, range(1, N2 - 1), pad2, 1)
    for s in (0, N2 + 1):
        pad2[s] = jnp.zeros((N2 + 2, Z, L), F32)
        pad2[:, s : s + 1] = jnp.zeros((N2 + 2, 1, Z, L), F32)
    for c in loads[1:]:
        c.wait()
    wf[...] = jnp.zeros(wf.shape, BF)
    for j in range(3):
        for k in range(3):
            t = (j * 3 + k) * L
            wf[t : t + C2, 0:C2] = wf_ref[j, k]
    fine_columns()

    def fine_forward(chunk, _):
        act = rounded(elu(nn(fine_rows(chunk), wf[...])))
        fa[pl.ds(chunk * 4, 4)] = act.reshape(4, N2, Z, L)
        return 0

    lax.fori_loop(0, 4, fine_forward, 0)

    take_halo(EX_IN, pad2, N2, 1, copies)
    inner = N2 - 2
    for j in range(3):
        for k in range(3):
            t = (j * 3 + k) * L
            at = 0
            for ys, xs in (
                (slice(j, j + 1), slice(k, k + N2)),
                (slice(N2 - 1 + j, N2 + j), slice(k, k + N2)),
                (slice(1 + j, 1 + j + inner), slice(k, k + 1)),
                (slice(1 + j, 1 + j + inner), slice(N2 - 1 + k, N2 + k)),
            ):
                part = pad2[ys, xs].reshape(-1, L).astype(BF)
                q[at : at + part.shape[0], t : t + L] = part
                at += part.shape[0]
    rim = rounded(elu(nn(q[0:at, :], wf[...]))).reshape(-1, Z, L)
    fa[0] = rim[0:N2]
    fa[N2 - 1] = rim[N2 : 2 * N2]
    fa[1 : N2 - 1, 0:1] = rim[2 * N2 : 2 * N2 + inner].reshape(inner, 1, Z, L)
    fa[1 : N2 - 1, N2 - 1 : N2] = rim[2 * N2 + inner :].reshape(inner, 1, Z, L)
    v = fa[...].reshape(N3, 2, N3, 2, Z, L)
    v = (v[:, 0, :, 0] + v[:, 0, :, 1]) + (v[:, 1, :, 0] + v[:, 1, :, 1])
    pad3[3 : N3 + 3, 3 : N3 + 3] = rounded(0.25 * v)
    copies = send_halo(EX_POOL, pad3, N3, 3)

    spread(u_ref)
    read_rows(0, N2, range(N2), e32, 0)
    low = e32[...].reshape(N3, 2, N3, 2, Z, L)
    low = (low[:, 0, :, 0] + low[:, 0, :, 1]) + (low[:, 1, :, 0] + low[:, 1, :, 1])
    ulp[1 : N3 + 1, 1 : N3 + 1] = rounded(low)
    low_copies = send_halo(EX_LOW, ulp, N3, 1)
    for ref in (wft, we, wet, wm, wmt, wl):
        ref[...] = jnp.zeros(ref.shape, BF)
    wl[0:C2, 0:C3] = wl_ref[...]
    for j in range(3):
        for k in range(3):
            t = (j * 3 + k) * L
            wft[0:C2, t : t + C2] = wf_ref[2 - j, 2 - k]
            for i in range(3):
                we[t : t + C2, i * L : i * L + C3] = we_ref[i, j, k]
                wm[t : t + C3, i * L : i * L + C3] = wm_ref[i, j, k]
                wet[i * L : i * L + C2, t : t + C3] = we_ref[2 - i, 2 - j, 2 - k]
                wmt[i * L : i * L + C3, t : t + C3] = wm_ref[2 - i, 2 - j, 2 - k]
    fine_columns()

    take_halo(EX_POOL, pad3, N3, 3, copies)
    c1p[...] = rounded(elu(joined(nn(columns(pad3, N3 + 4), we[...])))).reshape(N3 + 4, N3 + 4, Z, L)
    for there, ys, xs in (
        (gy > 0, slice(0, 2), slice(None)),
        (gy < GY - 1, slice(N3 + 2, N3 + 4), slice(None)),
        (gx > 0, slice(None), slice(0, 2)),
        (gx < GX - 1, slice(None), slice(N3 + 2, N3 + 4)),
    ):
        c1p[ys, xs] = c1p[ys, xs] * jnp.where(there, 1.0, 0.0).astype(F32)
    two = rounded(elu(joined(nn(columns(c1p, N3 + 2), wm[...]))))
    c2[...] = two.reshape(N3 + 2, N3 + 2, Z, L)
    take_halo(EX_LOW, ulp, N3, 1, low_copies)
    back = nn(ulp[...].reshape(-1, L).astype(BF), wl[...]).reshape(-1, Z, L)
    gp[...] = rounded(back * slope(two)).reshape(N3 + 2, N3 + 2, Z, L)
    own = c1p[2 : N3 + 2, 2 : N3 + 2].reshape(-1, Z, L)
    g1 = rounded(joined(nt(columns(gp, N3), wmt[...])) * slope(own))
    gup[1 : N3 + 1, 1 : N3 + 1] = g1.reshape(N3, N3, Z, L)
    copies = send_halo(EX_G1, gup, N3, 1)

    mid = coarse_weight_grad(
        columns(c1p, N3, 1), gp[1 : N3 + 1, 1 : N3 + 1].reshape(-1, Z, L)
    )
    two = c2[1 : N3 + 1, 1 : N3 + 1].reshape(-1, L).astype(BF)
    lift_grad = tn(ulp[1 : N3 + 1, 1 : N3 + 1].reshape(-1, L).astype(BF), two)
    blocks = [mid[t, :C3, i * L : (i + 1) * L] for i in range(3) for t in range(9)]
    blocks.append(lift_grad[:C3])
    for g in range(7):
        for d, part in enumerate(pack4(blocks[4 * g : 4 * g + 4])):
            m0[(g * 3 + d) * C3 : (g * 3 + d + 1) * C3, :] = part.astype(BF)
    m0[21 * C3 :, :] = jnp.zeros((ROWS_M - 21 * C3, L), BF)
    red_m = Reduce(ring, ROWS_M, (m0, m1), (mr0, mr1), mslot, mout, m_send, m_recv, sent)
    red_m.scatter_start(0)
    ent = coarse_weight_grad(columns(pad3, N3, 2), gup[1 : N3 + 1, 1 : N3 + 1].reshape(-1, Z, L))
    blocks = [ent[t, :C2, i * L : (i + 1) * L] for i in range(3) for t in range(9)]
    blocks.append(jnp.zeros((C2, L), F32))
    for g in range(7):
        for d, part in enumerate(pack4(blocks[4 * g : 4 * g + 4])):
            are32[(g * 3 + d) * C2 : (g * 3 + d + 1) * C2, :] = part
    are32[21 * C2 :, :] = jnp.zeros((ROWS_E - 21 * C2, L), F32)
    e0[...] = are32[...].astype(BF)
    red_e = Reduce(ring, ROWS_E, (e0, e1), (er0, er1), eslot, eout, e_send, e_recv, sent)
    red_e.scatter_start(0)
    red_m.scatter_end(0)
    red_m.scatter_start(1)

    take_halo(EX_G1, gup, N3, 1, copies)
    low = rounded(joined(nt(columns(gup, N3), wet[...])))
    gup[0:N3, 0:N3] = 0.25 * low.reshape(N3, N3, Z, L)
    red_e.scatter_end(0)
    red_e.scatter_start(1)

    for j in range(3):
        for y in range(N2 + 2):
            if not 0 <= y - j < N2:
                g3f[y, :, j * L : (j + 1) * L] = jnp.zeros((N2 * Z, L), BF)

    def fine_back(y, _):
        act = fa[pl.ds(y * 2, 2)].reshape(2, N3, 2, Z, L)
        e = e32[pl.ds(y * 2, 2)].reshape(2, N3, 2, Z, L)
        up = gup[pl.ds(y, 1), 0:N3].reshape(1, N3, 1, Z, L)
        g = ((e + up) * slope(act)).reshape(2, N2 * Z, L).astype(BF)
        for j in range(3):
            g3f[pl.ds(y * 2 + j, 2), :, j * L : (j + 1) * L] = g
        pad2[pl.ds(y * 2 + 1, 2), 1 : N2 + 1] = g.astype(F32).reshape(2, N2, Z, L)
        return 0

    lax.fori_loop(0, N3, fine_back, 0)
    copies = send_halo(EX_FINE, pad2, N2, 1)

    grad = tn(x3[...].reshape(-1, 3 * L), g3f[...].reshape(-1, 3 * L))
    for k in range(3):
        b0, b1, b2 = [grad[k * L : k * L + C2, j * L : (j + 1) * L] for j in range(3)]
        lane = lanes(b0.shape)
        r1, r2 = pltpu.roll(b1, C2, 1), pltpu.roll(b2, 2 * C2 - L, 1)
        arf32[2 * k * C2 : (2 * k + 1) * C2, :] = jnp.where(lane < C2, b0, r1)
        arf32[(2 * k + 1) * C2 : (2 * k + 2) * C2, :] = jnp.where(lane < 2 * C2 - L, r1, r2)
    arf32[6 * C2 :, :] = jnp.zeros((ROWS_F - 6 * C2, L), F32)
    f0[...] = arf32[...].astype(BF)
    red_f = Reduce(ring, ROWS_F, (f0, f1), (fr0, fr1), fslot, fout, f_send, f_recv, sent)
    red_f.scatter_start(0)
    red_m.scatter_end(1)
    red_m.last_start()
    red_f.scatter_end(0)
    red_f.scatter_start(1)

    two = c2[1 : N3 + 1, 1 : N3 + 1].reshape(-1, L).astype(BF)
    gup[0:N3, 0:N3] = rounded(nt(two, wl[...])).reshape(N3, N3, Z, L)

    def mix(y, _):
        act = fa[pl.ds(y * 2, 2)].reshape(2, N3, 2, Z, L)
        up = gup[pl.ds(y, 1), 0:N3].reshape(1, N3, 1, Z, L)
        d32[pl.ds(y * 2, 2)] = (act + up).reshape(2, N2, Z, L)
        return 0

    lax.fori_loop(0, N3, mix, 0)

    red_e.scatter_end(1)
    red_e.last_start()
    red_m.last_end()
    red_m.gather_start(1)

    write_cells(d32, raw, mixed_ref)
    stores = [pltpu.make_async_copy(mixed_ref, mixed_hbm, out_sem.at[0])]
    stores[0].start()

    red_f.scatter_end(1)
    red_f.last_start()
    red_e.last_end()
    red_e.gather_start(1)

    take_halo(EX_FINE, pad2, N2, 1, copies)
    fine_columns()

    def fine_backward(chunk, _):
        d32[pl.ds(chunk * 4, 4)] = nt(fine_rows(chunk), wft[...]).reshape(4, N2, Z, L)
        return 0

    lax.fori_loop(0, 4, fine_backward, 0)

    red_f.last_end()
    red_f.gather_start(1)

    write_cells(d32, raw2, ig_ref)
    stores.append(pltpu.make_async_copy(ig_ref, ig_hbm, out_sem.at[1]))
    stores[1].start()

    red_m.gather_end()
    red_m.gather_start(0)
    red_e.gather_end()
    red_e.gather_start(0)
    red_f.gather_end()
    red_f.gather_start(0)
    for c in stores:
        c.wait()
    red_m.gather_end()
    red_e.gather_end()
    red_f.gather_end()
    for c in sent:
        c.wait_send()


def finish(mixed_in, ig_in, mout, eout, fout, mixed, ig, gf_ref, ge_ref, gm_ref, gl_ref, are32, arf32, sem):
    copies = [
        pltpu.make_async_copy(mixed_in, mixed, sem.at[0]),
        pltpu.make_async_copy(ig_in, ig, sem.at[1]),
    ]
    for c in copies:
        c.start()
    for g in range(7):
        d = [mout[(g * 3 + s) * C3 : (g * 3 + s + 1) * C3, :].astype(F32) for s in range(3)]
        for s, b in enumerate(unpack4(d)):
            t = g * 4 + s
            if t < 27:
                gm_ref[t // 9, (t // 3) % 3, t % 3] = b[:, 0:C3]
            else:
                gl_ref[...] = b[0:C2, 0:C3]
    are32[...] = eout[...].astype(F32)
    for g in range(7):
        d = [are32[(g * 3 + s) * C2 : (g * 3 + s + 1) * C2, :] for s in range(3)]
        for s, b in enumerate(unpack4(d)):
            t = g * 4 + s
            if t < 27:
                ge_ref[t // 9, (t // 3) % 3, t % 3] = b[:, 0:C3]
    arf32[...] = fout[...].astype(F32)
    for k in range(3):
        d0 = arf32[2 * k * C2 : (2 * k + 1) * C2, :]
        d1 = arf32[(2 * k + 1) * C2 : (2 * k + 2) * C2, :]
        lane = lanes(d0.shape)
        b1 = pltpu.roll(jnp.where(lane >= C2, d0, d1), L - C2, 1)
        b2 = pltpu.roll(d1, 2 * L - 2 * C2, 1)
        for j, b in enumerate((d0, b1, b2)):
            gf_ref[j, k] = b[:, 0:C2]
    for c in copies:
        c.wait()


def body(fine_input, fine_weight, entry_weight, middle_weight, lift_weight, upstream):
    args = (fine_input, fine_weight, entry_weight, middle_weight, lift_weight.T, upstream)
    field = jax.ShapeDtypeStruct(fine_input.shape, BF)
    vmem = pl.BlockSpec(memory_space=pltpu.VMEM)
    whole = pl.BlockSpec(memory_space=pl.ANY)
    cells3 = (N3 + 4) * (N3 + 4) * Z

    def v(*shape):
        return pltpu.VMEM(shape, BF)

    def w(*shape):
        return pltpu.VMEM(shape, F32)

    def sems(n):
        return [pltpu.SemaphoreType.DMA((n,)), pltpu.SemaphoreType.DMA((n,))]

    def sums(rows):
        return [
            v(rows, L), v(rows // 2, L),
            v(1, rows // 2, L), v(15, rows // 32, L), v(4, rows // 32, L),
            *sems(35),
        ]

    scratch = [
        *[v(*arg.shape) for arg in args], v(*field.shape), v(*field.shape), *sems(6),
        w(TILES, Z * N2, L), w(TILES, Z * N2, L), w(N2 + 2, N2 + 2, Z, L), w(N3 + 6, N3 + 6, Z, L),
        w(N3 + 2, N3 + 2, Z, L), w(N2, N2, Z, L),
        v(N2 + 2, N2 * Z, 3 * L), v(N2 + 2, N2 * Z, 3 * L), w(N2, N2, Z, L),
        v(cells3, 9 * L), w(N3 + 4, N3 + 4, Z, L), w(N3 + 2, N3 + 2, Z, L), w(N3 + 2, N3 + 2, Z, L),
        w(N3 + 2, N3 + 2, Z, L), w(N2, N2, Z, L),
        v(9 * L, L), v(L, 9 * L), v(9 * L, 3 * L), v(3 * L, 9 * L), v(9 * L, 3 * L), v(3 * L, 9 * L), v(L, L),
        w(ROWS_E, L), w(ROWS_F, L),
        v(5, 8, 3 * N3 * Z, L), v(5, 8, 3 * N3 * Z, L), *sems(40),
        *sums(ROWS_M), *sums(ROWS_E), *sums(ROWS_F),
    ]
    packed = [jax.ShapeDtypeStruct((rows, L), BF) for rows in (ROWS_M, ROWS_E, ROWS_F)]
    fields_and_sums = pl.pallas_call(
        kernel,
        out_shape=(field, field, *packed),
        in_specs=[whole] * 6,
        out_specs=[whole] * 2 + [vmem] * 3,
        scratch_shapes=scratch,
        compiler_params=pltpu.CompilerParams(
            collective_id=0, has_side_effects=True, vmem_limit_bytes=60 * 1024 * 1024
        ),
    )(*args)
    mixed, input_grad, fine, entry, middle, lift = pl.pallas_call(
        finish,
        out_shape=(
            field,
            field,
            jax.ShapeDtypeStruct(fine_weight.shape, F32),
            jax.ShapeDtypeStruct(entry_weight.shape, F32),
            jax.ShapeDtypeStruct(middle_weight.shape, F32),
            jax.ShapeDtypeStruct(lift_weight.shape[::-1], F32),
        ),
        in_specs=[whole] * 2 + [vmem] * 3,
        out_specs=[whole] * 2 + [vmem] * 4,
        scratch_shapes=[w(ROWS_E, L), w(ROWS_F, L), pltpu.SemaphoreType.DMA((2,))],
        compiler_params=pltpu.CompilerParams(vmem_limit_bytes=32 * 1024 * 1024),
    )(*fields_and_sums)
    return mixed, input_grad, fine, entry, middle, lift.T


def solution(mesh):
    assert mesh.shape["gy"] == GY and mesh.shape["gx"] == GX
    return jax.shard_map(
        body,
        mesh=mesh,
        in_specs=(P("dp", None, "gy", "gx"), P(), P(), P(), P(), P("dp", None, "gy", "gx")),
        out_specs=(P("dp", None, "gy", "gx"), P("dp", None, "gy", "gx"), P(), P(), P(), P()),
        check_vma=False,
    )
```

```python
import jax
import jax.numpy as jnp
from jax import lax
from jax.experimental import pallas as pl
from jax.experimental.pallas import tpu as pltpu
from jax.sharding import PartitionSpec as P

MESH = pl.DeviceIdType.MESH
BF = jnp.bfloat16
F32 = jnp.float32

Z = 8
N2 = 16
N3 = 8
C2 = 72
C3 = 96
L = 128
GY = 8
GX = 8
MERGED = N2 * C2
TILES = MERGED // L
DIRS = [(-1, 0), (1, 0), (-1, -1), (-1, 1), (1, -1), (1, 1), (0, -1), (0, 1)]

EX_IN, EX_POOL, EX_LOW, EX_G1, EX_FINE = range(5)

ROWS_M = 2048
ROWS_E = 1536
ROWS_F = 512
ROWS = (ROWS_M, ROWS_E, ROWS_F)
PITCH = 80


def lanes(shape):
    return lax.broadcasted_iota(jnp.int32, shape, len(shape) - 1)


def elu(v):
    return jnp.where(v > 0, v, jnp.exp(jnp.minimum(v, 0.0)) - 1.0)


def slope(s):
    return jnp.where(s > 0, 1.0, 1.0 + s)


def rounded(v):
    return v.astype(BF).astype(F32)


def shift_z(v, step):
    moved = pltpu.roll(v, step % Z, 1)
    row = lax.broadcasted_iota(jnp.int32, v.shape, 1)
    return jnp.where(row == (0 if step == 1 else Z - 1), 0.0, moved)


def nt(a, b):
    return lax.dot_general(a, b, (((1,), (1,)), ((), ())), preferred_element_type=F32)


def tn(a, b):
    return lax.dot_general(a, b, (((0,), (0,)), ((), ())), preferred_element_type=F32)


def nn(a, b):
    return jnp.dot(a, b, preferred_element_type=F32)


class Ring:
    def __init__(self):
        self.dp = lax.axis_index("dp")
        self.gy = lax.axis_index("gy")
        self.gx = lax.axis_index("gx")

    def member(self, kind):
        if kind == "dp":
            return self.dp
        if kind == "y":
            return self.gx // 2
        if kind == "x":
            return self.gy // 2
        if kind == "xy":
            return (self.gy // 2) * 4 + self.gx // 2
        return (self.gy % 2) * 2 + self.gx % 2

    def device(self, kind, p):
        if kind == "dp":
            return (p, self.gy, self.gx)
        if kind == "y":
            return (self.dp, self.gy, p * 2 + self.gx % 2)
        if kind == "x":
            return (self.dp, p * 2 + self.gy % 2, self.gx)
        if kind == "xy":
            return (self.dp, (p // 4) * 2 + self.gy % 2, (p % 4) * 2 + self.gx % 2)
        return (self.dp, (self.gy // 2) * 2 + p // 2, (self.gx // 2) * 2 + p % 2)

    def others(self, kind):
        m = self.member(kind)
        if kind == "dp":
            return [1 - m]
        if kind in ("x", "y", "z"):
            return [(m + r) % 4 for r in (2, 1, 3)]
        steps = [(2, 2), (2, 1), (1, 2), (2, 3), (3, 2), (1, 1), (1, 3), (3, 1), (3, 3)]
        steps += [(2, 0), (0, 2), (1, 0), (0, 1), (3, 0), (0, 3)]
        return [((m // 4 + x) % 4) * 4 + (m % 4 + y) % 4 for x, y in steps]


SIZE = {"dp": 2, "x": 4, "y": 4, "xy": 16, "z": 4}


class Reduce:
    last = "z"

    def __init__(self, ring, rows, scatter, bufs, recvs, slots, out, send, recv, sent):
        self.ring = ring
        self.scatter = scatter
        self.bufs = bufs
        self.recvs = recvs
        self.slots = slots
        self.out = out
        self.send = send
        self.recv = recv
        self.sent = sent
        self.used = 0
        self.rows = [rows]
        self.offs = [0]
        for kind in self.scatter:
            n = self.rows[-1] // SIZE[kind]
            self.offs.append(self.offs[-1] + ring.member(kind) * n)
            self.rows.append(n)

    def _go(self, src, dst, device):
        i = self.used
        self.used += 1
        c = pltpu.make_async_remote_copy(
            src_ref=src,
            dst_ref=dst,
            send_sem=self.send.at[i],
            recv_sem=self.recv.at[i],
            device_id=device,
            device_id_type=MESH,
        )
        c.start()
        self.sent.append(c)
        return c

    def scatter_start(self, s):
        kind, n = self.scatter[s], self.rows[s + 1]
        self.now = []
        for r, p in enumerate(self.ring.others(kind)):
            src = self.bufs[s].at[pl.ds(pl.multiple_of(p * n, 16), n)]
            self.now.append(self._go(src, self.recvs[s].at[r], self.ring.device(kind, p)))

    def scatter_end(self, s):
        kind, n = self.scatter[s], self.rows[s + 1]
        m, size = self.ring.member(kind), SIZE[kind]
        for c in self.now:
            c.wait_recv()
        total = self.bufs[s][pl.ds(pl.multiple_of(m * n, 16), n), :].astype(F32)
        for r in range(size - 1):
            total = total + self.recvs[s][r].astype(F32)
        total = total.astype(BF)
        if s + 1 < len(self.scatter):
            self.bufs[s + 1][...] = total
        else:
            self.slots[self.ring.member(self.last)] = total

    def last_start(self):
        m = self.ring.member(self.last)
        self.now = []
        for p in self.ring.others(self.last):
            self.now.append(self._go(self.slots.at[m], self.slots.at[m], self.ring.device(self.last, p)))

    def last_end(self):
        for c in self.now:
            c.wait_recv()
        total = self.slots[0].astype(F32)
        for r in range(1, SIZE[self.last]):
            total = total + self.slots[r].astype(F32)
        self.out[pl.ds(pl.multiple_of(self.offs[-1], 16), self.rows[-1]), :] = total.astype(BF)

    def gather_start(self, s):
        kind, n = self.scatter[s], self.rows[s + 1]
        part = self.out.at[pl.ds(pl.multiple_of(self.offs[s + 1], 16), n)]
        self.now = []
        for p in self.ring.others(kind):
            self.now.append(self._go(part, part, self.ring.device(kind, p)))

    def gather_end(self):
        for c in self.now:
            c.wait_recv()


def pack4(b):
    lane = lanes(b[0].shape)
    r1, r2, r3 = pltpu.roll(b[1], 96, 1), pltpu.roll(b[2], 64, 1), pltpu.roll(b[3], 32, 1)
    return (
        jnp.where(lane >= 96, r1, b[0]),
        jnp.where(lane < 64, r1, r2),
        jnp.where(lane < 32, r2, r3),
    )


def unpack4(d):
    lane = lanes(d[0].shape)
    return (
        d[0],
        pltpu.roll(jnp.where(lane >= 96, d[0], d[1]), 32, 1),
        pltpu.roll(jnp.where(lane >= 64, d[1], d[2]), 64, 1),
        pltpu.roll(d[2], 96, 1),
    )


def kernel(
    a_hbm, wf_hbm, we_hbm, wm_hbm, wl_hbm, u_hbm,
    mixed_hbm, ig_hbm, m_hbm, e_hbm, f_hbm,
    a_ref, wf_ref, we_ref, wm_ref, wl_ref, u_ref, mixed_ref, ig_ref, mout, eout, fout, mflat, eflat, in_sem, out_sem,
    raw, raw2, pad2, pad3, ulp, e32, x3, g3f, fa, q, c1p, c2, gp, gup, up, gsum, grim, d32,
    wf, wft, we, wet, wm, wmt, wl, are32, arf32,
    sbuf, rbuf, h_send, h_recv,
    m0, m1, mr0, mr1, mslot, m_send, m_recv,
    e0, e1, er0, er1, eslot, e_send, e_recv,
    f0, f1, fr0, fr1, fslot, f_send, f_recv,
):
    ring = Ring()
    dp, gy, gx = ring.dp, ring.gy, ring.gx

    loads = [
        pltpu.make_async_copy(src, dst, in_sem.at[i])
        for i, (src, dst) in enumerate(
            (
                (a_hbm, a_ref), (u_hbm, u_ref), (wf_hbm, wf_ref),
                (we_hbm, we_ref), (wm_hbm, wm_ref), (wl_hbm, wl_ref),
            )
        )
    ]
    for load in loads:
        load.start()

    barrier = pltpu.get_barrier_semaphore()
    met = [(dp, (gy + dy + GY) % GY, (gx + dx + GX) % GX) for dy, dx in DIRS]
    met += [ring.device(kind, p) for kind in ("dp", "xy") for p in ring.others(kind)]
    for device in met:
        pl.semaphore_signal(barrier, inc=1, device_id=device, device_id_type=MESH)

    sent = []
    stores = []

    def store(src, dst):
        stores.append(pltpu.make_async_copy(src, dst, out_sem.at[len(stores)]))
        stores[-1].start()

    def edge(step, n, w):
        return {1: slice(n, n + w), -1: slice(w, 2 * w), 0: slice(w, n + w)}[step]

    def outside(step, n, w):
        return {1: slice(0, w), -1: slice(n + w, n + 2 * w), 0: slice(w, n + w)}[step]

    def send_halo(ex, ref, n, w):
        copies = []
        for d, (dy, dx) in enumerate(DIRS):
            part = ref[edge(dy, n, w), edge(dx, n, w)].reshape(-1, L)
            if part.shape[0] % 16:
                part = jnp.concatenate([part, part[:Z]], axis=0)
            rows = part.shape[0]
            sbuf[ex, d, 0:rows, :] = part.astype(BF)
            c = pltpu.make_async_remote_copy(
                src_ref=sbuf.at[ex, d, pl.ds(0, rows)],
                dst_ref=rbuf.at[ex, d, pl.ds(0, rows)],
                send_sem=h_send.at[ex * 8 + d],
                recv_sem=h_recv.at[ex * 8 + d],
                device_id=(dp, (gy + dy + GY) % GY, (gx + dx + GX) % GX),
                device_id_type=MESH,
            )
            c.start()
            sent.append(c)
            copies.append(c)
        return copies

    def take_halo(ex, ref, n, w, copies):
        for d, (dy, dx) in enumerate(DIRS):
            copies[d].wait_recv()
            there = jnp.logical_and(
                jnp.logical_and(gy - dy >= 0, gy - dy < GY),
                jnp.logical_and(gx - dx >= 0, gx - dx < GX),
            )
            keep = jnp.where(there, 1.0, 0.0).astype(F32)
            ys, xs = outside(dy, n, w), outside(dx, n, w)
            ny, nx = ys.stop - ys.start, xs.stop - xs.start
            part = rbuf[ex, d, 0 : max(ny * nx * Z, 16), :].astype(F32)[: ny * nx * Z]
            ref[ys, xs] = (part * keep).reshape(ny, nx, Z, L)

    def spread(src_ref):
        for t in range(TILES):
            raw[t] = src_ref[0, :, :, t * L : (t + 1) * L].astype(F32).reshape(Z * N2, L)

    def read_row(y, xs, dst, shift):
        lane = lanes((Z, L))
        tiles = {}
        for x in xs:
            t, o = (x * C2) // L, (x * C2) % L
            for s in (t, t + 1) if o + C2 > L else (t,):
                if s not in tiles:
                    tiles[s] = raw[s, pl.ds(y, Z, stride=N2), :]
            cell = tiles[t] if o == 0 else pltpu.roll(tiles[t], L - o, 1)
            if o + C2 > L:
                cell = jnp.where(lane < L - o, cell, pltpu.roll(tiles[t + 1], L - o, 1))
            dst[y + shift, x + shift] = jnp.where(lane < C2, cell, 0.0)

    def read_rows(first, last, xs, dst, shift):
        def row(y, _):
            read_row(y, xs, dst, shift)
            return 0

        lax.fori_loop(first, last, row, 0)

    def write_cells(src, out32, dst_ref):
        def row(y, _):
            tiles = [None] * TILES
            lane = lanes((Z, L))
            for x in range(N2):
                t, o = (x * C2) // L, (x * C2) % L
                cell = src[y, x]
                cell = cell if o == 0 else pltpu.roll(cell, o, 1)
                tiles[t] = cell if o == 0 else jnp.where(lane >= o, cell, tiles[t])
                if o + C2 > L:
                    tiles[t + 1] = cell
            for t in range(TILES):
                out32[t, pl.ds(y, Z, stride=N2), :] = tiles[t]
            return 0

        lax.fori_loop(0, N2, row, 0)
        for t in range(TILES):
            dst_ref[0, :, :, t * L : (t + 1) * L] = out32[t].reshape(Z, N2, L).astype(BF)

    def fine_columns():
        def row(y, _):
            for k in range(3):
                x3[y, :, k * L : (k + 1) * L] = pad2[y, k : k + N2].reshape(N2 * Z, L).astype(BF)
            return 0

        lax.fori_loop(0, N2 + 2, row, 0)

    def fine_rows(chunk):
        parts = [x3[pl.ds(chunk * 4 + j, 4)].reshape(4 * N2 * Z, 3 * L) for j in range(3)]
        return jnp.concatenate(parts, axis=1)

    def columns(ref, n, off=0):
        rows = n * n * Z
        for j in range(3):
            for k in range(3):
                t = (j * 3 + k) * L
                q[0:rows, t : t + L] = (
                    ref[off + j : off + j + n, off + k : off + k + n].reshape(rows, L).astype(BF)
                )
        return q[0:rows, :]

    def tap_rows(ref, blocks, at=0):
        for y0, y1, x0, x1 in blocks:
            rows = (y1 - y0) * (x1 - x0) * Z
            for j in range(3):
                for k in range(3):
                    t = (j * 3 + k) * L
                    part = ref[y0 + j : y1 + j, x0 + k : x1 + k]
                    q[at : at + rows, t : t + L] = part.reshape(rows, L).astype(BF)
            at += rows
        return q[0:at, :]

    def put_rows(dst, blocks, cells):
        at = 0
        for y0, y1, x0, x1 in blocks:
            n = (y1 - y0) * (x1 - x0)
            dst[y0:y1, x0:x1] = cells[at : at + n].reshape(y1 - y0, x1 - x0, Z, L)
            at += n

    def rim(n, w):
        return [(0, w, 0, n), (n - w, n, 0, n), (w, n - w, 0, w), (w, n - w, n - w, n)]

    def joined(acc):
        acc = acc.reshape(-1, Z, 3 * L)
        return shift_z(acc[:, :, 0:L], 1) + acc[:, :, L : 2 * L] + shift_z(acc[:, :, 2 * L :], -1)

    def coarse_weight_grad(taps, g):
        g3 = jnp.concatenate([shift_z(g, -1), g, shift_z(g, 1)], axis=2)
        g3 = g3.reshape(N3 * N3 * Z, 3 * L).astype(BF)
        return tn(taps, g3).reshape(9, L, 3 * L)

    loads[0].wait()
    spread(a_ref)
    read_row(0, range(N2), pad2, 1)
    read_row(N2 - 1, range(N2), pad2, 1)
    read_rows(1, N2 - 1, (0, N2 - 1), pad2, 1)
    pl.semaphore_wait(barrier, len(met))
    copies = send_halo(EX_IN, pad2, N2, 1)

    read_rows(1, N2 - 1, range(1, N2 - 1), pad2, 1)
    for s in (0, N2 + 1):
        pad2[s] = jnp.zeros((N2 + 2, Z, L), F32)
        pad2[:, s : s + 1] = jnp.zeros((N2 + 2, 1, Z, L), F32)
    for load in loads[1:]:
        load.wait()
    wf[...] = jnp.zeros(wf.shape, BF)
    for j in range(3):
        for k in range(3):
            t = (j * 3 + k) * L
            wf[t : t + C2, 0:C2] = wf_ref[j, k]
    fine_columns()

    def fine_forward(chunk, _):
        act = rounded(elu(nn(fine_rows(chunk), wf[...])))
        fa[pl.ds(chunk * 4, 4)] = act.reshape(4, N2, Z, L)
        return 0

    lax.fori_loop(0, 4, fine_forward, 0)

    take_halo(EX_IN, pad2, N2, 1, copies)
    put_rows(fa, rim(N2, 1), rounded(elu(nn(tap_rows(pad2, rim(N2, 1)), wf[...]))).reshape(-1, Z, L))
    v = fa[...].reshape(N3, 2, N3, 2, Z, L)
    v = (v[:, 0, :, 0] + v[:, 0, :, 1]) + (v[:, 1, :, 0] + v[:, 1, :, 1])
    pad3[3 : N3 + 3, 3 : N3 + 3] = rounded(0.25 * v)
    copies = send_halo(EX_POOL, pad3, N3, 3)

    spread(u_ref)
    read_rows(0, N2, range(N2), e32, 0)
    low = e32[...].reshape(N3, 2, N3, 2, Z, L)
    low = (low[:, 0, :, 0] + low[:, 0, :, 1]) + (low[:, 1, :, 0] + low[:, 1, :, 1])
    ulp[1 : N3 + 1, 1 : N3 + 1] = rounded(low)
    low_copies = send_halo(EX_LOW, ulp, N3, 1)
    for ref in (wft, we, wet, wm, wmt, wl):
        ref[...] = jnp.zeros(ref.shape, BF)
    wl[0:C2, 0:C3] = wl_ref[...]
    for j in range(3):
        for k in range(3):
            t = (j * 3 + k) * L
            wft[0:C2, t : t + C2] = wf_ref[2 - j, 2 - k]
            for i in range(3):
                we[t : t + C2, i * L : i * L + C3] = we_ref[i, j, k]
                wm[t : t + C3, i * L : i * L + C3] = wm_ref[i, j, k]
                wet[i * L : i * L + C2, t : t + C3] = we_ref[2 - i, 2 - j, 2 - k]
                wmt[i * L : i * L + C3, t : t + C3] = wm_ref[2 - i, 2 - j, 2 - k]
    fine_columns()
    g3f[...] = jnp.zeros(g3f.shape, BF)
    inner = [(3, N3 + 1, 3, N3 + 1)]
    put_rows(c1p, inner, rounded(elu(joined(nn(tap_rows(pad3, inner), we[...])))))

    take_halo(EX_POOL, pad3, N3, 3, copies)
    outer = rim(N3 + 4, 3)
    put_rows(c1p, outer, rounded(elu(joined(nn(tap_rows(pad3, outer), we[...])))))
    for there, ys, xs in (
        (gy > 0, slice(0, 2), slice(None)),
        (gy < GY - 1, slice(N3 + 2, N3 + 4), slice(None)),
        (gx > 0, slice(None), slice(0, 2)),
        (gx < GX - 1, slice(None), slice(N3 + 2, N3 + 4)),
    ):
        c1p[ys, xs] = c1p[ys, xs] * jnp.where(there, 1.0, 0.0).astype(F32)
    two = rounded(elu(joined(nn(columns(c1p, N3 + 2), wm[...]))))
    c2[...] = two.reshape(N3 + 2, N3 + 2, Z, L)
    take_halo(EX_LOW, ulp, N3, 1, low_copies)
    back = nn(ulp[...].reshape(-1, L).astype(BF), wl[...]).reshape(-1, Z, L)
    gp[...] = rounded(back * slope(two)).reshape(N3 + 2, N3 + 2, Z, L)
    own = c1p[2 : N3 + 2, 2 : N3 + 2].reshape(-1, Z, L)
    g1 = rounded(joined(nt(columns(gp, N3), wmt[...])) * slope(own))
    gup[1 : N3 + 1, 1 : N3 + 1] = g1.reshape(N3, N3, Z, L)
    copies = send_halo(EX_G1, gup, N3, 1)

    mid = coarse_weight_grad(
        columns(c1p, N3, 1), gp[1 : N3 + 1, 1 : N3 + 1].reshape(-1, Z, L)
    )
    two = c2[1 : N3 + 1, 1 : N3 + 1].reshape(-1, L).astype(BF)
    lift_grad = tn(ulp[1 : N3 + 1, 1 : N3 + 1].reshape(-1, L).astype(BF), two)
    blocks = [mid[t, :C3, i * L : (i + 1) * L] for i in range(3) for t in range(9)]
    blocks.append(lift_grad[:C3])
    for g in range(7):
        for d, part in enumerate(pack4(blocks[4 * g : 4 * g + 4])):
            m0[(g * 3 + d) * C3 : (g * 3 + d + 1) * C3, :] = part.astype(BF)
    m0[21 * C3 :, :] = jnp.zeros((ROWS_M - 21 * C3, L), BF)
    red_m = Reduce(ring, ROWS_M, ("dp", "xy"), (m0, m1), (mr0, mr1), mslot, mout, m_send, m_recv, sent)
    red_m.scatter_start(0)
    ent = coarse_weight_grad(columns(pad3, N3, 2), gup[1 : N3 + 1, 1 : N3 + 1].reshape(-1, Z, L))
    blocks = [ent[t, :C2, i * L : (i + 1) * L] for i in range(3) for t in range(9)]
    blocks.append(jnp.zeros((C2, L), F32))
    for g in range(7):
        for d, part in enumerate(pack4(blocks[4 * g : 4 * g + 4])):
            are32[(g * 3 + d) * C2 : (g * 3 + d + 1) * C2, :] = part
    are32[21 * C2 :, :] = jnp.zeros((ROWS_E - 21 * C2, L), F32)
    e0[...] = are32[...].astype(BF)
    red_e = Reduce(ring, ROWS_E, ("dp", "xy"), (e0, e1), (er0, er1), eslot, eout, e_send, e_recv, sent)
    red_e.scatter_start(0)
    red_m.scatter_end(0)
    red_m.scatter_start(1)

    inner = [(1, N3 - 1, 1, N3 - 1)]
    low = rounded(joined(nt(tap_rows(gup, inner), wet[...])))
    put_rows(up, inner, 0.25 * low)

    def fine_back(y, _):
        act = fa[pl.ds(y * 2, 2), 2 : N2 - 2].reshape(2, N3 - 2, 2, Z, L)
        e = e32[pl.ds(y * 2, 2), 2 : N2 - 2].reshape(2, N3 - 2, 2, Z, L)
        g = e + up[pl.ds(y, 1), 1 : N3 - 1].reshape(1, N3 - 2, 1, Z, L)
        g = (g * slope(act)).reshape(2, (N2 - 4) * Z, L).astype(BF)
        for j in range(3):
            g3f[pl.ds(y * 2 + j, 2), 2 * Z : (N2 - 2) * Z, j * L : (j + 1) * L] = g
        pad2[pl.ds(y * 2 + 1, 2), 3 : N2 - 1] = g.astype(F32).reshape(2, N2 - 4, Z, L)
        return 0

    lax.fori_loop(1, N3 - 1, fine_back, 0)
    red_e.scatter_end(0)
    red_e.scatter_start(1)
    gsum[...] = tn(x3[...].reshape(-1, 3 * L), g3f[...].reshape(-1, 3 * L))
    start = at = 4 * (N3 - 1) * Z
    for y0, y1, x0, x1 in rim(N2, 2):
        rows = (y1 - y0) * (x1 - x0) * Z
        for j in range(3):
            part = x3[y0 + j : y1 + j, x0 * Z : x1 * Z, :].reshape(rows, 3 * L)
            q[at : at + rows, 3 * j * L : 3 * (j + 1) * L] = part
        at += rows

    take_halo(EX_G1, gup, N3, 1, copies)
    low = rounded(joined(nt(tap_rows(gup, rim(N3, 1)), wet[...])))
    put_rows(up, rim(N3, 1), 0.25 * low)
    rows = 0
    for y0, y1, x0, x1 in rim(N2, 2):
        ny, nx = (y1 - y0) // 2, (x1 - x0) // 2
        act = fa[y0:y1, x0:x1].reshape(ny, 2, nx, 2, Z, L)
        e = e32[y0:y1, x0:x1].reshape(ny, 2, nx, 2, Z, L)
        g = e + up[y0 // 2 : y1 // 2, x0 // 2 : x1 // 2].reshape(ny, 1, nx, 1, Z, L)
        g = (g * slope(act)).reshape(-1, L).astype(BF)
        grim[rows : rows + g.shape[0], :] = g
        rows += g.shape[0]
        pad2[y0 + 1 : y1 + 1, x0 + 1 : x1 + 1] = g.astype(F32).reshape(y1 - y0, x1 - x0, Z, L)
    copies = send_halo(EX_FINE, pad2, N2, 1)

    grad = tn(q[start:at, :], grim[...])
    for k in range(3):
        b0, b1, b2 = [
            gsum[k * L : k * L + C2, j * L : (j + 1) * L] + grad[(j * 3 + k) * L : (j * 3 + k) * L + C2]
            for j in range(3)
        ]
        lane = lanes(b0.shape)
        r1, r2 = pltpu.roll(b1, C2, 1), pltpu.roll(b2, 2 * C2 - L, 1)
        arf32[2 * k * C2 : (2 * k + 1) * C2, :] = jnp.where(lane < C2, b0, r1)
        arf32[(2 * k + 1) * C2 : (2 * k + 2) * C2, :] = jnp.where(lane < 2 * C2 - L, r1, r2)
    arf32[6 * C2 :, :] = jnp.zeros((ROWS_F - 6 * C2, L), F32)
    f0[...] = arf32[...].astype(BF)
    red_f = Reduce(ring, ROWS_F, ("dp", "xy"), (f0, f1), (fr0, fr1), fslot, fout, f_send, f_recv, sent)
    red_f.scatter_start(0)
    red_m.scatter_end(1)
    red_m.last_start()
    red_f.scatter_end(0)
    red_f.scatter_start(1)

    two = c2[1 : N3 + 1, 1 : N3 + 1].reshape(-1, L).astype(BF)
    up[...] = rounded(nt(two, wl[...])).reshape(N3, N3, Z, L)

    def mix(y, _):
        act = fa[pl.ds(y * 2, 2)].reshape(2, N3, 2, Z, L)
        lifted = up[pl.ds(y, 1)].reshape(1, N3, 1, Z, L)
        d32[pl.ds(y * 2, 2)] = (act + lifted).reshape(2, N2, Z, L)
        return 0

    lax.fori_loop(0, N3, mix, 0)

    red_e.scatter_end(1)
    red_e.last_start()
    red_m.last_end()
    red_m.gather_start(1)

    write_cells(d32, raw, mixed_ref)
    store(mixed_ref, mixed_hbm)

    red_f.scatter_end(1)
    red_f.last_start()
    red_e.last_end()
    red_e.gather_start(1)

    take_halo(EX_FINE, pad2, N2, 1, copies)
    fine_columns()

    def fine_backward(chunk, _):
        d32[pl.ds(chunk * 4, 4)] = nt(fine_rows(chunk), wft[...]).reshape(4, N2, Z, L)
        return 0

    lax.fori_loop(0, 4, fine_backward, 0)

    red_f.last_end()
    red_f.gather_start(1)

    write_cells(d32, raw2, ig_ref)
    store(ig_ref, ig_hbm)

    red_m.gather_end()
    red_m.gather_start(0)
    red_e.gather_end()
    red_e.gather_start(0)
    red_f.gather_end()
    red_f.gather_start(0)
    red_m.gather_end()
    for g in range(7):
        d = [mout[(g * 3 + s) * C3 : (g * 3 + s + 1) * C3, :].astype(F32) for s in range(3)]
        for s, b in enumerate(unpack4(d)):
            mflat[(g * 4 + s) * C3 : (g * 4 + s + 1) * C3, :] = b.astype(BF)
    store(mflat, m_hbm)
    red_e.gather_end()
    are32[...] = eout[...].astype(F32)
    for g in range(7):
        d = [are32[(g * 3 + s) * C2 : (g * 3 + s + 1) * C2, :] for s in range(3)]
        for s, b in enumerate(unpack4(d)):
            eflat[(g * 4 + s) * PITCH : (g * 4 + s) * PITCH + C2, :] = b.astype(BF)
    store(eflat, e_hbm)
    red_f.gather_end()
    store(fout, f_hbm)
    for c in sent:
        c.wait_send()
    for done in stores:
        done.wait()


def finish(
    mixed_in, ig_in, m_hbm, e_hbm, f_hbm, mixed, ig, gf_hbm, ge_hbm, gm_hbm, gl_hbm,
    mixed_ref, ig_ref, mflat, eflat, fout, gf, ge, gm, gl, arf32, in_sem, out_sem,
):
    loads = [
        pltpu.make_async_copy(src, dst, in_sem.at[i])
        for i, (src, dst) in enumerate(
            ((m_hbm, mflat), (e_hbm, eflat), (f_hbm, fout), (mixed_in, mixed_ref), (ig_in, ig_ref))
        )
    ]
    stores = [
        pltpu.make_async_copy(src, dst, out_sem.at[i])
        for i, (src, dst) in enumerate(
            ((mixed_ref, mixed), (ig_ref, ig), (gm, gm_hbm), (gl, gl_hbm), (ge, ge_hbm), (gf, gf_hbm))
        )
    ]
    for load in loads:
        load.start()

    loads[0].wait()
    for t in range(28):
        b = mflat[t * C3 : (t + 1) * C3, :].astype(F32)
        if t < 27:
            gm[t // 9, (t // 3) % 3, t % 3] = b[:, 0:C3]
        else:
            gl[...] = b[0:C2, 0:C3]
    stores[2].start()
    stores[3].start()
    for i in (3, 4):
        loads[i].wait()
        stores[i - 3].start()

    loads[1].wait()
    for t in range(27):
        b = eflat[t * PITCH : t * PITCH + C2, :].astype(F32)
        ge[t // 9, (t // 3) % 3, t % 3] = b[:, 0:C3]
    stores[4].start()

    loads[2].wait()
    arf32[...] = fout[...].astype(F32)
    for k in range(3):
        d0 = arf32[2 * k * C2 : (2 * k + 1) * C2, :]
        d1 = arf32[(2 * k + 1) * C2 : (2 * k + 2) * C2, :]
        lane = lanes(d0.shape)
        b1 = pltpu.roll(jnp.where(lane >= C2, d0, d1), L - C2, 1)
        b2 = pltpu.roll(d1, 2 * L - 2 * C2, 1)
        for j, b in enumerate((d0, b1, b2)):
            gf[j, k] = b[:, 0:C2]
    stores[5].start()
    for done in stores:
        done.wait()


def body(fine_input, fine_weight, entry_weight, middle_weight, lift_weight, upstream):
    args = (fine_input, fine_weight, entry_weight, middle_weight, lift_weight.T, upstream)
    field = jax.ShapeDtypeStruct(fine_input.shape, BF)
    whole = pl.BlockSpec(memory_space=pl.ANY)
    cells3 = (N3 + 4) * (N3 + 4) * Z
    flat = [(28 * C3, L), (28 * PITCH, L), (ROWS_F, L)]

    def v(*shape):
        return pltpu.VMEM(shape, BF)

    def w(*shape):
        return pltpu.VMEM(shape, F32)

    def sems(n):
        return [pltpu.SemaphoreType.DMA((n,)), pltpu.SemaphoreType.DMA((n,))]

    def sums(rows, *sizes):
        left, sent, got = rows, [], []
        for size in sizes:
            sent.append(v(left, L))
            left //= size
            got.append(v(size - 1, left, L))
        return [*sent, *got, v(4, left, L), *sems(3 + 2 * sum(size - 1 for size in sizes))]

    scratch = [
        *[v(*arg.shape) for arg in args], v(*field.shape), v(*field.shape),
        *[v(rows, L) for rows in ROWS], v(*flat[0]), v(*flat[1]), *sems(6),
        w(TILES, Z * N2, L), w(TILES, Z * N2, L), w(N2 + 2, N2 + 2, Z, L), w(N3 + 6, N3 + 6, Z, L),
        w(N3 + 2, N3 + 2, Z, L), w(N2, N2, Z, L),
        v(N2 + 2, N2 * Z, 3 * L), v(N2 + 2, N2 * Z, 3 * L), w(N2, N2, Z, L),
        v(cells3, 9 * L), w(N3 + 4, N3 + 4, Z, L), w(N3 + 2, N3 + 2, Z, L), w(N3 + 2, N3 + 2, Z, L),
        w(N3 + 2, N3 + 2, Z, L), w(N3, N3, Z, L), w(3 * L, 3 * L), v(8 * (N2 - 2) * Z, L), w(N2, N2, Z, L),
        v(9 * L, L), v(L, 9 * L), v(9 * L, 3 * L), v(3 * L, 9 * L), v(9 * L, 3 * L), v(3 * L, 9 * L), v(L, L),
        w(ROWS_E, L), w(ROWS_F, L),
        v(5, 8, 3 * N3 * Z, L), v(5, 8, 3 * N3 * Z, L), *sems(40),
        *sums(ROWS_M, 2, 16), *sums(ROWS_E, 2, 16), *sums(ROWS_F, 2, 16),
    ]
    packed = [jax.ShapeDtypeStruct(size, BF) for size in flat]
    fields_and_sums = pl.pallas_call(
        kernel,
        out_shape=(field, field, *packed),
        in_specs=[whole] * 6,
        out_specs=[whole] * 5,
        scratch_shapes=scratch,
        compiler_params=pltpu.CompilerParams(
            collective_id=0, has_side_effects=True, vmem_limit_bytes=60 * 1024 * 1024
        ),
    )(*args)
    mixed, input_grad, fine, entry, middle, lift = pl.pallas_call(
        finish,
        out_shape=(
            field,
            field,
            jax.ShapeDtypeStruct(fine_weight.shape, F32),
            jax.ShapeDtypeStruct(entry_weight.shape, F32),
            jax.ShapeDtypeStruct(middle_weight.shape, F32),
            jax.ShapeDtypeStruct(lift_weight.shape[::-1], F32),
        ),
        in_specs=[whole] * 5,
        out_specs=[whole] * 6,
        scratch_shapes=[
            v(*field.shape), v(*field.shape), *[v(*size) for size in flat],
            w(*fine_weight.shape), w(*entry_weight.shape), w(*middle_weight.shape), w(*lift_weight.shape[::-1]),
            w(ROWS_F, L), *sems(6),
        ],
        compiler_params=pltpu.CompilerParams(vmem_limit_bytes=60 * 1024 * 1024),
    )(*fields_and_sums)
    return mixed, input_grad, fine, entry, middle, lift.T


def solution(mesh):
    assert mesh.shape["gy"] == GY and mesh.shape["gx"] == GX
    return jax.shard_map(
        body,
        mesh=mesh,
        in_specs=(P("dp", None, "gy", "gx"), P(), P(), P(), P(), P("dp", None, "gy", "gx")),
        out_specs=(P("dp", None, "gy", "gx"), P("dp", None, "gy", "gx"), P(), P(), P(), P()),
        check_vma=False,
    )
```

```python
import jax
import jax.numpy as jnp
from jax import lax
from jax.experimental import pallas as pl
from jax.experimental.pallas import tpu as pltpu
from jax.sharding import PartitionSpec as P

MESH = pl.DeviceIdType.MESH
BF = jnp.bfloat16
F32 = jnp.float32

Z = 8
N2 = 16
N3 = 8
C2 = 72
C3 = 96
L = 128
GY = 8
GX = 8
MERGED = N2 * C2
TILES = MERGED // L
DIRS = [(-1, -1), (-1, 1), (1, -1), (1, 1), (-1, 0), (1, 0), (0, -1), (0, 1)]

EX_IN, EX_POOL, EX_LOW, EX_G1, EX_FINE = range(5)

ROWS_M = 2048
ROWS_E = 1536
ROWS_F = 512
ROWS = (ROWS_M, ROWS_E, ROWS_F)
GROUPS = ("dp", "xy")
PITCH = 80


def lanes(shape):
    return lax.broadcasted_iota(jnp.int32, shape, len(shape) - 1)


def elu(v):
    return jnp.where(v > 0, v, jnp.exp(jnp.minimum(v, 0.0)) - 1.0)


def slope(s):
    return jnp.where(s > 0, 1.0, 1.0 + s)


def rounded(v):
    return v.astype(BF).astype(F32)


def shift_z(v, step):
    moved = pltpu.roll(v, step % Z, 1)
    row = lax.broadcasted_iota(jnp.int32, v.shape, 1)
    return jnp.where(row == (0 if step == 1 else Z - 1), 0.0, moved)


def nt(a, b):
    return lax.dot_general(a, b, (((1,), (1,)), ((), ())), preferred_element_type=F32)


def tn(a, b):
    return lax.dot_general(a, b, (((0,), (0,)), ((), ())), preferred_element_type=F32)


def nn(a, b):
    return jnp.dot(a, b, preferred_element_type=F32)


class Ring:
    def __init__(self):
        self.dp = lax.axis_index("dp")
        self.gy = lax.axis_index("gy")
        self.gx = lax.axis_index("gx")

    def place(self):
        return {"x": self.gy // 2, "y": self.gx // 2, "z": (self.gy % 2) * 2 + self.gx % 2}

    def member(self, kind):
        if kind == "dp":
            return self.dp
        place, m = self.place(), 0
        for axis in kind:
            m = m * 4 + place[axis]
        return m

    def device(self, kind, p):
        if kind == "dp":
            return (p, self.gy, self.gx)
        place = self.place()
        for axis in reversed(kind):
            place[axis] = p % 4
            p = p // 4
        return (self.dp, place["x"] * 2 + place["z"] // 2, place["y"] * 2 + place["z"] % 2)

    def others(self, kind):
        m = self.member(kind)
        if kind == "dp":
            return [1 - m]
        if len(kind) == 1:
            return [(m + r) % 4 for r in (2, 1, 3)]
        steps = [(2, 2), (2, 1), (1, 2), (2, 3), (3, 2), (1, 1), (1, 3), (3, 1), (3, 3)]
        steps += [(2, 0), (0, 2), (1, 0), (0, 1), (3, 0), (0, 3)]
        return [((m // 4 + x) % 4) * 4 + (m % 4 + y) % 4 for x, y in steps]


SIZE = {"dp": 2, "x": 4, "y": 4, "z": 4, "xy": 16, "xz": 16, "yz": 16}


class Reduce:
    def __init__(self, ring, rows, plan, back, bufs, recvs, slots, out, send, recv, sent):
        self.ring = ring
        self.scatter, self.last = plan[:-1], plan[-1]
        self.back = list(back)
        self.bufs = bufs
        self.recvs = recvs
        self.slots = slots
        self.out = out
        self.send = send
        self.recv = recv
        self.sent = sent
        self.used = 0
        self.rows = [rows]
        self.offs = [0]
        for kind in self.scatter:
            n = self.rows[-1] // SIZE[kind]
            self.offs.append(self.offs[-1] + ring.member(kind) * n)
            self.rows.append(n)
        self.held = self.offs[-1], n

    def _go(self, src, dst, device):
        i = self.used
        self.used += 1
        c = pltpu.make_async_remote_copy(
            src_ref=src,
            dst_ref=dst,
            send_sem=self.send.at[i],
            recv_sem=self.recv.at[i],
            device_id=device,
            device_id_type=MESH,
        )
        c.start()
        self.sent.append(c)
        return c

    def scatter_start(self, s):
        kind, n = self.scatter[s], self.rows[s + 1]
        self.now = []
        for r, p in enumerate(self.ring.others(kind)):
            src = self.bufs[s].at[pl.ds(pl.multiple_of(p * n, 16), n)]
            self.now.append(self._go(src, self.recvs[s].at[r], self.ring.device(kind, p)))

    def scatter_end(self, s):
        kind, n = self.scatter[s], self.rows[s + 1]
        m, size = self.ring.member(kind), SIZE[kind]
        for c in self.now:
            c.wait_recv()
        total = self.bufs[s][pl.ds(pl.multiple_of(m * n, 16), n), :].astype(F32)
        for r in range(size - 1):
            total = total + self.recvs[s][r].astype(F32)
        total = total.astype(BF)
        if s + 1 < len(self.scatter):
            self.bufs[s + 1][...] = total
        else:
            self.slots[self.ring.member(self.last)] = total

    def last_start(self):
        m = self.ring.member(self.last)
        self.now = []
        for p in self.ring.others(self.last):
            self.now.append(self._go(self.slots.at[m], self.slots.at[m], self.ring.device(self.last, p)))

    def last_end(self):
        for c in self.now:
            c.wait_recv()
        total = self.slots[0].astype(F32)
        for r in range(1, SIZE[self.last]):
            total = total + self.slots[r].astype(F32)
        self.out[pl.ds(pl.multiple_of(self.offs[-1], 16), self.rows[-1]), :] = total.astype(BF)

    def gather_start(self):
        kind, (off, n) = self.back.pop(0), self.held
        part = self.out.at[pl.ds(pl.multiple_of(off, 16), n)]
        self.now = []
        for p in self.ring.others(kind):
            self.now.append(self._go(part, part, self.ring.device(kind, p)))
        self.held = off - self.ring.member(kind) * n, n * SIZE[kind]

    def gather_end(self):
        for c in self.now:
            c.wait_recv()


def pack4(b):
    lane = lanes(b[0].shape)
    r1, r2, r3 = pltpu.roll(b[1], 96, 1), pltpu.roll(b[2], 64, 1), pltpu.roll(b[3], 32, 1)
    return (
        jnp.where(lane >= 96, r1, b[0]),
        jnp.where(lane < 64, r1, r2),
        jnp.where(lane < 32, r2, r3),
    )


def unpack4(d):
    lane = lanes(d[0].shape)
    return (
        d[0],
        pltpu.roll(jnp.where(lane >= 96, d[0], d[1]), 32, 1),
        pltpu.roll(jnp.where(lane >= 64, d[1], d[2]), 64, 1),
        pltpu.roll(d[2], 96, 1),
    )


def kernel(
    a_hbm, wf_hbm, we_hbm, wm_hbm, wl_hbm, u_hbm,
    mixed_hbm, ig_hbm, m_hbm, e_hbm, f_hbm,
    a_ref, wf_ref, we_ref, wm_ref, wl_ref, u_ref, mixed_ref, ig_ref, mout, eout, fout, mflat, eflat, in_sem, out_sem,
    raw, raw2, pad2, pad3, ulp, e32, x3, g3f, fa, q, c1p, c2, gp, gup, up, gsum, grim, d32,
    wf, wft, we, wet, wm, wmt, wl, are32, arf32,
    sbuf, rbuf, h_send, h_recv,
    m0, m1, mr0, mr1, mslot, m_send, m_recv,
    e0, e1, er0, er1, eslot, e_send, e_recv,
    f0, f1, fr0, fr1, fslot, f_send, f_recv,
):
    ring = Ring()
    dp, gy, gx = ring.dp, ring.gy, ring.gx

    barrier = pltpu.get_barrier_semaphore()
    met = [(dp, (gy + dy + GY) % GY, (gx + dx + GX) % GX) for dy, dx in DIRS]
    met += [ring.device(kind, p) for kind in GROUPS for p in ring.others(kind)]
    for device in met:
        pl.semaphore_signal(barrier, inc=1, device_id=device, device_id_type=MESH)

    loads = [
        pltpu.make_async_copy(src, dst, in_sem.at[i])
        for i, (src, dst) in enumerate(
            (
                (a_hbm, a_ref), (u_hbm, u_ref), (wf_hbm, wf_ref),
                (we_hbm, we_ref), (wm_hbm, wm_ref), (wl_hbm, wl_ref),
            )
        )
    ]
    for load in loads:
        load.start()

    sent = []
    stores = []

    def store(src, dst):
        stores.append(pltpu.make_async_copy(src, dst, out_sem.at[len(stores)]))
        stores[-1].start()

    def edge(step, n, w):
        return {1: slice(n, n + w), -1: slice(w, 2 * w), 0: slice(w, n + w)}[step]

    def outside(step, n, w):
        return {1: slice(0, w), -1: slice(n + w, n + 2 * w), 0: slice(w, n + w)}[step]

    def send_halo(ex, ref, n, w):
        copies = []
        for d, (dy, dx) in enumerate(DIRS):
            part = ref[edge(dy, n, w), edge(dx, n, w)].reshape(-1, L)
            if part.shape[0] % 16:
                part = jnp.concatenate([part, part[:Z]], axis=0)
            rows = part.shape[0]
            sbuf[ex, d, 0:rows, :] = part.astype(BF)
            c = pltpu.make_async_remote_copy(
                src_ref=sbuf.at[ex, d, pl.ds(0, rows)],
                dst_ref=rbuf.at[ex, d, pl.ds(0, rows)],
                send_sem=h_send.at[ex * 8 + d],
                recv_sem=h_recv.at[ex * 8 + d],
                device_id=(dp, (gy + dy + GY) % GY, (gx + dx + GX) % GX),
                device_id_type=MESH,
            )
            c.start()
            sent.append(c)
            copies.append(c)
        return copies

    def take_halo(ex, ref, n, w, copies):
        for d, (dy, dx) in enumerate(DIRS):
            copies[d].wait_recv()
            there = jnp.logical_and(
                jnp.logical_and(gy - dy >= 0, gy - dy < GY),
                jnp.logical_and(gx - dx >= 0, gx - dx < GX),
            )
            keep = jnp.where(there, 1.0, 0.0).astype(F32)
            ys, xs = outside(dy, n, w), outside(dx, n, w)
            ny, nx = ys.stop - ys.start, xs.stop - xs.start
            part = rbuf[ex, d, 0 : max(ny * nx * Z, 16), :].astype(F32)[: ny * nx * Z]
            ref[ys, xs] = (part * keep).reshape(ny, nx, Z, L)

    def spread(src_ref):
        for t in range(TILES):
            raw[t] = src_ref[0, :, :, t * L : (t + 1) * L].astype(F32).reshape(Z * N2, L)

    def read_row(y, xs, dst, shift):
        lane = lanes((Z, L))
        tiles = {}
        for x in xs:
            t, o = (x * C2) // L, (x * C2) % L
            for s in (t, t + 1) if o + C2 > L else (t,):
                if s not in tiles:
                    tiles[s] = raw[s, pl.ds(y, Z, stride=N2), :]
            cell = tiles[t] if o == 0 else pltpu.roll(tiles[t], L - o, 1)
            if o + C2 > L:
                cell = jnp.where(lane < L - o, cell, pltpu.roll(tiles[t + 1], L - o, 1))
            dst[y + shift, x + shift] = jnp.where(lane < C2, cell, 0.0)

    def read_rows(first, last, xs, dst, shift):
        def row(y, _):
            read_row(y, xs, dst, shift)
            return 0

        lax.fori_loop(first, last, row, 0)

    def write_cells(src, out32, dst_ref):
        def row(y, _):
            tiles = [None] * TILES
            lane = lanes((Z, L))
            for x in range(N2):
                t, o = (x * C2) // L, (x * C2) % L
                cell = src[y, x]
                cell = cell if o == 0 else pltpu.roll(cell, o, 1)
                tiles[t] = cell if o == 0 else jnp.where(lane >= o, cell, tiles[t])
                if o + C2 > L:
                    tiles[t + 1] = cell
            for t in range(TILES):
                out32[t, pl.ds(y, Z, stride=N2), :] = tiles[t]
            return 0

        lax.fori_loop(0, N2, row, 0)
        for t in range(TILES):
            dst_ref[0, :, :, t * L : (t + 1) * L] = out32[t].reshape(Z, N2, L).astype(BF)

    def fine_columns():
        def row(y, _):
            for k in range(3):
                x3[y, :, k * L : (k + 1) * L] = pad2[y, k : k + N2].reshape(N2 * Z, L).astype(BF)
            return 0

        lax.fori_loop(0, N2 + 2, row, 0)

    def fine_rows(chunk):
        parts = [x3[pl.ds(chunk * 4 + j, 4)].reshape(4 * N2 * Z, 3 * L) for j in range(3)]
        return jnp.concatenate(parts, axis=1)

    def columns(ref, n, off=0):
        rows = n * n * Z
        for j in range(3):
            for k in range(3):
                t = (j * 3 + k) * L
                q[0:rows, t : t + L] = (
                    ref[off + j : off + j + n, off + k : off + k + n].reshape(rows, L).astype(BF)
                )
        return q[0:rows, :]

    def tap_rows(ref, blocks, at=0):
        for y0, y1, x0, x1 in blocks:
            rows = (y1 - y0) * (x1 - x0) * Z
            for j in range(3):
                for k in range(3):
                    t = (j * 3 + k) * L
                    part = ref[y0 + j : y1 + j, x0 + k : x1 + k]
                    q[at : at + rows, t : t + L] = part.reshape(rows, L).astype(BF)
            at += rows
        return q[0:at, :]

    def put_rows(dst, blocks, cells):
        at = 0
        for y0, y1, x0, x1 in blocks:
            n = (y1 - y0) * (x1 - x0)
            dst[y0:y1, x0:x1] = cells[at : at + n].reshape(y1 - y0, x1 - x0, Z, L)
            at += n

    def rim(n, w):
        return [(0, w, 0, n), (n - w, n, 0, n), (w, n - w, 0, w), (w, n - w, n - w, n)]

    def joined(acc):
        acc = acc.reshape(-1, Z, 3 * L)
        return shift_z(acc[:, :, 0:L], 1) + acc[:, :, L : 2 * L] + shift_z(acc[:, :, 2 * L :], -1)

    def coarse_weight_grad(taps, g):
        g3 = jnp.concatenate([shift_z(g, -1), g, shift_z(g, 1)], axis=2)
        g3 = g3.reshape(N3 * N3 * Z, 3 * L).astype(BF)
        return tn(taps, g3).reshape(9, L, 3 * L)

    loads[0].wait()
    spread(a_ref)
    read_row(0, range(N2), pad2, 1)
    read_row(N2 - 1, range(N2), pad2, 1)
    read_rows(1, N2 - 1, (0, N2 - 1), pad2, 1)
    pl.semaphore_wait(barrier, len(met))
    copies = send_halo(EX_IN, pad2, N2, 1)

    read_rows(1, N2 - 1, range(1, N2 - 1), pad2, 1)
    for s in (0, N2 + 1):
        pad2[s] = jnp.zeros((N2 + 2, Z, L), F32)
        pad2[:, s : s + 1] = jnp.zeros((N2 + 2, 1, Z, L), F32)
    for load in loads[1:]:
        load.wait()
    wf[...] = jnp.zeros(wf.shape, BF)
    for j in range(3):
        for k in range(3):
            t = (j * 3 + k) * L
            wf[t : t + C2, 0:C2] = wf_ref[j, k]
    fine_columns()

    def fine_forward(chunk, _):
        act = rounded(elu(nn(fine_rows(chunk), wf[...])))
        fa[pl.ds(chunk * 4, 4)] = act.reshape(4, N2, Z, L)
        return 0

    lax.fori_loop(0, 4, fine_forward, 0)

    take_halo(EX_IN, pad2, N2, 1, copies)
    put_rows(fa, rim(N2, 1), rounded(elu(nn(tap_rows(pad2, rim(N2, 1)), wf[...]))).reshape(-1, Z, L))
    v = fa[...].reshape(N3, 2, N3, 2, Z, L)
    v = (v[:, 0, :, 0] + v[:, 0, :, 1]) + (v[:, 1, :, 0] + v[:, 1, :, 1])
    pad3[3 : N3 + 3, 3 : N3 + 3] = rounded(0.25 * v)
    copies = send_halo(EX_POOL, pad3, N3, 3)

    spread(u_ref)
    read_rows(0, N2, range(N2), e32, 0)
    low = e32[...].reshape(N3, 2, N3, 2, Z, L)
    low = (low[:, 0, :, 0] + low[:, 0, :, 1]) + (low[:, 1, :, 0] + low[:, 1, :, 1])
    ulp[1 : N3 + 1, 1 : N3 + 1] = rounded(low)
    low_copies = send_halo(EX_LOW, ulp, N3, 1)
    for ref in (wft, we, wet, wm, wmt, wl):
        ref[...] = jnp.zeros(ref.shape, BF)
    wl[0:C2, 0:C3] = wl_ref[...]
    for j in range(3):
        for k in range(3):
            t = (j * 3 + k) * L
            wft[0:C2, t : t + C2] = wf_ref[2 - j, 2 - k]
            for i in range(3):
                we[t : t + C2, i * L : i * L + C3] = we_ref[i, j, k]
                wm[t : t + C3, i * L : i * L + C3] = wm_ref[i, j, k]
                wet[i * L : i * L + C2, t : t + C3] = we_ref[2 - i, 2 - j, 2 - k]
                wmt[i * L : i * L + C3, t : t + C3] = wm_ref[2 - i, 2 - j, 2 - k]
    fine_columns()
    g3f[...] = jnp.zeros(g3f.shape, BF)
    inner = [(3, N3 + 1, 3, N3 + 1)]
    put_rows(c1p, inner, rounded(elu(joined(nn(tap_rows(pad3, inner), we[...])))))

    take_halo(EX_POOL, pad3, N3, 3, copies)
    outer = rim(N3 + 4, 3)
    put_rows(c1p, outer, rounded(elu(joined(nn(tap_rows(pad3, outer), we[...])))))
    for there, ys, xs in (
        (gy > 0, slice(0, 2), slice(None)),
        (gy < GY - 1, slice(N3 + 2, N3 + 4), slice(None)),
        (gx > 0, slice(None), slice(0, 2)),
        (gx < GX - 1, slice(None), slice(N3 + 2, N3 + 4)),
    ):
        c1p[ys, xs] = c1p[ys, xs] * jnp.where(there, 1.0, 0.0).astype(F32)
    two = rounded(elu(joined(nn(columns(c1p, N3 + 2), wm[...]))))
    c2[...] = two.reshape(N3 + 2, N3 + 2, Z, L)
    take_halo(EX_LOW, ulp, N3, 1, low_copies)
    back = nn(ulp[...].reshape(-1, L).astype(BF), wl[...]).reshape(-1, Z, L)
    gp[...] = rounded(back * slope(two)).reshape(N3 + 2, N3 + 2, Z, L)

    def grad_one(blocks):
        acc = joined(nt(tap_rows(gp, blocks), wmt[...]))
        at = 0
        for y0, y1, x0, x1 in blocks:
            n = (y1 - y0) * (x1 - x0)
            one = c1p[2 + y0 : 2 + y1, 2 + x0 : 2 + x1].reshape(n, Z, L)
            g1 = rounded(acc[at : at + n] * slope(one))
            gup[1 + y0 : 1 + y1, 1 + x0 : 1 + x1] = g1.reshape(y1 - y0, x1 - x0, Z, L)
            at += n

    inner = [(1, N3 - 1, 1, N3 - 1)]
    grad_one(rim(N3, 1))
    copies = send_halo(EX_G1, gup, N3, 1)

    mid = coarse_weight_grad(
        columns(c1p, N3, 1), gp[1 : N3 + 1, 1 : N3 + 1].reshape(-1, Z, L)
    )
    two = c2[1 : N3 + 1, 1 : N3 + 1].reshape(-1, L).astype(BF)
    lift_grad = tn(ulp[1 : N3 + 1, 1 : N3 + 1].reshape(-1, L).astype(BF), two)
    blocks = [mid[t, :C3, i * L : (i + 1) * L] for i in range(3) for t in range(9)]
    blocks.append(lift_grad[:C3])
    for g in range(7):
        for d, part in enumerate(pack4(blocks[4 * g : 4 * g + 4])):
            m0[(g * 3 + d) * C3 : (g * 3 + d + 1) * C3, :] = part.astype(BF)
    m0[21 * C3 :, :] = jnp.zeros((ROWS_M - 21 * C3, L), BF)
    red_m = Reduce(ring, ROWS_M, ("dp", "xy", "z"), ("xy", "dp"), (m0, m1), (mr0, mr1), mslot, mout, m_send, m_recv, sent)
    red_m.scatter_start(0)
    grad_one(inner)
    ent = coarse_weight_grad(columns(pad3, N3, 2), gup[1 : N3 + 1, 1 : N3 + 1].reshape(-1, Z, L))
    blocks = [ent[t, :C2, i * L : (i + 1) * L] for i in range(3) for t in range(9)]
    blocks.append(jnp.zeros((C2, L), F32))
    for g in range(7):
        for d, part in enumerate(pack4(blocks[4 * g : 4 * g + 4])):
            are32[(g * 3 + d) * C2 : (g * 3 + d + 1) * C2, :] = part
    are32[21 * C2 :, :] = jnp.zeros((ROWS_E - 21 * C2, L), F32)
    e0[...] = are32[...].astype(BF)
    red_e = Reduce(ring, ROWS_E, ("dp", "xy", "z"), ("xy", "dp"), (e0, e1), (er0, er1), eslot, eout, e_send, e_recv, sent)
    red_e.scatter_start(0)
    red_m.scatter_end(0)
    red_m.scatter_start(1)

    low = rounded(joined(nt(tap_rows(gup, inner), wet[...])))
    put_rows(up, inner, 0.25 * low)

    red_e.scatter_end(0)
    red_e.scatter_start(1)

    def fine_back(y, _):
        act = fa[pl.ds(y * 2, 2), 2 : N2 - 2].reshape(2, N3 - 2, 2, Z, L)
        e = e32[pl.ds(y * 2, 2), 2 : N2 - 2].reshape(2, N3 - 2, 2, Z, L)
        g = e + up[pl.ds(y, 1), 1 : N3 - 1].reshape(1, N3 - 2, 1, Z, L)
        g = (g * slope(act)).reshape(2, (N2 - 4) * Z, L).astype(BF)
        for j in range(3):
            g3f[pl.ds(y * 2 + j, 2), 2 * Z : (N2 - 2) * Z, j * L : (j + 1) * L] = g
        pad2[pl.ds(y * 2 + 1, 2), 3 : N2 - 1] = g.astype(F32).reshape(2, N2 - 4, Z, L)
        return 0

    lax.fori_loop(1, N3 - 1, fine_back, 0)
    gsum[...] = tn(x3[...].reshape(-1, 3 * L), g3f[...].reshape(-1, 3 * L))
    start = at = 4 * (N3 - 1) * Z
    for y0, y1, x0, x1 in rim(N2, 2):
        rows = (y1 - y0) * (x1 - x0) * Z
        for j in range(3):
            part = x3[y0 + j : y1 + j, x0 * Z : x1 * Z, :].reshape(rows, 3 * L)
            q[at : at + rows, 3 * j * L : 3 * (j + 1) * L] = part
        at += rows

    take_halo(EX_G1, gup, N3, 1, copies)
    low = rounded(joined(nt(tap_rows(gup, rim(N3, 1)), wet[...])))
    put_rows(up, rim(N3, 1), 0.25 * low)
    rows = 0
    for y0, y1, x0, x1 in rim(N2, 2):
        ny, nx = (y1 - y0) // 2, (x1 - x0) // 2
        act = fa[y0:y1, x0:x1].reshape(ny, 2, nx, 2, Z, L)
        e = e32[y0:y1, x0:x1].reshape(ny, 2, nx, 2, Z, L)
        g = e + up[y0 // 2 : y1 // 2, x0 // 2 : x1 // 2].reshape(ny, 1, nx, 1, Z, L)
        g = (g * slope(act)).reshape(-1, L).astype(BF)
        grim[rows : rows + g.shape[0], :] = g
        rows += g.shape[0]
        pad2[y0 + 1 : y1 + 1, x0 + 1 : x1 + 1] = g.astype(F32).reshape(y1 - y0, x1 - x0, Z, L)

    grad = tn(q[start:at, :], grim[...])
    for k in range(3):
        b0, b1, b2 = [
            gsum[k * L : k * L + C2, j * L : (j + 1) * L] + grad[(j * 3 + k) * L : (j * 3 + k) * L + C2]
            for j in range(3)
        ]
        lane = lanes(b0.shape)
        r1, r2 = pltpu.roll(b1, C2, 1), pltpu.roll(b2, 2 * C2 - L, 1)
        arf32[2 * k * C2 : (2 * k + 1) * C2, :] = jnp.where(lane < C2, b0, r1)
        arf32[(2 * k + 1) * C2 : (2 * k + 2) * C2, :] = jnp.where(lane < 2 * C2 - L, r1, r2)
    arf32[6 * C2 :, :] = jnp.zeros((ROWS_F - 6 * C2, L), F32)
    f0[...] = arf32[...].astype(BF)
    red_f = Reduce(ring, ROWS_F, ("dp", "xy", "z"), ("xy", "dp"), (f0, f1), (fr0, fr1), fslot, fout, f_send, f_recv, sent)
    red_f.scatter_start(0)
    copies = send_halo(EX_FINE, pad2, N2, 1)
    red_f.scatter_end(0)
    red_f.scatter_start(1)
    red_m.scatter_end(1)
    red_m.last_start()

    two = c2[1 : N3 + 1, 1 : N3 + 1].reshape(-1, L).astype(BF)
    up[...] = rounded(nt(two, wl[...])).reshape(N3, N3, Z, L)

    def mix(y, _):
        act = fa[pl.ds(y * 2, 2)].reshape(2, N3, 2, Z, L)
        lifted = up[pl.ds(y, 1)].reshape(1, N3, 1, Z, L)
        d32[pl.ds(y * 2, 2)] = (act + lifted).reshape(2, N2, Z, L)
        return 0

    lax.fori_loop(0, N3, mix, 0)

    red_e.scatter_end(1)
    red_e.last_start()
    write_cells(d32, raw, mixed_ref)
    red_m.last_end()
    red_m.gather_start()
    store(mixed_ref, mixed_hbm)

    red_f.scatter_end(1)
    red_f.last_start()
    red_e.last_end()
    red_e.gather_start()

    take_halo(EX_FINE, pad2, N2, 1, copies)
    fine_columns()

    def fine_backward(chunk, _):
        d32[pl.ds(chunk * 4, 4)] = nt(fine_rows(chunk), wft[...]).reshape(4, N2, Z, L)
        return 0

    lax.fori_loop(0, 4, fine_backward, 0)

    red_f.last_end()
    red_f.gather_start()

    write_cells(d32, raw2, ig_ref)
    store(ig_ref, ig_hbm)
    for c in sent[:-45]:
        c.wait_send()
    del sent[:-45]

    red_m.gather_end()
    red_m.gather_start()
    red_e.gather_end()
    red_e.gather_start()
    red_f.gather_end()
    red_f.gather_start()
    red_m.gather_end()
    for g in range(7):
        d = [mout[(g * 3 + s) * C3 : (g * 3 + s + 1) * C3, :].astype(F32) for s in range(3)]
        for s, b in enumerate(unpack4(d)):
            mflat[(g * 4 + s) * C3 : (g * 4 + s + 1) * C3, :] = b.astype(BF)
    store(mflat, m_hbm)
    red_e.gather_end()
    are32[...] = eout[...].astype(F32)
    for g in range(7):
        d = [are32[(g * 3 + s) * C2 : (g * 3 + s + 1) * C2, :] for s in range(3)]
        for s, b in enumerate(unpack4(d)):
            eflat[(g * 4 + s) * PITCH : (g * 4 + s) * PITCH + C2, :] = b.astype(BF)
    store(eflat, e_hbm)
    red_f.gather_end()
    store(fout, f_hbm)
    for c in sent:
        c.wait_send()
    for done in stores:
        done.wait()


def finish(
    mixed_in, ig_in, m_hbm, e_hbm, f_hbm, mixed, ig, gf_hbm, ge_hbm, gm_hbm, gl_hbm,
    mixed_ref, ig_ref, mflat, eflat, fout, gf, ge, gm, gl, arf32, in_sem, out_sem,
):
    loads = [
        pltpu.make_async_copy(src, dst, in_sem.at[i])
        for i, (src, dst) in enumerate(
            ((m_hbm, mflat), (e_hbm, eflat), (f_hbm, fout), (mixed_in, mixed_ref), (ig_in, ig_ref))
        )
    ]
    stores = [
        pltpu.make_async_copy(src, dst, out_sem.at[i])
        for i, (src, dst) in enumerate(
            ((mixed_ref, mixed), (ig_ref, ig), (gm, gm_hbm), (gl, gl_hbm), (ge, ge_hbm), (gf, gf_hbm))
        )
    ]
    for load in loads:
        load.start()

    loads[0].wait()
    for t in range(28):
        b = mflat[t * C3 : (t + 1) * C3, :].astype(F32)
        if t < 27:
            gm[t // 9, (t // 3) % 3, t % 3] = b[:, 0:C3]
        else:
            gl[...] = b[0:C2, 0:C3]
    stores[2].start()
    stores[3].start()
    for i in (3, 4):
        loads[i].wait()
        stores[i - 3].start()

    loads[1].wait()
    for t in range(27):
        b = eflat[t * PITCH : t * PITCH + C2, :].astype(F32)
        ge[t // 9, (t // 3) % 3, t % 3] = b[:, 0:C3]
    stores[4].start()

    loads[2].wait()
    arf32[...] = fout[...].astype(F32)
    for k in range(3):
        d0 = arf32[2 * k * C2 : (2 * k + 1) * C2, :]
        d1 = arf32[(2 * k + 1) * C2 : (2 * k + 2) * C2, :]
        lane = lanes(d0.shape)
        b1 = pltpu.roll(jnp.where(lane >= C2, d0, d1), L - C2, 1)
        b2 = pltpu.roll(d1, 2 * L - 2 * C2, 1)
        for j, b in enumerate((d0, b1, b2)):
            gf[j, k] = b[:, 0:C2]
    stores[5].start()
    for done in stores:
        done.wait()


def body(fine_input, fine_weight, entry_weight, middle_weight, lift_weight, upstream):
    args = (fine_input, fine_weight, entry_weight, middle_weight, lift_weight.T, upstream)
    field = jax.ShapeDtypeStruct(fine_input.shape, BF)
    whole = pl.BlockSpec(memory_space=pl.ANY)
    cells3 = (N3 + 4) * (N3 + 4) * Z
    flat = [(28 * C3, L), (28 * PITCH, L), (ROWS_F, L)]

    def v(*shape):
        return pltpu.VMEM(shape, BF)

    def w(*shape):
        return pltpu.VMEM(shape, F32)

    def sems(n):
        return [pltpu.SemaphoreType.DMA((n,)), pltpu.SemaphoreType.DMA((n,))]

    def sums(rows, *sizes):
        left, sent, got = rows, [], []
        for size in sizes:
            sent.append(v(left, L))
            left //= size
            got.append(v(size - 1, left, L))
        return [*sent, *got, v(4, left, L), *sems(3 + 2 * sum(size - 1 for size in sizes))]

    scratch = [
        *[v(*arg.shape) for arg in args], v(*field.shape), v(*field.shape),
        *[v(rows, L) for rows in ROWS], v(*flat[0]), v(*flat[1]), *sems(6),
        w(TILES, Z * N2, L), w(TILES, Z * N2, L), w(N2 + 2, N2 + 2, Z, L), w(N3 + 6, N3 + 6, Z, L),
        w(N3 + 2, N3 + 2, Z, L), w(N2, N2, Z, L),
        v(N2 + 2, N2 * Z, 3 * L), v(N2 + 2, N2 * Z, 3 * L), w(N2, N2, Z, L),
        v(cells3, 9 * L), w(N3 + 4, N3 + 4, Z, L), w(N3 + 2, N3 + 2, Z, L), w(N3 + 2, N3 + 2, Z, L),
        w(N3 + 2, N3 + 2, Z, L), w(N3, N3, Z, L), w(3 * L, 3 * L), v(8 * (N2 - 2) * Z, L), w(N2, N2, Z, L),
        v(9 * L, L), v(L, 9 * L), v(9 * L, 3 * L), v(3 * L, 9 * L), v(9 * L, 3 * L), v(3 * L, 9 * L), v(L, L),
        w(ROWS_E, L), w(ROWS_F, L),
        v(5, 8, 3 * N3 * Z, L), v(5, 8, 3 * N3 * Z, L), *sems(40),
        *sums(ROWS_M, 2, 16), *sums(ROWS_E, 2, 16), *sums(ROWS_F, 2, 16),
    ]
    packed = [jax.ShapeDtypeStruct(size, BF) for size in flat]
    fields_and_sums = pl.pallas_call(
        kernel,
        out_shape=(field, field, *packed),
        in_specs=[whole] * 6,
        out_specs=[whole] * 5,
        scratch_shapes=scratch,
        compiler_params=pltpu.CompilerParams(
            collective_id=0, has_side_effects=True, vmem_limit_bytes=60 * 1024 * 1024
        ),
    )(*args)
    mixed, input_grad, fine, entry, middle, lift = pl.pallas_call(
        finish,
        out_shape=(
            field,
            field,
            jax.ShapeDtypeStruct(fine_weight.shape, F32),
            jax.ShapeDtypeStruct(entry_weight.shape, F32),
            jax.ShapeDtypeStruct(middle_weight.shape, F32),
            jax.ShapeDtypeStruct(lift_weight.shape[::-1], F32),
        ),
        in_specs=[whole] * 5,
        out_specs=[whole] * 6,
        scratch_shapes=[
            v(*field.shape), v(*field.shape), *[v(*size) for size in flat],
            w(*fine_weight.shape), w(*entry_weight.shape), w(*middle_weight.shape), w(*lift_weight.shape[::-1]),
            w(ROWS_F, L), *sems(6),
        ],
        compiler_params=pltpu.CompilerParams(vmem_limit_bytes=60 * 1024 * 1024),
    )(*fields_and_sums)
    return mixed, input_grad, fine, entry, middle, lift.T


def solution(mesh):
    assert mesh.shape["gy"] == GY and mesh.shape["gx"] == GX
    return jax.shard_map(
        body,
        mesh=mesh,
        in_specs=(P("dp", None, "gy", "gx"), P(), P(), P(), P(), P("dp", None, "gy", "gx")),
        out_specs=(P("dp", None, "gy", "gx"), P("dp", None, "gy", "gx"), P(), P(), P(), P()),
        check_vma=False,
    )
```

```python
import jax
import jax.numpy as jnp
from jax import lax
from jax.experimental import pallas as pl
from jax.experimental.pallas import tpu as pltpu
from jax.sharding import PartitionSpec as P

MESH = pl.DeviceIdType.MESH
BF = jnp.bfloat16
F32 = jnp.float32

Z = 8
N2 = 16
N3 = 8
C2 = 72
C3 = 96
L = 128
GY = 8
GX = 8
MERGED = N2 * C2
TILES = MERGED // L
DIRS = [(-1, -1), (-1, 1), (1, -1), (1, 1), (-1, 0), (1, 0), (0, -1), (0, 1)]

EX_IN, EX_POOL, EX_LOW, EX_G1, EX_FINE = range(5)

ROWS_M = 2048
ROWS_E = 1536
ROWS_F = 512
ROWS = (ROWS_M, ROWS_E, ROWS_F)
GROUPS = ("dp", "xy")
PITCH = 80


def lanes(shape):
    return lax.broadcasted_iota(jnp.int32, shape, len(shape) - 1)


def elu(v):
    return jnp.where(v > 0, v, jnp.exp(jnp.minimum(v, 0.0)) - 1.0)


def slope(s):
    return jnp.where(s > 0, 1.0, 1.0 + s)


def rounded(v):
    return v.astype(BF).astype(F32)


def shift_z(v, step):
    moved = pltpu.roll(v, step % Z, 1)
    row = lax.broadcasted_iota(jnp.int32, v.shape, 1)
    return jnp.where(row == (0 if step == 1 else Z - 1), 0.0, moved)


def nt(a, b):
    return lax.dot_general(a, b, (((1,), (1,)), ((), ())), preferred_element_type=F32)


def tn(a, b):
    return lax.dot_general(a, b, (((0,), (0,)), ((), ())), preferred_element_type=F32)


def nn(a, b):
    return jnp.dot(a, b, preferred_element_type=F32)


class Ring:
    def __init__(self):
        self.dp = lax.axis_index("dp")
        self.gy = lax.axis_index("gy")
        self.gx = lax.axis_index("gx")

    def place(self):
        return {"x": self.gy // 2, "y": self.gx // 2, "z": (self.gy % 2) * 2 + self.gx % 2}

    def member(self, kind):
        if kind == "dp":
            return self.dp
        place, m = self.place(), 0
        for axis in kind:
            m = m * 4 + place[axis]
        return m

    def device(self, kind, p):
        if kind == "dp":
            return (p, self.gy, self.gx)
        place = self.place()
        for axis in reversed(kind):
            place[axis] = p % 4
            p = p // 4
        return (self.dp, place["x"] * 2 + place["z"] // 2, place["y"] * 2 + place["z"] % 2)

    def others(self, kind):
        m = self.member(kind)
        if kind == "dp":
            return [1 - m]
        if len(kind) == 1:
            return [(m + r) % 4 for r in (2, 1, 3)]
        steps = [(2, 2), (2, 1), (1, 2), (2, 3), (3, 2), (1, 1), (1, 3), (3, 1), (3, 3)]
        steps += [(2, 0), (0, 2), (1, 0), (0, 1), (3, 0), (0, 3)]
        return [((m // 4 + x) % 4) * 4 + (m % 4 + y) % 4 for x, y in steps]


SIZE = {"dp": 2, "x": 4, "y": 4, "z": 4, "xy": 16, "xz": 16, "yz": 16}


class Reduce:
    def __init__(self, ring, rows, plan, back, bufs, recvs, slots, out, send, recv, sent):
        self.ring = ring
        self.scatter, self.last = plan[:-1], plan[-1]
        self.back = list(back)
        self.bufs = bufs
        self.recvs = recvs
        self.slots = slots
        self.out = out
        self.send = send
        self.recv = recv
        self.sent = sent
        self.used = 0
        self.rows = [rows]
        self.offs = [0]
        for kind in self.scatter:
            n = self.rows[-1] // SIZE[kind]
            self.offs.append(self.offs[-1] + ring.member(kind) * n)
            self.rows.append(n)
        self.held = self.offs[-1], n

    def _go(self, src, dst, device):
        i = self.used
        self.used += 1
        c = pltpu.make_async_remote_copy(
            src_ref=src,
            dst_ref=dst,
            send_sem=self.send.at[i],
            recv_sem=self.recv.at[i],
            device_id=device,
            device_id_type=MESH,
        )
        c.start()
        self.sent.append(c)
        return c

    def scatter_start(self, s):
        kind, n = self.scatter[s], self.rows[s + 1]
        self.now = []
        for r, p in enumerate(self.ring.others(kind)):
            src = self.bufs[s].at[pl.ds(pl.multiple_of(p * n, 16), n)]
            self.now.append(self._go(src, self.recvs[s].at[r], self.ring.device(kind, p)))

    def scatter_end(self, s):
        kind, n = self.scatter[s], self.rows[s + 1]
        m, size = self.ring.member(kind), SIZE[kind]
        for c in self.now:
            c.wait_recv()
        total = self.bufs[s][pl.ds(pl.multiple_of(m * n, 16), n), :].astype(F32)
        for r in range(size - 1):
            total = total + self.recvs[s][r].astype(F32)
        total = total.astype(BF)
        if s + 1 < len(self.scatter):
            self.bufs[s + 1][...] = total
        else:
            self.slots[self.ring.member(self.last)] = total

    def last_start(self):
        m = self.ring.member(self.last)
        self.now = []
        for p in self.ring.others(self.last):
            self.now.append(self._go(self.slots.at[m], self.slots.at[m], self.ring.device(self.last, p)))

    def last_end(self):
        for c in self.now:
            c.wait_recv()
        total = self.slots[0].astype(F32)
        for r in range(1, SIZE[self.last]):
            total = total + self.slots[r].astype(F32)
        self.out[pl.ds(pl.multiple_of(self.offs[-1], 16), self.rows[-1]), :] = total.astype(BF)

    def gather_start(self):
        kind, (off, n) = self.back.pop(0), self.held
        part = self.out.at[pl.ds(pl.multiple_of(off, 16), n)]
        self.now = []
        for p in self.ring.others(kind):
            self.now.append(self._go(part, part, self.ring.device(kind, p)))
        self.held = off - self.ring.member(kind) * n, n * SIZE[kind]

    def gather_end(self):
        for c in self.now:
            c.wait_recv()


def pack4(b):
    lane = lanes(b[0].shape)
    r1, r2, r3 = pltpu.roll(b[1], 96, 1), pltpu.roll(b[2], 64, 1), pltpu.roll(b[3], 32, 1)
    return (
        jnp.where(lane >= 96, r1, b[0]),
        jnp.where(lane < 64, r1, r2),
        jnp.where(lane < 32, r2, r3),
    )


def unpack4(d):
    lane = lanes(d[0].shape)
    return (
        d[0],
        pltpu.roll(jnp.where(lane >= 96, d[0], d[1]), 32, 1),
        pltpu.roll(jnp.where(lane >= 64, d[1], d[2]), 64, 1),
        pltpu.roll(d[2], 96, 1),
    )


def kernel(
    a_hbm, wf_hbm, we_hbm, wm_hbm, wl_hbm, u_hbm,
    mixed_hbm, ig_hbm, m_hbm, e_hbm, f_hbm,
    a_ref, wf_ref, we_ref, wm_ref, wl_ref, u_ref, mixed_ref, ig_ref, mout, eout, fout, mflat, eflat, in_sem, out_sem,
    raw, raw2, pad2, pad3, ulp, e32, x3, g3f, fa, q, c1p, c2, gp, gup, up, gsum, grim, d32,
    wf, wft, we, wet, wm, wmt, wl, are32, arf32,
    sbuf, rbuf, h_send, h_recv,
    m0, m1, mr0, mr1, mslot, m_send, m_recv,
    e0, e1, er0, er1, eslot, e_send, e_recv,
    f0, f1, fr0, fr1, fslot, f_send, f_recv,
):
    ring = Ring()
    dp, gy, gx = ring.dp, ring.gy, ring.gx

    barrier = pltpu.get_barrier_semaphore()
    met = [(dp, (gy + dy + GY) % GY, (gx + dx + GX) % GX) for dy, dx in DIRS]
    met += [ring.device(kind, p) for kind in GROUPS for p in ring.others(kind)]
    for device in met:
        pl.semaphore_signal(barrier, inc=1, device_id=device, device_id_type=MESH)

    loads = [
        pltpu.make_async_copy(src, dst, in_sem.at[i])
        for i, (src, dst) in enumerate(
            (
                (a_hbm, a_ref), (u_hbm, u_ref), (wf_hbm, wf_ref),
                (we_hbm, we_ref), (wm_hbm, wm_ref), (wl_hbm, wl_ref),
            )
        )
    ]
    for load in loads:
        load.start()

    sent = []
    stores = []

    def store(src, dst):
        stores.append(pltpu.make_async_copy(src, dst, out_sem.at[len(stores)]))
        stores[-1].start()

    def edge(step, n, w):
        return {1: slice(n, n + w), -1: slice(w, 2 * w), 0: slice(w, n + w)}[step]

    def outside(step, n, w):
        return {1: slice(0, w), -1: slice(n + w, n + 2 * w), 0: slice(w, n + w)}[step]

    def send_halo(ex, ref, n, w):
        copies = []
        for d, (dy, dx) in enumerate(DIRS):
            part = ref[edge(dy, n, w), edge(dx, n, w)].reshape(-1, L)
            if part.shape[0] % 16:
                part = jnp.concatenate([part, part[:Z]], axis=0)
            rows = part.shape[0]
            sbuf[ex, d, 0:rows, :] = part.astype(BF)
            c = pltpu.make_async_remote_copy(
                src_ref=sbuf.at[ex, d, pl.ds(0, rows)],
                dst_ref=rbuf.at[ex, d, pl.ds(0, rows)],
                send_sem=h_send.at[ex * 8 + d],
                recv_sem=h_recv.at[ex * 8 + d],
                device_id=(dp, (gy + dy + GY) % GY, (gx + dx + GX) % GX),
                device_id_type=MESH,
            )
            c.start()
            sent.append(c)
            copies.append(c)
        return copies

    def take_halo(ex, ref, n, w, copies):
        for d, (dy, dx) in enumerate(DIRS):
            copies[d].wait_recv()
            there = jnp.logical_and(
                jnp.logical_and(gy - dy >= 0, gy - dy < GY),
                jnp.logical_and(gx - dx >= 0, gx - dx < GX),
            )
            keep = jnp.where(there, 1.0, 0.0).astype(F32)
            ys, xs = outside(dy, n, w), outside(dx, n, w)
            ny, nx = ys.stop - ys.start, xs.stop - xs.start
            part = rbuf[ex, d, 0 : max(ny * nx * Z, 16), :].astype(F32)[: ny * nx * Z]
            ref[ys, xs] = (part * keep).reshape(ny, nx, Z, L)

    def spread(src_ref):
        for t in range(TILES):
            raw[t] = src_ref[0, :, :, t * L : (t + 1) * L].astype(F32).reshape(Z * N2, L)

    def read_row(y, xs, dst, shift):
        lane = lanes((Z, L))
        tiles = {}
        for x in xs:
            t, o = (x * C2) // L, (x * C2) % L
            for s in (t, t + 1) if o + C2 > L else (t,):
                if s not in tiles:
                    tiles[s] = raw[s, pl.ds(y, Z, stride=N2), :]
            cell = tiles[t] if o == 0 else pltpu.roll(tiles[t], L - o, 1)
            if o + C2 > L:
                cell = jnp.where(lane < L - o, cell, pltpu.roll(tiles[t + 1], L - o, 1))
            dst[y + shift, x + shift] = jnp.where(lane < C2, cell, 0.0)

    def read_rows(first, last, xs, dst, shift):
        def row(y, _):
            read_row(y, xs, dst, shift)
            return 0

        lax.fori_loop(first, last, row, 0)

    def write_cells(src, out32, dst_ref):
        def row(y, _):
            tiles = [None] * TILES
            lane = lanes((Z, L))
            for x in range(N2):
                t, o = (x * C2) // L, (x * C2) % L
                cell = src[y, x]
                cell = cell if o == 0 else pltpu.roll(cell, o, 1)
                tiles[t] = cell if o == 0 else jnp.where(lane >= o, cell, tiles[t])
                if o + C2 > L:
                    tiles[t + 1] = cell
            for t in range(TILES):
                out32[t, pl.ds(y, Z, stride=N2), :] = tiles[t]
            return 0

        lax.fori_loop(0, N2, row, 0)
        for t in range(TILES):
            dst_ref[0, :, :, t * L : (t + 1) * L] = out32[t].reshape(Z, N2, L).astype(BF)

    def fine_columns():
        def row(y, _):
            for k in range(3):
                x3[y, :, k * L : (k + 1) * L] = pad2[y, k : k + N2].reshape(N2 * Z, L).astype(BF)
            return 0

        lax.fori_loop(0, N2 + 2, row, 0)

    def fine_rows(chunk):
        parts = [x3[pl.ds(chunk * 4 + j, 4)].reshape(4 * N2 * Z, 3 * L) for j in range(3)]
        return jnp.concatenate(parts, axis=1)

    def columns(ref, n, off=0):
        rows = n * n * Z
        for j in range(3):
            for k in range(3):
                t = (j * 3 + k) * L
                q[0:rows, t : t + L] = (
                    ref[off + j : off + j + n, off + k : off + k + n].reshape(rows, L).astype(BF)
                )
        return q[0:rows, :]

    def tap_rows(ref, blocks, at=0):
        for y0, y1, x0, x1 in blocks:
            rows = (y1 - y0) * (x1 - x0) * Z
            for j in range(3):
                for k in range(3):
                    t = (j * 3 + k) * L
                    part = ref[y0 + j : y1 + j, x0 + k : x1 + k]
                    q[at : at + rows, t : t + L] = part.reshape(rows, L).astype(BF)
            at += rows
        return q[0:at, :]

    def put_rows(dst, blocks, cells):
        at = 0
        for y0, y1, x0, x1 in blocks:
            n = (y1 - y0) * (x1 - x0)
            dst[y0:y1, x0:x1] = cells[at : at + n].reshape(y1 - y0, x1 - x0, Z, L)
            at += n

    def rim(n, w):
        return [(0, w, 0, n), (n - w, n, 0, n), (w, n - w, 0, w), (w, n - w, n - w, n)]

    def joined(acc):
        acc = acc.reshape(-1, Z, 3 * L)
        return shift_z(acc[:, :, 0:L], 1) + acc[:, :, L : 2 * L] + shift_z(acc[:, :, 2 * L :], -1)

    def coarse_weight_grad(taps, g):
        g3 = jnp.concatenate([shift_z(g, -1), g, shift_z(g, 1)], axis=2)
        g3 = g3.reshape(N3 * N3 * Z, 3 * L).astype(BF)
        return tn(taps, g3).reshape(9, L, 3 * L)

    loads[0].wait()
    spread(a_ref)
    read_row(0, range(N2), pad2, 1)
    read_row(N2 - 1, range(N2), pad2, 1)
    read_rows(1, N2 - 1, (0, N2 - 1), pad2, 1)
    pl.semaphore_wait(barrier, len(met))
    copies = send_halo(EX_IN, pad2, N2, 1)

    read_rows(1, N2 - 1, range(1, N2 - 1), pad2, 1)
    for s in (0, N2 + 1):
        pad2[s] = jnp.zeros((N2 + 2, Z, L), F32)
        pad2[:, s : s + 1] = jnp.zeros((N2 + 2, 1, Z, L), F32)
    for load in loads[1:]:
        load.wait()
    wf[...] = jnp.zeros(wf.shape, BF)
    for j in range(3):
        for k in range(3):
            t = (j * 3 + k) * L
            wf[t : t + C2, 0:C2] = wf_ref[j, k]
    fine_columns()

    def fine_forward(chunk, _):
        act = rounded(elu(nn(fine_rows(chunk), wf[...])))
        fa[pl.ds(chunk * 4, 4)] = act.reshape(4, N2, Z, L)
        return 0

    lax.fori_loop(0, 4, fine_forward, 0)

    take_halo(EX_IN, pad2, N2, 1, copies)
    put_rows(fa, rim(N2, 1), rounded(elu(nn(tap_rows(pad2, rim(N2, 1)), wf[...]))).reshape(-1, Z, L))
    v = fa[...].reshape(N3, 2, N3, 2, Z, L)
    v = (v[:, 0, :, 0] + v[:, 0, :, 1]) + (v[:, 1, :, 0] + v[:, 1, :, 1])
    pad3[3 : N3 + 3, 3 : N3 + 3] = rounded(0.25 * v)
    copies = send_halo(EX_POOL, pad3, N3, 3)

    spread(u_ref)
    read_rows(0, N2, range(N2), e32, 0)
    low = e32[...].reshape(N3, 2, N3, 2, Z, L)
    low = (low[:, 0, :, 0] + low[:, 0, :, 1]) + (low[:, 1, :, 0] + low[:, 1, :, 1])
    ulp[1 : N3 + 1, 1 : N3 + 1] = rounded(low)
    low_copies = send_halo(EX_LOW, ulp, N3, 1)
    for ref in (wft, we, wet, wm, wmt, wl):
        ref[...] = jnp.zeros(ref.shape, BF)
    wl[0:C2, 0:C3] = wl_ref[...]
    for j in range(3):
        for k in range(3):
            t = (j * 3 + k) * L
            wft[0:C2, t : t + C2] = wf_ref[2 - j, 2 - k]
            for i in range(3):
                we[t : t + C2, i * L : i * L + C3] = we_ref[i, j, k]
                wm[t : t + C3, i * L : i * L + C3] = wm_ref[i, j, k]
                wet[i * L : i * L + C2, t : t + C3] = we_ref[2 - i, 2 - j, 2 - k]
                wmt[i * L : i * L + C3, t : t + C3] = wm_ref[2 - i, 2 - j, 2 - k]
    fine_columns()
    g3f[...] = jnp.zeros(g3f.shape, BF)
    inner = [(3, N3 + 1, 3, N3 + 1)]
    put_rows(c1p, inner, rounded(elu(joined(nn(tap_rows(pad3, inner), we[...])))))

    take_halo(EX_POOL, pad3, N3, 3, copies)
    outer = rim(N3 + 4, 3)
    put_rows(c1p, outer, rounded(elu(joined(nn(tap_rows(pad3, outer), we[...])))))
    for there, ys, xs in (
        (gy > 0, slice(0, 2), slice(None)),
        (gy < GY - 1, slice(N3 + 2, N3 + 4), slice(None)),
        (gx > 0, slice(None), slice(0, 2)),
        (gx < GX - 1, slice(None), slice(N3 + 2, N3 + 4)),
    ):
        c1p[ys, xs] = c1p[ys, xs] * jnp.where(there, 1.0, 0.0).astype(F32)
    take_halo(EX_LOW, ulp, N3, 1, low_copies)
    two = rounded(elu(joined(nn(columns(c1p, N3 + 2), wm[...]))))
    c2[...] = two.reshape(N3 + 2, N3 + 2, Z, L)
    back = nn(ulp[...].reshape(-1, L).astype(BF), wl[...]).reshape(-1, Z, L)
    gp[...] = rounded(back * slope(two)).reshape(N3 + 2, N3 + 2, Z, L)

    def grad_one(blocks):
        acc = joined(nt(tap_rows(gp, blocks), wmt[...]))
        at = 0
        for y0, y1, x0, x1 in blocks:
            n = (y1 - y0) * (x1 - x0)
            one = c1p[2 + y0 : 2 + y1, 2 + x0 : 2 + x1].reshape(n, Z, L)
            g1 = rounded(acc[at : at + n] * slope(one))
            gup[1 + y0 : 1 + y1, 1 + x0 : 1 + x1] = g1.reshape(y1 - y0, x1 - x0, Z, L)
            at += n

    inner = [(1, N3 - 1, 1, N3 - 1)]
    grad_one(rim(N3, 1))
    copies = send_halo(EX_G1, gup, N3, 1)

    mid = coarse_weight_grad(
        columns(c1p, N3, 1), gp[1 : N3 + 1, 1 : N3 + 1].reshape(-1, Z, L)
    )
    two = c2[1 : N3 + 1, 1 : N3 + 1].reshape(-1, L).astype(BF)
    lift_grad = tn(ulp[1 : N3 + 1, 1 : N3 + 1].reshape(-1, L).astype(BF), two)
    blocks = [mid[t, :C3, i * L : (i + 1) * L] for i in range(3) for t in range(9)]
    blocks.append(lift_grad[:C3])
    for g in range(7):
        for d, part in enumerate(pack4(blocks[4 * g : 4 * g + 4])):
            m0[(g * 3 + d) * C3 : (g * 3 + d + 1) * C3, :] = part.astype(BF)
    m0[21 * C3 :, :] = jnp.zeros((ROWS_M - 21 * C3, L), BF)
    red_m = Reduce(ring, ROWS_M, ("dp", "xy", "z"), ("xy", "dp"), (m0, m1), (mr0, mr1), mslot, mout, m_send, m_recv, sent)
    red_m.scatter_start(0)
    grad_one(inner)
    ent = coarse_weight_grad(columns(pad3, N3, 2), gup[1 : N3 + 1, 1 : N3 + 1].reshape(-1, Z, L))
    blocks = [ent[t, :C2, i * L : (i + 1) * L] for i in range(3) for t in range(9)]
    blocks.append(jnp.zeros((C2, L), F32))
    for g in range(7):
        for d, part in enumerate(pack4(blocks[4 * g : 4 * g + 4])):
            are32[(g * 3 + d) * C2 : (g * 3 + d + 1) * C2, :] = part
    are32[21 * C2 :, :] = jnp.zeros((ROWS_E - 21 * C2, L), F32)
    e0[...] = are32[...].astype(BF)
    red_e = Reduce(ring, ROWS_E, ("dp", "xy", "z"), ("xy", "dp"), (e0, e1), (er0, er1), eslot, eout, e_send, e_recv, sent)
    red_e.scatter_start(0)
    red_m.scatter_end(0)
    red_m.scatter_start(1)

    low = rounded(joined(nt(tap_rows(gup, inner), wet[...])))
    put_rows(up, inner, 0.25 * low)

    red_e.scatter_end(0)
    red_e.scatter_start(1)

    def fine_back(y, _):
        act = fa[pl.ds(y * 2, 2), 2 : N2 - 2].reshape(2, N3 - 2, 2, Z, L)
        e = e32[pl.ds(y * 2, 2), 2 : N2 - 2].reshape(2, N3 - 2, 2, Z, L)
        g = e + up[pl.ds(y, 1), 1 : N3 - 1].reshape(1, N3 - 2, 1, Z, L)
        g = (g * slope(act)).reshape(2, (N2 - 4) * Z, L).astype(BF)
        for j in range(3):
            g3f[pl.ds(y * 2 + j, 2), 2 * Z : (N2 - 2) * Z, j * L : (j + 1) * L] = g
        pad2[pl.ds(y * 2 + 1, 2), 3 : N2 - 1] = g.astype(F32).reshape(2, N2 - 4, Z, L)
        return 0

    lax.fori_loop(1, N3 - 1, fine_back, 0)
    gsum[...] = tn(x3[...].reshape(-1, 3 * L), g3f[...].reshape(-1, 3 * L))
    start = at = 4 * (N3 - 1) * Z
    for y0, y1, x0, x1 in rim(N2, 2):
        rows = (y1 - y0) * (x1 - x0) * Z
        for j in range(3):
            part = x3[y0 + j : y1 + j, x0 * Z : x1 * Z, :].reshape(rows, 3 * L)
            q[at : at + rows, 3 * j * L : 3 * (j + 1) * L] = part
        at += rows

    take_halo(EX_G1, gup, N3, 1, copies)
    low = rounded(joined(nt(tap_rows(gup, rim(N3, 1)), wet[...])))
    put_rows(up, rim(N3, 1), 0.25 * low)
    rows = 0
    for y0, y1, x0, x1 in rim(N2, 2):
        ny, nx = (y1 - y0) // 2, (x1 - x0) // 2
        act = fa[y0:y1, x0:x1].reshape(ny, 2, nx, 2, Z, L)
        e = e32[y0:y1, x0:x1].reshape(ny, 2, nx, 2, Z, L)
        g = e + up[y0 // 2 : y1 // 2, x0 // 2 : x1 // 2].reshape(ny, 1, nx, 1, Z, L)
        g = (g * slope(act)).reshape(-1, L).astype(BF)
        grim[rows : rows + g.shape[0], :] = g
        rows += g.shape[0]
        pad2[y0 + 1 : y1 + 1, x0 + 1 : x1 + 1] = g.astype(F32).reshape(y1 - y0, x1 - x0, Z, L)

    grad = tn(q[start:at, :], grim[...])
    for k in range(3):
        b0, b1, b2 = [
            gsum[k * L : k * L + C2, j * L : (j + 1) * L] + grad[(j * 3 + k) * L : (j * 3 + k) * L + C2]
            for j in range(3)
        ]
        lane = lanes(b0.shape)
        r1, r2 = pltpu.roll(b1, C2, 1), pltpu.roll(b2, 2 * C2 - L, 1)
        arf32[2 * k * C2 : (2 * k + 1) * C2, :] = jnp.where(lane < C2, b0, r1)
        arf32[(2 * k + 1) * C2 : (2 * k + 2) * C2, :] = jnp.where(lane < 2 * C2 - L, r1, r2)
    arf32[6 * C2 :, :] = jnp.zeros((ROWS_F - 6 * C2, L), F32)
    f0[...] = arf32[...].astype(BF)
    red_f = Reduce(ring, ROWS_F, ("dp", "xy", "z"), ("xy", "dp"), (f0, f1), (fr0, fr1), fslot, fout, f_send, f_recv, sent)
    red_f.scatter_start(0)
    copies = send_halo(EX_FINE, pad2, N2, 1)
    red_f.scatter_end(0)
    red_f.scatter_start(1)
    red_m.scatter_end(1)
    red_m.last_start()

    two = c2[1 : N3 + 1, 1 : N3 + 1].reshape(-1, L).astype(BF)
    up[...] = rounded(nt(two, wl[...])).reshape(N3, N3, Z, L)

    def mix(y, _):
        act = fa[pl.ds(y * 2, 2)].reshape(2, N3, 2, Z, L)
        lifted = up[pl.ds(y, 1)].reshape(1, N3, 1, Z, L)
        d32[pl.ds(y * 2, 2)] = (act + lifted).reshape(2, N2, Z, L)
        return 0

    lax.fori_loop(0, N3, mix, 0)

    red_e.scatter_end(1)
    red_e.last_start()
    write_cells(d32, raw, mixed_ref)
    store(mixed_ref, mixed_hbm)

    red_f.scatter_end(1)
    red_f.last_start()
    red_m.last_end()
    red_m.gather_start()
    red_e.last_end()
    red_e.gather_start()

    take_halo(EX_FINE, pad2, N2, 1, copies)
    fine_columns()

    def fine_backward(chunk, _):
        d32[pl.ds(chunk * 4, 4)] = nt(fine_rows(chunk), wft[...]).reshape(4, N2, Z, L)
        return 0

    lax.fori_loop(0, 4, fine_backward, 0)

    red_f.last_end()
    red_f.gather_start()

    write_cells(d32, raw2, ig_ref)
    store(ig_ref, ig_hbm)
    for c in sent[:-45]:
        c.wait_send()
    del sent[:-45]

    red_m.gather_end()
    red_m.gather_start()
    red_e.gather_end()
    red_e.gather_start()
    red_f.gather_end()
    red_f.gather_start()
    red_m.gather_end()
    for g in range(7):
        d = [mout[(g * 3 + s) * C3 : (g * 3 + s + 1) * C3, :].astype(F32) for s in range(3)]
        for s, b in enumerate(unpack4(d)):
            mflat[(g * 4 + s) * C3 : (g * 4 + s + 1) * C3, :] = b.astype(BF)
    store(mflat, m_hbm)
    red_e.gather_end()
    are32[...] = eout[...].astype(F32)
    for g in range(7):
        d = [are32[(g * 3 + s) * C2 : (g * 3 + s + 1) * C2, :] for s in range(3)]
        for s, b in enumerate(unpack4(d)):
            eflat[(g * 4 + s) * PITCH : (g * 4 + s) * PITCH + C2, :] = b.astype(BF)
    store(eflat, e_hbm)
    red_f.gather_end()
    store(fout, f_hbm)
    for c in sent:
        c.wait_send()
    for done in stores:
        done.wait()


def finish(
    mixed_in, ig_in, m_hbm, e_hbm, f_hbm, mixed, ig, gf_hbm, ge_hbm, gm_hbm, gl_hbm,
    mixed_ref, ig_ref, mflat, eflat, fout, gf, ge, gm, gl, arf32, in_sem, out_sem,
):
    mid, low = 9 * C3, 9 * PITCH
    ends = (mid, 2 * mid, 28 * C3)
    parts = [(mixed_in, mixed_ref), (ig_in, ig_ref)]
    for i in range(3):
        rows = pl.ds(i * mid, ends[i] - i * mid)
        parts.append((m_hbm.at[rows], mflat.at[rows]))
    for i in range(3):
        parts.append((e_hbm.at[pl.ds(i * low, low)], eflat.at[pl.ds(i * low, low)]))
    parts.append((f_hbm, fout))
    loads = [pltpu.make_async_copy(src, dst, in_sem.at[i]) for i, (src, dst) in enumerate(parts)]
    for load in loads:
        load.start()
    parts = [(mixed_ref, mixed), (ig_ref, ig)]
    parts += [(gm.at[i], gm_hbm.at[i]) for i in range(3)]
    parts += [(ge.at[i], ge_hbm.at[i]) for i in range(3)]
    parts += [(gf, gf_hbm), (gl, gl_hbm)]
    stores = [pltpu.make_async_copy(src, dst, out_sem.at[i]) for i, (src, dst) in enumerate(parts)]

    for i in range(2):
        loads[i].wait()
        stores[i].start()
    for i in range(3):
        loads[2 + i].wait()
        for t in range(9):
            at = (i * 9 + t) * C3
            gm[i, t // 3, t % 3] = mflat[at : at + C3, :].astype(F32)[:, 0:C3]
        stores[2 + i].start()
    gl[...] = mflat[27 * C3 :, :].astype(F32)[0:C2, 0:C3]
    stores[9].start()
    for i in range(3):
        loads[5 + i].wait()
        for t in range(9):
            at = (i * 9 + t) * PITCH
            ge[i, t // 3, t % 3] = eflat[at : at + C2, :].astype(F32)[:, 0:C3]
        stores[5 + i].start()

    loads[8].wait()
    arf32[...] = fout[...].astype(F32)
    for k in range(3):
        d0 = arf32[2 * k * C2 : (2 * k + 1) * C2, :]
        d1 = arf32[(2 * k + 1) * C2 : (2 * k + 2) * C2, :]
        lane = lanes(d0.shape)
        b1 = pltpu.roll(jnp.where(lane >= C2, d0, d1), L - C2, 1)
        b2 = pltpu.roll(d1, 2 * L - 2 * C2, 1)
        for j, b in enumerate((d0, b1, b2)):
            gf[j, k] = b[:, 0:C2]
    stores[8].start()
    for done in stores:
        done.wait()


def body(fine_input, fine_weight, entry_weight, middle_weight, lift_weight, upstream):
    args = (fine_input, fine_weight, entry_weight, middle_weight, lift_weight.T, upstream)
    field = jax.ShapeDtypeStruct(fine_input.shape, BF)
    whole = pl.BlockSpec(memory_space=pl.ANY)
    cells3 = (N3 + 4) * (N3 + 4) * Z
    flat = [(28 * C3, L), (28 * PITCH, L), (ROWS_F, L)]

    def v(*shape):
        return pltpu.VMEM(shape, BF)

    def w(*shape):
        return pltpu.VMEM(shape, F32)

    def sems(n):
        return [pltpu.SemaphoreType.DMA((n,)), pltpu.SemaphoreType.DMA((n,))]

    def sums(rows, *sizes):
        left, sent, got = rows, [], []
        for size in sizes:
            sent.append(v(left, L))
            left //= size
            got.append(v(size - 1, left, L))
        return [*sent, *got, v(4, left, L), *sems(3 + 2 * sum(size - 1 for size in sizes))]

    scratch = [
        *[v(*arg.shape) for arg in args], v(*field.shape), v(*field.shape),
        *[v(rows, L) for rows in ROWS], v(*flat[0]), v(*flat[1]), *sems(6),
        w(TILES, Z * N2, L), w(TILES, Z * N2, L), w(N2 + 2, N2 + 2, Z, L), w(N3 + 6, N3 + 6, Z, L),
        w(N3 + 2, N3 + 2, Z, L), w(N2, N2, Z, L),
        v(N2 + 2, N2 * Z, 3 * L), v(N2 + 2, N2 * Z, 3 * L), w(N2, N2, Z, L),
        v(cells3, 9 * L), w(N3 + 4, N3 + 4, Z, L), w(N3 + 2, N3 + 2, Z, L), w(N3 + 2, N3 + 2, Z, L),
        w(N3 + 2, N3 + 2, Z, L), w(N3, N3, Z, L), w(3 * L, 3 * L), v(8 * (N2 - 2) * Z, L), w(N2, N2, Z, L),
        v(9 * L, L), v(L, 9 * L), v(9 * L, 3 * L), v(3 * L, 9 * L), v(9 * L, 3 * L), v(3 * L, 9 * L), v(L, L),
        w(ROWS_E, L), w(ROWS_F, L),
        v(5, 8, 3 * N3 * Z, L), v(5, 8, 3 * N3 * Z, L), *sems(40),
        *sums(ROWS_M, 2, 16), *sums(ROWS_E, 2, 16), *sums(ROWS_F, 2, 16),
    ]
    packed = [jax.ShapeDtypeStruct(size, BF) for size in flat]
    fields_and_sums = pl.pallas_call(
        kernel,
        out_shape=(field, field, *packed),
        in_specs=[whole] * 6,
        out_specs=[whole] * 5,
        scratch_shapes=scratch,
        compiler_params=pltpu.CompilerParams(
            collective_id=0, has_side_effects=True, vmem_limit_bytes=60 * 1024 * 1024
        ),
    )(*args)
    mixed, input_grad, fine, entry, middle, lift = pl.pallas_call(
        finish,
        out_shape=(
            field,
            field,
            jax.ShapeDtypeStruct(fine_weight.shape, F32),
            jax.ShapeDtypeStruct(entry_weight.shape, F32),
            jax.ShapeDtypeStruct(middle_weight.shape, F32),
            jax.ShapeDtypeStruct(lift_weight.shape[::-1], F32),
        ),
        in_specs=[whole] * 5,
        out_specs=[whole] * 6,
        scratch_shapes=[
            v(*field.shape), v(*field.shape), *[v(*size) for size in flat],
            w(*fine_weight.shape), w(*entry_weight.shape), w(*middle_weight.shape), w(*lift_weight.shape[::-1]),
            w(ROWS_F, L), *sems(10),
        ],
        compiler_params=pltpu.CompilerParams(vmem_limit_bytes=60 * 1024 * 1024),
    )(*fields_and_sums)
    return mixed, input_grad, fine, entry, middle, lift.T


def solution(mesh):
    assert mesh.shape["gy"] == GY and mesh.shape["gx"] == GX
    return jax.shard_map(
        body,
        mesh=mesh,
        in_specs=(P("dp", None, "gy", "gx"), P(), P(), P(), P(), P("dp", None, "gy", "gx")),
        out_specs=(P("dp", None, "gy", "gx"), P("dp", None, "gy", "gx"), P(), P(), P(), P()),
        check_vma=False,
    )
```

```python
import jax
import jax.numpy as jnp
from jax import lax
from jax.experimental import pallas as pl
from jax.experimental.pallas import tpu as pltpu
from jax.sharding import PartitionSpec as P

MESH = pl.DeviceIdType.MESH
BF = jnp.bfloat16
F32 = jnp.float32

Z = 8
N2 = 16
N3 = 8
C2 = 72
C3 = 96
L = 128
GY = 8
GX = 8
MERGED = N2 * C2
TILES = MERGED // L
DIRS = [(-1, -1), (-1, 1), (1, -1), (1, 1), (-1, 0), (1, 0), (0, -1), (0, 1)]

EX_IN, EX_POOL, EX_LOW, EX_G1, EX_FINE = range(5)

ROWS_M = 2048
ROWS_E = 1536
ROWS_F = 512
ROWS = (ROWS_M, ROWS_E, ROWS_F)
GROUPS = ("dp", "xy")
PITCH = 80


def lanes(shape):
    return lax.broadcasted_iota(jnp.int32, shape, len(shape) - 1)


def elu(v):
    return jnp.where(v > 0, v, jnp.exp(jnp.minimum(v, 0.0)) - 1.0)


def slope(s):
    return jnp.where(s > 0, 1.0, 1.0 + s)


def rounded(v):
    return v.astype(BF).astype(F32)


def shift_z(v, step):
    moved = pltpu.roll(v, step % Z, 1)
    row = lax.broadcasted_iota(jnp.int32, v.shape, 1)
    return jnp.where(row == (0 if step == 1 else Z - 1), 0.0, moved)


def nt(a, b):
    return lax.dot_general(a, b, (((1,), (1,)), ((), ())), preferred_element_type=F32)


def tn(a, b):
    return lax.dot_general(a, b, (((0,), (0,)), ((), ())), preferred_element_type=F32)


def nn(a, b):
    return jnp.dot(a, b, preferred_element_type=F32)


class Ring:
    def __init__(self):
        self.dp = lax.axis_index("dp")
        self.gy = lax.axis_index("gy")
        self.gx = lax.axis_index("gx")

    def place(self):
        return {"x": self.gy // 2, "y": self.gx // 2, "z": (self.gy % 2) * 2 + self.gx % 2}

    def member(self, kind):
        if kind == "dp":
            return self.dp
        place, m = self.place(), 0
        for axis in kind:
            m = m * 4 + place[axis]
        return m

    def device(self, kind, p):
        if kind == "dp":
            return (p, self.gy, self.gx)
        place = self.place()
        for axis in reversed(kind):
            place[axis] = p % 4
            p = p // 4
        return (self.dp, place["x"] * 2 + place["z"] // 2, place["y"] * 2 + place["z"] % 2)

    def others(self, kind):
        m = self.member(kind)
        if kind == "dp":
            return [1 - m]
        if len(kind) == 1:
            return [(m + r) % 4 for r in (2, 1, 3)]
        steps = [(2, 2), (2, 1), (1, 2), (2, 3), (3, 2), (1, 1), (1, 3), (3, 1), (3, 3)]
        steps += [(2, 0), (0, 2), (1, 0), (0, 1), (3, 0), (0, 3)]
        return [((m // 4 + x) % 4) * 4 + (m % 4 + y) % 4 for x, y in steps]


SIZE = {"dp": 2, "x": 4, "y": 4, "z": 4, "xy": 16, "xz": 16, "yz": 16}


class Reduce:
    def __init__(self, ring, rows, plan, back, bufs, recvs, slots, out, send, recv, sent):
        self.ring = ring
        self.scatter, self.last = plan[:-1], plan[-1]
        self.back = list(back)
        self.bufs = bufs
        self.recvs = recvs
        self.slots = slots
        self.out = out
        self.send = send
        self.recv = recv
        self.sent = sent
        self.used = 0
        self.rows = [rows]
        self.offs = [0]
        for kind in self.scatter:
            n = self.rows[-1] // SIZE[kind]
            self.offs.append(self.offs[-1] + ring.member(kind) * n)
            self.rows.append(n)
        self.held = self.offs[-1], n

    def _go(self, src, dst, device):
        i = self.used
        self.used += 1
        c = pltpu.make_async_remote_copy(
            src_ref=src,
            dst_ref=dst,
            send_sem=self.send.at[i],
            recv_sem=self.recv.at[i],
            device_id=device,
            device_id_type=MESH,
        )
        c.start()
        self.sent.append(c)
        return c

    def scatter_start(self, s):
        kind, n = self.scatter[s], self.rows[s + 1]
        self.now = []
        for r, p in enumerate(self.ring.others(kind)):
            src = self.bufs[s].at[pl.ds(pl.multiple_of(p * n, 16), n)]
            self.now.append(self._go(src, self.recvs[s].at[r], self.ring.device(kind, p)))

    def scatter_end(self, s):
        kind, n = self.scatter[s], self.rows[s + 1]
        m, size = self.ring.member(kind), SIZE[kind]
        for c in self.now:
            c.wait_recv()
        total = self.bufs[s][pl.ds(pl.multiple_of(m * n, 16), n), :].astype(F32)
        for r in range(size - 1):
            total = total + self.recvs[s][r].astype(F32)
        total = total.astype(BF)
        if s + 1 < len(self.scatter):
            self.bufs[s + 1][...] = total
        else:
            self.slots[self.ring.member(self.last)] = total

    def last_start(self):
        m = self.ring.member(self.last)
        self.now = []
        for p in self.ring.others(self.last):
            self.now.append(self._go(self.slots.at[m], self.slots.at[m], self.ring.device(self.last, p)))

    def last_end(self):
        for c in self.now:
            c.wait_recv()
        total = self.slots[0].astype(F32)
        for r in range(1, SIZE[self.last]):
            total = total + self.slots[r].astype(F32)
        self.out[pl.ds(pl.multiple_of(self.offs[-1], 16), self.rows[-1]), :] = total.astype(BF)

    def gather_start(self):
        kind, (off, n) = self.back.pop(0), self.held
        part = self.out.at[pl.ds(pl.multiple_of(off, 16), n)]
        self.now = []
        for p in self.ring.others(kind):
            self.now.append(self._go(part, part, self.ring.device(kind, p)))
        self.held = off - self.ring.member(kind) * n, n * SIZE[kind]

    def gather_end(self):
        for c in self.now:
            c.wait_recv()


def pack4(b):
    lane = lanes(b[0].shape)
    r1, r2, r3 = pltpu.roll(b[1], 96, 1), pltpu.roll(b[2], 64, 1), pltpu.roll(b[3], 32, 1)
    return (
        jnp.where(lane >= 96, r1, b[0]),
        jnp.where(lane < 64, r1, r2),
        jnp.where(lane < 32, r2, r3),
    )


def unpack4(d):
    lane = lanes(d[0].shape)
    return (
        d[0],
        pltpu.roll(jnp.where(lane >= 96, d[0], d[1]), 32, 1),
        pltpu.roll(jnp.where(lane >= 64, d[1], d[2]), 64, 1),
        pltpu.roll(d[2], 96, 1),
    )


def kernel(
    a_hbm, wf_hbm, we_hbm, wm_hbm, wl_hbm, u_hbm,
    mixed_hbm, ig_hbm, m_hbm, e_hbm, f_hbm,
    a_ref, wf_ref, we_ref, wm_ref, wl_ref, u_ref, mixed_ref, ig_ref, mout, eout, fout, mflat, eflat, in_sem, out_sem,
    raw, raw2, pad2, pad3, ulp, e32, x3, g3f, fa, q, c1p, c2, gp, gup, up, gsum, grim, d32,
    wf, wft, we, wet, wm, wmt, wl, are32, arf32,
    sbuf, rbuf, h_send, h_recv,
    m0, m1, mr0, mr1, mslot, m_send, m_recv,
    e0, e1, er0, er1, eslot, e_send, e_recv,
    f0, f1, fr0, fr1, fslot, f_send, f_recv,
):
    ring = Ring()
    dp, gy, gx = ring.dp, ring.gy, ring.gx

    barrier = pltpu.get_barrier_semaphore()
    met = [(dp, (gy + dy + GY) % GY, (gx + dx + GX) % GX) for dy, dx in DIRS]
    met += [ring.device(kind, p) for kind in GROUPS for p in ring.others(kind)]
    for device in met:
        pl.semaphore_signal(barrier, inc=1, device_id=device, device_id_type=MESH)

    loads = [
        pltpu.make_async_copy(src, dst, in_sem.at[i])
        for i, (src, dst) in enumerate(
            (
                (a_hbm, a_ref), (u_hbm, u_ref), (wf_hbm, wf_ref),
                (we_hbm, we_ref), (wm_hbm, wm_ref), (wl_hbm, wl_ref),
            )
        )
    ]
    for load in loads:
        load.start()

    sent = []
    stores = []

    def store(src, dst):
        stores.append(pltpu.make_async_copy(src, dst, out_sem.at[len(stores)]))
        stores[-1].start()

    def edge(step, n, w):
        return {1: slice(n, n + w), -1: slice(w, 2 * w), 0: slice(w, n + w)}[step]

    def outside(step, n, w):
        return {1: slice(0, w), -1: slice(n + w, n + 2 * w), 0: slice(w, n + w)}[step]

    def send_halo(ex, ref, n, w):
        copies = []
        for d, (dy, dx) in enumerate(DIRS):
            part = ref[edge(dy, n, w), edge(dx, n, w)].reshape(-1, L)
            if part.shape[0] % 16:
                part = jnp.concatenate([part, part[:Z]], axis=0)
            rows = part.shape[0]
            sbuf[ex, d, 0:rows, :] = part.astype(BF)
            c = pltpu.make_async_remote_copy(
                src_ref=sbuf.at[ex, d, pl.ds(0, rows)],
                dst_ref=rbuf.at[ex, d, pl.ds(0, rows)],
                send_sem=h_send.at[ex * 8 + d],
                recv_sem=h_recv.at[ex * 8 + d],
                device_id=(dp, (gy + dy + GY) % GY, (gx + dx + GX) % GX),
                device_id_type=MESH,
            )
            c.start()
            sent.append(c)
            copies.append(c)
        return copies

    def take_halo(ex, ref, n, w, copies):
        for d, (dy, dx) in enumerate(DIRS):
            copies[d].wait_recv()
            there = jnp.logical_and(
                jnp.logical_and(gy - dy >= 0, gy - dy < GY),
                jnp.logical_and(gx - dx >= 0, gx - dx < GX),
            )
            keep = jnp.where(there, 1.0, 0.0).astype(F32)
            ys, xs = outside(dy, n, w), outside(dx, n, w)
            ny, nx = ys.stop - ys.start, xs.stop - xs.start
            part = rbuf[ex, d, 0 : max(ny * nx * Z, 16), :].astype(F32)[: ny * nx * Z]
            ref[ys, xs] = (part * keep).reshape(ny, nx, Z, L)

    def spread(src_ref):
        for t in range(TILES):
            raw[t, 0 : Z * N2] = src_ref[0, :, :, t * L : (t + 1) * L].astype(F32).reshape(Z * N2, L)

    def read_row(y, xs, dst, shift):
        lane = lanes((Z, L))
        tiles = {}
        for x in xs:
            t, o = (x * C2) // L, (x * C2) % L
            for s in (t, t + 1) if o + C2 > L else (t,):
                if s not in tiles:
                    tiles[s] = raw[s, pl.ds(y, Z, stride=N2), :]
            cell = tiles[t] if o == 0 else pltpu.roll(tiles[t], L - o, 1)
            if o + C2 > L:
                cell = jnp.where(lane < L - o, cell, pltpu.roll(tiles[t + 1], L - o, 1))
            dst[y + shift, x + shift] = jnp.where(lane < C2, cell, 0.0)

    def read_rows(first, last, xs, dst, shift):
        def row(y, _):
            read_row(y, xs, dst, shift)
            return 0

        lax.fori_loop(first, last, row, 0)

    def write_cells(src, out32, dst_ref):
        def row(y, _):
            tiles = [None] * TILES
            lane = lanes((Z, L))
            for x in range(N2):
                t, o = (x * C2) // L, (x * C2) % L
                cell = src[y, x]
                cell = cell if o == 0 else pltpu.roll(cell, o, 1)
                tiles[t] = cell if o == 0 else jnp.where(lane >= o, cell, tiles[t])
                if o + C2 > L:
                    tiles[t + 1] = cell
            for t in range(TILES):
                out32[t, pl.ds(y, Z, stride=N2), :] = tiles[t]
            return 0

        lax.fori_loop(0, N2, row, 0)
        for t in range(TILES):
            dst_ref[0, :, :, t * L : (t + 1) * L] = out32[t, 0 : Z * N2].reshape(Z, N2, L).astype(BF)

    def fine_columns():
        def row(y, _):
            for k in range(3):
                x3[y, :, k * L : (k + 1) * L] = pad2[y, k : k + N2].reshape(N2 * Z, L).astype(BF)
            return 0

        lax.fori_loop(0, N2 + 2, row, 0)

    def fine_rows(chunk):
        parts = [x3[pl.ds(chunk * 4 + j, 4)].reshape(4 * N2 * Z, 3 * L) for j in range(3)]
        return jnp.concatenate(parts, axis=1)

    def columns(ref, n, off=0):
        rows = n * n * Z
        for j in range(3):
            for k in range(3):
                t = (j * 3 + k) * L
                q[0:rows, t : t + L] = (
                    ref[off + j : off + j + n, off + k : off + k + n].reshape(rows, L).astype(BF)
                )
        return q[0:rows, :]

    def tap_rows(ref, blocks, at=0):
        for y0, y1, x0, x1 in blocks:
            rows = (y1 - y0) * (x1 - x0) * Z
            for j in range(3):
                for k in range(3):
                    t = (j * 3 + k) * L
                    part = ref[y0 + j : y1 + j, x0 + k : x1 + k]
                    q[at : at + rows, t : t + L] = part.reshape(rows, L).astype(BF)
            at += rows
        return q[0:at, :]

    def put_rows(dst, blocks, cells):
        at = 0
        for y0, y1, x0, x1 in blocks:
            n = (y1 - y0) * (x1 - x0)
            dst[y0:y1, x0:x1] = cells[at : at + n].reshape(y1 - y0, x1 - x0, Z, L)
            at += n

    def rim(n, w):
        return [(0, w, 0, n), (n - w, n, 0, n), (w, n - w, 0, w), (w, n - w, n - w, n)]

    def joined(acc):
        acc = acc.reshape(-1, Z, 3 * L)
        return shift_z(acc[:, :, 0:L], 1) + acc[:, :, L : 2 * L] + shift_z(acc[:, :, 2 * L :], -1)

    def coarse_weight_grad(taps, g):
        g3 = jnp.concatenate([shift_z(g, -1), g, shift_z(g, 1)], axis=2)
        g3 = g3.reshape(N3 * N3 * Z, 3 * L).astype(BF)
        return tn(taps, g3).reshape(9, L, 3 * L)

    loads[0].wait()
    spread(a_ref)
    read_row(0, range(N2), pad2, 1)
    read_row(N2 - 1, range(N2), pad2, 1)
    read_rows(1, N2 - 1, (0, N2 - 1), pad2, 1)
    pl.semaphore_wait(barrier, len(met))
    copies = send_halo(EX_IN, pad2, N2, 1)

    read_rows(1, N2 - 1, range(1, N2 - 1), pad2, 1)
    for s in (0, N2 + 1):
        pad2[s] = jnp.zeros((N2 + 2, Z, L), F32)
        pad2[:, s : s + 1] = jnp.zeros((N2 + 2, 1, Z, L), F32)
    for load in loads[1:]:
        load.wait()
    wf[...] = jnp.zeros(wf.shape, BF)
    for j in range(3):
        for k in range(3):
            t = (j * 3 + k) * L
            wf[t : t + C2, 0:C2] = wf_ref[j, k]
    fine_columns()

    def fine_forward(chunk, _):
        act = rounded(elu(nn(fine_rows(chunk), wf[...])))
        fa[pl.ds(chunk * 4, 4)] = act.reshape(4, N2, Z, L)
        return 0

    lax.fori_loop(0, 4, fine_forward, 0)

    take_halo(EX_IN, pad2, N2, 1, copies)
    put_rows(fa, rim(N2, 1), rounded(elu(nn(tap_rows(pad2, rim(N2, 1)), wf[...]))).reshape(-1, Z, L))
    v = fa[...].reshape(N3, 2, N3, 2, Z, L)
    v = (v[:, 0, :, 0] + v[:, 0, :, 1]) + (v[:, 1, :, 0] + v[:, 1, :, 1])
    pad3[3 : N3 + 3, 3 : N3 + 3] = rounded(0.25 * v)
    copies = send_halo(EX_POOL, pad3, N3, 3)

    spread(u_ref)
    read_rows(0, N2, range(N2), e32, 0)
    low = e32[...].reshape(N3, 2, N3, 2, Z, L)
    low = (low[:, 0, :, 0] + low[:, 0, :, 1]) + (low[:, 1, :, 0] + low[:, 1, :, 1])
    ulp[1 : N3 + 1, 1 : N3 + 1] = rounded(low)
    low_copies = send_halo(EX_LOW, ulp, N3, 1)
    for ref in (wft, we, wet, wm, wmt, wl):
        ref[...] = jnp.zeros(ref.shape, BF)
    wl[0:C2, 0:C3] = wl_ref[...]
    for j in range(3):
        for k in range(3):
            t = (j * 3 + k) * L
            wft[0:C2, t : t + C2] = wf_ref[2 - j, 2 - k]
            for i in range(3):
                we[t : t + C2, i * L : i * L + C3] = we_ref[i, j, k]
                wm[t : t + C3, i * L : i * L + C3] = wm_ref[i, j, k]
                wet[i * L : i * L + C2, t : t + C3] = we_ref[2 - i, 2 - j, 2 - k]
                wmt[i * L : i * L + C3, t : t + C3] = wm_ref[2 - i, 2 - j, 2 - k]
    fine_columns()
    g3f[...] = jnp.zeros(g3f.shape, BF)
    inner = [(3, N3 + 1, 3, N3 + 1)]
    put_rows(c1p, inner, rounded(elu(joined(nn(tap_rows(pad3, inner), we[...])))))

    take_halo(EX_POOL, pad3, N3, 3, copies)
    outer = rim(N3 + 4, 3)
    put_rows(c1p, outer, rounded(elu(joined(nn(tap_rows(pad3, outer), we[...])))))
    for there, ys, xs in (
        (gy > 0, slice(0, 2), slice(None)),
        (gy < GY - 1, slice(N3 + 2, N3 + 4), slice(None)),
        (gx > 0, slice(None), slice(0, 2)),
        (gx < GX - 1, slice(None), slice(N3 + 2, N3 + 4)),
    ):
        c1p[ys, xs] = c1p[ys, xs] * jnp.where(there, 1.0, 0.0).astype(F32)
    take_halo(EX_LOW, ulp, N3, 1, low_copies)
    two = rounded(elu(joined(nn(columns(c1p, N3 + 2), wm[...]))))
    c2[...] = two.reshape(N3 + 2, N3 + 2, Z, L)
    back = nn(ulp[...].reshape(-1, L).astype(BF), wl[...]).reshape(-1, Z, L)
    gp[...] = rounded(back * slope(two)).reshape(N3 + 2, N3 + 2, Z, L)

    def grad_one(blocks):
        acc = joined(nt(tap_rows(gp, blocks), wmt[...]))
        at = 0
        for y0, y1, x0, x1 in blocks:
            n = (y1 - y0) * (x1 - x0)
            one = c1p[2 + y0 : 2 + y1, 2 + x0 : 2 + x1].reshape(n, Z, L)
            g1 = rounded(acc[at : at + n] * slope(one))
            gup[1 + y0 : 1 + y1, 1 + x0 : 1 + x1] = g1.reshape(y1 - y0, x1 - x0, Z, L)
            at += n

    inner = [(1, N3 - 1, 1, N3 - 1)]
    grad_one(rim(N3, 1))
    copies = send_halo(EX_G1, gup, N3, 1)

    mid = coarse_weight_grad(
        columns(c1p, N3, 1), gp[1 : N3 + 1, 1 : N3 + 1].reshape(-1, Z, L)
    )
    two = c2[1 : N3 + 1, 1 : N3 + 1].reshape(-1, L).astype(BF)
    lift_grad = tn(ulp[1 : N3 + 1, 1 : N3 + 1].reshape(-1, L).astype(BF), two)
    blocks = [mid[t, :C3, i * L : (i + 1) * L] for i in range(3) for t in range(9)]
    blocks.append(lift_grad[:C3])
    for g in range(7):
        for d, part in enumerate(pack4(blocks[4 * g : 4 * g + 4])):
            m0[(g * 3 + d) * C3 : (g * 3 + d + 1) * C3, :] = part.astype(BF)
    m0[21 * C3 :, :] = jnp.zeros((ROWS_M - 21 * C3, L), BF)
    red_m = Reduce(ring, ROWS_M, ("dp", "xy", "z"), ("xy", "dp"), (m0, m1), (mr0, mr1), mslot, mout, m_send, m_recv, sent)
    red_m.scatter_start(0)
    grad_one(inner)
    ent = coarse_weight_grad(columns(pad3, N3, 2), gup[1 : N3 + 1, 1 : N3 + 1].reshape(-1, Z, L))
    blocks = [ent[t, :C2, i * L : (i + 1) * L] for i in range(3) for t in range(9)]
    blocks.append(jnp.zeros((C2, L), F32))
    for g in range(7):
        for d, part in enumerate(pack4(blocks[4 * g : 4 * g + 4])):
            are32[(g * 3 + d) * C2 : (g * 3 + d + 1) * C2, :] = part
    are32[21 * C2 :, :] = jnp.zeros((ROWS_E - 21 * C2, L), F32)
    e0[...] = are32[...].astype(BF)
    red_e = Reduce(ring, ROWS_E, ("dp", "xy", "z"), ("xy", "dp"), (e0, e1), (er0, er1), eslot, eout, e_send, e_recv, sent)
    red_e.scatter_start(0)
    red_m.scatter_end(0)
    red_m.scatter_start(1)

    low = rounded(joined(nt(tap_rows(gup, inner), wet[...])))
    put_rows(up, inner, 0.25 * low)

    red_e.scatter_end(0)
    red_e.scatter_start(1)

    def fine_back(y, _):
        act = fa[pl.ds(y * 2, 2), 2 : N2 - 2].reshape(2, N3 - 2, 2, Z, L)
        e = e32[pl.ds(y * 2, 2), 2 : N2 - 2].reshape(2, N3 - 2, 2, Z, L)
        g = e + up[pl.ds(y, 1), 1 : N3 - 1].reshape(1, N3 - 2, 1, Z, L)
        g = (g * slope(act)).reshape(2, (N2 - 4) * Z, L).astype(BF)
        for j in range(3):
            g3f[pl.ds(y * 2 + j, 2), 2 * Z : (N2 - 2) * Z, j * L : (j + 1) * L] = g
        pad2[pl.ds(y * 2 + 1, 2), 3 : N2 - 1] = g.astype(F32).reshape(2, N2 - 4, Z, L)
        return 0

    lax.fori_loop(1, N3 - 1, fine_back, 0)
    gsum[...] = tn(x3[...].reshape(-1, 3 * L), g3f[...].reshape(-1, 3 * L))
    start = at = 4 * (N3 - 1) * Z
    for y0, y1, x0, x1 in rim(N2, 2):
        rows = (y1 - y0) * (x1 - x0) * Z
        for j in range(3):
            part = x3[y0 + j : y1 + j, x0 * Z : x1 * Z, :].reshape(rows, 3 * L)
            q[at : at + rows, 3 * j * L : 3 * (j + 1) * L] = part
        at += rows

    take_halo(EX_G1, gup, N3, 1, copies)
    low = rounded(joined(nt(tap_rows(gup, rim(N3, 1)), wet[...])))
    put_rows(up, rim(N3, 1), 0.25 * low)
    rows = 0
    for y0, y1, x0, x1 in rim(N2, 2):
        ny, nx = (y1 - y0) // 2, (x1 - x0) // 2
        act = fa[y0:y1, x0:x1].reshape(ny, 2, nx, 2, Z, L)
        e = e32[y0:y1, x0:x1].reshape(ny, 2, nx, 2, Z, L)
        g = e + up[y0 // 2 : y1 // 2, x0 // 2 : x1 // 2].reshape(ny, 1, nx, 1, Z, L)
        g = (g * slope(act)).reshape(-1, L).astype(BF)
        grim[rows : rows + g.shape[0], :] = g
        rows += g.shape[0]
        pad2[y0 + 1 : y1 + 1, x0 + 1 : x1 + 1] = g.astype(F32).reshape(y1 - y0, x1 - x0, Z, L)

    grad = tn(q[start:at, :], grim[...])
    for k in range(3):
        b0, b1, b2 = [
            gsum[k * L : k * L + C2, j * L : (j + 1) * L] + grad[(j * 3 + k) * L : (j * 3 + k) * L + C2]
            for j in range(3)
        ]
        lane = lanes(b0.shape)
        r1, r2 = pltpu.roll(b1, C2, 1), pltpu.roll(b2, 2 * C2 - L, 1)
        arf32[2 * k * C2 : (2 * k + 1) * C2, :] = jnp.where(lane < C2, b0, r1)
        arf32[(2 * k + 1) * C2 : (2 * k + 2) * C2, :] = jnp.where(lane < 2 * C2 - L, r1, r2)
    arf32[6 * C2 :, :] = jnp.zeros((ROWS_F - 6 * C2, L), F32)
    f0[...] = arf32[...].astype(BF)
    red_f = Reduce(ring, ROWS_F, ("dp", "xy", "z"), ("xy", "dp"), (f0, f1), (fr0, fr1), fslot, fout, f_send, f_recv, sent)
    red_f.scatter_start(0)
    copies = send_halo(EX_FINE, pad2, N2, 1)
    red_f.scatter_end(0)
    red_f.scatter_start(1)
    red_m.scatter_end(1)
    red_m.last_start()

    two = c2[1 : N3 + 1, 1 : N3 + 1].reshape(-1, L).astype(BF)
    up[...] = rounded(nt(two, wl[...])).reshape(N3, N3, Z, L)

    def mix(y, _):
        act = fa[pl.ds(y * 2, 2)].reshape(2, N3, 2, Z, L)
        lifted = up[pl.ds(y, 1)].reshape(1, N3, 1, Z, L)
        d32[pl.ds(y * 2, 2)] = (act + lifted).reshape(2, N2, Z, L)
        return 0

    lax.fori_loop(0, N3, mix, 0)

    red_e.scatter_end(1)
    red_e.last_start()
    write_cells(d32, raw, mixed_ref)
    store(mixed_ref, mixed_hbm)

    red_f.scatter_end(1)
    red_f.last_start()
    red_m.last_end()
    red_m.gather_start()
    red_e.last_end()
    red_e.gather_start()

    take_halo(EX_FINE, pad2, N2, 1, copies)
    fine_columns()

    def fine_backward(chunk, _):
        d32[pl.ds(chunk * 4, 4)] = nt(fine_rows(chunk), wft[...]).reshape(4, N2, Z, L)
        return 0

    lax.fori_loop(0, 4, fine_backward, 0)

    red_f.last_end()
    red_f.gather_start()

    write_cells(d32, raw2, ig_ref)
    store(ig_ref, ig_hbm)
    for c in sent[:-45]:
        c.wait_send()
    del sent[:-45]

    red_m.gather_end()
    red_m.gather_start()
    red_e.gather_end()
    red_e.gather_start()
    red_f.gather_end()
    red_f.gather_start()
    red_m.gather_end()
    for g in range(7):
        d = [mout[(g * 3 + s) * C3 : (g * 3 + s + 1) * C3, :].astype(F32) for s in range(3)]
        for s, b in enumerate(unpack4(d)):
            mflat[(g * 4 + s) * C3 : (g * 4 + s + 1) * C3, :] = b.astype(BF)
    store(mflat, m_hbm)
    red_e.gather_end()
    are32[...] = eout[...].astype(F32)
    for g in range(7):
        d = [are32[(g * 3 + s) * C2 : (g * 3 + s + 1) * C2, :] for s in range(3)]
        for s, b in enumerate(unpack4(d)):
            eflat[(g * 4 + s) * PITCH : (g * 4 + s) * PITCH + C2, :] = b.astype(BF)
    store(eflat, e_hbm)
    red_f.gather_end()
    store(fout, f_hbm)
    for c in sent:
        c.wait_send()
    for done in stores:
        done.wait()


def finish(
    mixed_in, ig_in, m_hbm, e_hbm, f_hbm, mixed, ig, gf_hbm, ge_hbm, gm_hbm, gl_hbm,
    mixed_ref, ig_ref, mflat, eflat, fout, gf, ge, gm, gl, arf32, in_sem, out_sem,
):
    mid, low = 9 * C3, 9 * PITCH
    ends = (mid, 2 * mid, 28 * C3)
    parts = [(mixed_in, mixed_ref), (ig_in, ig_ref)]
    for i in range(3):
        rows = pl.ds(i * mid, ends[i] - i * mid)
        parts.append((m_hbm.at[rows], mflat.at[rows]))
    for i in range(3):
        parts.append((e_hbm.at[pl.ds(i * low, low)], eflat.at[pl.ds(i * low, low)]))
    parts.append((f_hbm, fout))
    loads = [pltpu.make_async_copy(src, dst, in_sem.at[i]) for i, (src, dst) in enumerate(parts)]
    for load in loads:
        load.start()
    parts = [(mixed_ref, mixed), (ig_ref, ig)]
    parts += [(gm.at[i], gm_hbm.at[i]) for i in range(3)]
    parts += [(ge.at[i], ge_hbm.at[i]) for i in range(3)]
    parts += [(gf, gf_hbm), (gl, gl_hbm)]
    stores = [pltpu.make_async_copy(src, dst, out_sem.at[i]) for i, (src, dst) in enumerate(parts)]

    for i in range(2):
        loads[i].wait()
        stores[i].start()
    for i in range(3):
        loads[2 + i].wait()
        for t in range(9):
            at = (i * 9 + t) * C3
            gm[i, t // 3, t % 3] = mflat[at : at + C3, :].astype(F32)[:, 0:C3]
        stores[2 + i].start()
    gl[...] = mflat[27 * C3 :, :].astype(F32)[0:C2, 0:C3]
    stores[9].start()
    for i in range(3):
        loads[5 + i].wait()
        for t in range(9):
            at = (i * 9 + t) * PITCH
            ge[i, t // 3, t % 3] = eflat[at : at + C2, :].astype(F32)[:, 0:C3]
        stores[5 + i].start()

    loads[8].wait()
    arf32[...] = fout[...].astype(F32)
    for k in range(3):
        d0 = arf32[2 * k * C2 : (2 * k + 1) * C2, :]
        d1 = arf32[(2 * k + 1) * C2 : (2 * k + 2) * C2, :]
        lane = lanes(d0.shape)
        b1 = pltpu.roll(jnp.where(lane >= C2, d0, d1), L - C2, 1)
        b2 = pltpu.roll(d1, 2 * L - 2 * C2, 1)
        for j, b in enumerate((d0, b1, b2)):
            gf[j, k] = b[:, 0:C2]
    stores[8].start()
    for done in stores:
        done.wait()


def body(fine_input, fine_weight, entry_weight, middle_weight, lift_weight, upstream):
    args = (fine_input, fine_weight, entry_weight, middle_weight, lift_weight.T, upstream)
    field = jax.ShapeDtypeStruct(fine_input.shape, BF)
    whole = pl.BlockSpec(memory_space=pl.ANY)
    cells3 = (N3 + 4) * (N3 + 4) * Z
    flat = [(28 * C3, L), (28 * PITCH, L), (ROWS_F, L)]

    def v(*shape):
        return pltpu.VMEM(shape, BF)

    def w(*shape):
        return pltpu.VMEM(shape, F32)

    def sems(n):
        return [pltpu.SemaphoreType.DMA((n,)), pltpu.SemaphoreType.DMA((n,))]

    def sums(rows, *sizes):
        left, sent, got = rows, [], []
        for size in sizes:
            sent.append(v(left, L))
            left //= size
            got.append(v(size - 1, left, L))
        return [*sent, *got, v(4, left, L), *sems(3 + 2 * sum(size - 1 for size in sizes))]

    scratch = [
        *[v(*arg.shape) for arg in args], v(*field.shape), v(*field.shape),
        *[v(rows, L) for rows in ROWS], v(*flat[0]), v(*flat[1]), *sems(6),
        w(TILES, (Z + 1) * N2, L), w(TILES, (Z + 1) * N2, L), w(N2 + 2, N2 + 2, Z, L), w(N3 + 6, N3 + 6, Z, L),
        w(N3 + 2, N3 + 2, Z, L), w(N2, N2, Z, L),
        v(N2 + 2, N2 * Z, 3 * L), v(N2 + 2, N2 * Z, 3 * L), w(N2, N2, Z, L),
        v(cells3, 9 * L), w(N3 + 4, N3 + 4, Z, L), w(N3 + 2, N3 + 2, Z, L), w(N3 + 2, N3 + 2, Z, L),
        w(N3 + 2, N3 + 2, Z, L), w(N3, N3, Z, L), w(3 * L, 3 * L), v(8 * (N2 - 2) * Z, L), w(N2, N2, Z, L),
        v(9 * L, L), v(L, 9 * L), v(9 * L, 3 * L), v(3 * L, 9 * L), v(9 * L, 3 * L), v(3 * L, 9 * L), v(L, L),
        w(ROWS_E, L), w(ROWS_F, L),
        v(5, 8, 3 * N3 * Z, L), v(5, 8, 3 * N3 * Z, L), *sems(40),
        *sums(ROWS_M, 2, 16), *sums(ROWS_E, 2, 16), *sums(ROWS_F, 2, 16),
    ]
    packed = [jax.ShapeDtypeStruct(size, BF) for size in flat]
    fields_and_sums = pl.pallas_call(
        kernel,
        out_shape=(field, field, *packed),
        in_specs=[whole] * 6,
        out_specs=[whole] * 5,
        scratch_shapes=scratch,
        compiler_params=pltpu.CompilerParams(
            collective_id=0, has_side_effects=True, vmem_limit_bytes=60 * 1024 * 1024
        ),
    )(*args)
    mixed, input_grad, fine, entry, middle, lift = pl.pallas_call(
        finish,
        out_shape=(
            field,
            field,
            jax.ShapeDtypeStruct(fine_weight.shape, F32),
            jax.ShapeDtypeStruct(entry_weight.shape, F32),
            jax.ShapeDtypeStruct(middle_weight.shape, F32),
            jax.ShapeDtypeStruct(lift_weight.shape[::-1], F32),
        ),
        in_specs=[whole] * 5,
        out_specs=[whole] * 6,
        scratch_shapes=[
            v(*field.shape), v(*field.shape), *[v(*size) for size in flat],
            w(*fine_weight.shape), w(*entry_weight.shape), w(*middle_weight.shape), w(*lift_weight.shape[::-1]),
            w(ROWS_F, L), *sems(10),
        ],
        compiler_params=pltpu.CompilerParams(vmem_limit_bytes=60 * 1024 * 1024),
    )(*fields_and_sums)
    return mixed, input_grad, fine, entry, middle, lift.T


def solution(mesh):
    assert mesh.shape["gy"] == GY and mesh.shape["gx"] == GX
    return jax.shard_map(
        body,
        mesh=mesh,
        in_specs=(P("dp", None, "gy", "gx"), P(), P(), P(), P(), P("dp", None, "gy", "gx")),
        out_specs=(P("dp", None, "gy", "gx"), P("dp", None, "gy", "gx"), P(), P(), P(), P()),
        check_vma=False,
    )
```
